32 devices in a mesh: dp: 16 (over z, y, core), tensor: 2 (over x).
Axes of the slice: x: 2, y: 2, z: 4, core: 2. Of those that a mesh axis runs over, the one named last changes fastest.
Arguments:
- layer_input: bfloat16 [16384, 2304], P(('dp', 'tensor')), may hold values from -6 to 6
- query_weight: bfloat16 [2304, 2048], P('dp', 'tensor'), may hold values from -0.125 to 0.125
- key_weight: bfloat16 [2304, 1024], P('dp', 'tensor'), may hold values from -0.125 to 0.125
- value_weight: bfloat16 [2304, 1024], P('dp', 'tensor'), may hold values from -0.125 to 0.125
- w_output: bfloat16 [2048, 2304], P('tensor', 'dp'), may hold values from -0.5 to 0.5
- w_gate: bfloat16 [2304, 9216], P('dp', 'tensor'), may hold values from -0.125 to 0.125
- w_up: bfloat16 [2304, 9216], P('dp', 'tensor'), may hold values from -0.125 to 0.125
- w_down: bfloat16 [9216, 2304], P('tensor', 'dp'), may hold values from -0.0625 to 0.0625
- gain_attn_in: float32 [2304], P(('dp', 'tensor')), may hold values from 0.25 to 1.75
- gain_attn_out: float32 [2304], P(('dp', 'tensor')), may hold values from 0.25 to 1.75
- gain_ffn_in: float32 [2304], P(('dp', 'tensor')), may hold values from 0.25 to 1.75
- gain_ffn_out: float32 [2304], P(('dp', 'tensor')), may hold values from 0.25 to 1.75
- cotangent: bfloat16 [16384, 2304], P(('dp', 'tensor')), may hold values from -6 to 6
Outputs:
- layer_output: bfloat16 [16384, 2304], P(('dp', 'tensor'))
- input_grad: float32 [16384, 2304], P(('dp', 'tensor'))
- grad_query: float32 [2304, 2048], P('dp', 'tensor')
- grad_key: float32 [2304, 1024], P('dp', 'tensor')
- grad_value: float32 [2304, 1024], P('dp', 'tensor')
- grad_output: float32 [2048, 2304], P('tensor', 'dp')
- grad_gate: float32 [2304, 9216], P('dp', 'tensor')
- grad_up: float32 [2304, 9216], P('dp', 'tensor')
- grad_down: float32 [9216, 2304], P('tensor', 'dp')
- grad_attn_in: float32 [2304], P(('dp', 'tensor'))
- grad_attn_out: float32 [2304], P(('dp', 'tensor'))
- grad_ffn_in: float32 [2304], P(('dp', 'tensor'))
- grad_ffn_out: float32 [2304], P(('dp', 'tensor'))
The draws below stay inside these ranges and needn't reach their ends.
All inputs are finite; a program needn't handle non-finite values.
Results may differ from the reference program's by a relative error of at most 0.018.
Values may be sent and summed in bfloat16 or wider, within the bound.
A program may use at most 512 MiB of HBM per device.

```python
import jax
import jax.numpy as jnp
from jax import lax

MODEL_WIDTH = 2304
QUERY_HEADS = 8
KEY_VALUE_HEADS = 4
HEAD_WIDTH = 256
FF = 9216
SEQ_LEN = 1024
SEQS = 16
TOKENS = 16384


def raised(array, stream_key, source, target, parts, factor):
    def block_of(axis_at):
        return (jnp.arange(array.shape[axis_at]) // (array.shape[axis_at] // parts)).reshape((-1,) + (1,) * (array.ndim - 1 - axis_at))

    near = jax.random.permutation(stream_key, parts)[block_of(target)]
    far = (block_of(target) + parts // 2) % parts
    return jnp.where((block_of(source) == near) | (block_of(source) == far), factor * array, array)


def steps_of(own_key, extent, split, least, top_value):
    level, own = 1.0, jax.random.fold_in(own_key, 6)
    for dim, shards_of in split:
        draws = jnp.exp(jax.random.uniform(jax.random.fold_in(own, dim), (shards_of,), jnp.float32, least / len(split), top_value / len(split)))
        level = level * jnp.repeat(draws, extent[dim] // shards_of).reshape([-1 if axis == dim else 1 for axis in range(len(extent))])
    return level


def gaussian(rng, shape, spread, most, cuts=(), kind=jnp.bfloat16):
    loudness = steps_of(rng, shape, cuts, -0.22, 0.18) if cuts else 1.0
    entries = jax.random.normal(rng, shape, jnp.float32) * spread * loudness
    return jnp.minimum(jnp.maximum(entries, -most), most).astype(kind)


def gaussian_with(own_key, extent, scale, limit, split, heavy, dtype=jnp.bfloat16):
    array = scale * jax.random.normal(own_key, extent, jnp.float32)
    if split:
        array = array * steps_of(own_key, extent, split, -0.22, 0.18)
    return jnp.clip(raised(array, jax.random.fold_in(own_key, 3), *heavy), -limit, limit).astype(dtype)


def setup_inputs(seed: int = 0) -> dict:
    splits = jax.random.split(jax.random.key(seed), 14)
    return {
        "layer_input": gaussian(splits[0], (TOKENS, MODEL_WIDTH), 1.0, 6.0, ((0, 32),)),
        "query_weight": gaussian(splits[1], (MODEL_WIDTH, QUERY_HEADS * HEAD_WIDTH), MODEL_WIDTH ** -0.5, 0.125, ((0, 16), (1, 2))),
        "key_weight": gaussian(splits[2], (MODEL_WIDTH, KEY_VALUE_HEADS * HEAD_WIDTH), MODEL_WIDTH ** -0.5, 0.125, ((0, 16), (1, 2))),
        "value_weight": gaussian(splits[3], (MODEL_WIDTH, KEY_VALUE_HEADS * HEAD_WIDTH), MODEL_WIDTH ** -0.5, 0.125, ((0, 16), (1, 2))),
        "w_output": gaussian(splits[4], (QUERY_HEADS * HEAD_WIDTH, MODEL_WIDTH), (QUERY_HEADS * HEAD_WIDTH // 16) ** -0.5, 0.5, ((0, 2), (1, 16))),
        "w_gate": gaussian(splits[5], (MODEL_WIDTH, FF), MODEL_WIDTH ** -0.5, 0.125, ((0, 16), (1, 2))),
        "w_up": gaussian(splits[6], (MODEL_WIDTH, FF), MODEL_WIDTH ** -0.5, 0.125, ((0, 16), (1, 2))),
        "w_down": gaussian(splits[7], (FF, MODEL_WIDTH), FF ** -0.5, 0.0625, ((0, 2), (1, 16))),
        "gain_attn_in": jnp.clip(1.0 + 0.15 * jax.random.normal(splits[8], (MODEL_WIDTH,), jnp.float32), 0.25, 1.75),
        "gain_attn_out": jnp.clip(1.0 + 0.15 * jax.random.normal(splits[9], (MODEL_WIDTH,), jnp.float32), 0.25, 1.75),
        "gain_ffn_in": jnp.clip(1.0 + 0.15 * jax.random.normal(splits[10], (MODEL_WIDTH,), jnp.float32), 0.25, 1.75),
        "gain_ffn_out": jnp.clip(1.0 + 0.15 * jax.random.normal(splits[11], (MODEL_WIDTH,), jnp.float32), 0.25, 1.75),
        "cotangent": gaussian_with(splits[12], (TOKENS, MODEL_WIDTH), 1.0, 6.0, ((0, 32),), (0, 1, 32, 2.75)),
    }


EPSILON = 1e-06
LOGIT_CAP = 50.0

@jax.custom_vjp
def low(v):
    return lax.optimization_barrier(v.astype(jnp.bfloat16)).astype(jnp.float32)

@jax.custom_vjp
def low_back(v):
    return v

def low_keep(v):
    return (low(v), None)

def low_pass(kept, grad):
    return (grad,)

def back_keep(v):
    return (v, None)

def back_low(kept, grad):
    return (low(grad),)
low.defvjp(low_keep, low_pass)
low_back.defvjp(back_keep, back_low)

def rms_norm(values, gain):
    return values * lax.rsqrt(lax.optimization_barrier(jnp.mean(values * values, axis=-1, keepdims=True)) + EPSILON) * gain

def matrix_product(left, right):
    return jnp.dot(left, right, precision=lax.Precision.HIGHEST)

def rounded_pair(values):
    return low_back(low(values))

def layer(tokens, params):
    query_weight, key_weight, value_weight, w_output, w_gate, w_up, w_down, gain_a, gain_b, gain_c, gain_d = params
    sequence_length = tokens.shape[0]
    head_group = QUERY_HEADS // KEY_VALUE_HEADS
    normalized_input = low(rms_norm(tokens, gain_a))
    query_matrix_rows = rounded_pair(matrix_product(normalized_input, query_weight)).reshape(sequence_length, KEY_VALUE_HEADS, head_group, HEAD_WIDTH)
    key_matrix_rows = rounded_pair(matrix_product(normalized_input, key_weight)).reshape(sequence_length, KEY_VALUE_HEADS, HEAD_WIDTH)
    value_matrix_rows = rounded_pair(matrix_product(normalized_input, value_weight)).reshape(sequence_length, KEY_VALUE_HEADS, HEAD_WIDTH)
    scores = jnp.einsum('qhgd,khd->hgqk', query_matrix_rows, key_matrix_rows, precision=lax.Precision.HIGHEST) * HEAD_WIDTH ** (-0.5)
    scores = low_back(scores)
    capped = LOGIT_CAP * jnp.tanh(scores / LOGIT_CAP)
    position = jnp.arange(sequence_length)
    allowed = position[None, :] <= position[:, None]
    capped = jnp.where(allowed, capped, -jnp.inf)
    soft_low = low(jax.nn.softmax(capped, axis=-1))
    attended = jnp.einsum('hgqk,khd->qhgd', soft_low, value_matrix_rows, precision=lax.Precision.HIGHEST)
    attended = rounded_pair(attended.reshape(sequence_length, QUERY_HEADS * HEAD_WIDTH))
    branch_attn = low_back(matrix_product(attended, w_output))
    middle = tokens + rms_norm(branch_attn, gain_b)
    normed_mid = low(rms_norm(middle, gain_c))
    gate = low_back(matrix_product(normed_mid, w_gate))
    up_rows = low_back(matrix_product(normed_mid, w_up))
    hidden = low(jax.nn.gelu(gate, approximate=True) * up_rows)
    branch_ffn = low_back(matrix_product(hidden, w_down))
    return middle + rms_norm(branch_ffn, gain_d)

def reference(layer_input, query_weight, key_weight, value_weight, w_output, w_gate, w_up, w_down, gain_attn_in, gain_attn_out, gain_ffn_in, gain_ffn_out, cotangent):
    params = (query_weight.astype(jnp.float32), key_weight.astype(jnp.float32), value_weight.astype(jnp.float32), w_output.astype(jnp.float32), w_gate.astype(jnp.float32), w_up.astype(jnp.float32), w_down.astype(jnp.float32), gain_attn_in.astype(jnp.float32), gain_attn_out.astype(jnp.float32), gain_ffn_in.astype(jnp.float32), gain_ffn_out.astype(jnp.float32))
    inputs = layer_input.astype(jnp.float32).reshape(SEQS, SEQ_LEN, MODEL_WIDTH)
    upstream = cotangent.astype(jnp.float32).reshape(SEQS, SEQ_LEN, MODEL_WIDTH)

    def step(totals, item):
        tokens, seq_grad = item
        result, pull = jax.vjp(layer, tokens, params)
        token_grad, param_grads = pull(seq_grad)
        totals = jax.tree.map(lambda first, second: first + second, totals, param_grads)
        return (totals, (result.astype(jnp.bfloat16), token_grad))
    start_totals = tuple((jnp.zeros_like(value) for value in params))
    totals, (results, token_grads) = lax.scan(step, start_totals, (inputs, upstream))
    return (results.reshape(TOKENS, MODEL_WIDTH), token_grads.reshape(TOKENS, MODEL_WIDTH), totals[0], totals[1], totals[2], totals[3], totals[4], totals[5], totals[6], totals[7], totals[8], totals[9], totals[10])
```

```python
import jax
import jax.numpy as jnp
from jax import lax
from jax.sharding import PartitionSpec as P

QUERY_HEADS = 8
KEY_VALUE_HEADS = 4
HEAD_WIDTH = 256
SEQ_LEN = 1024


EPSILON = 1e-06
LOGIT_CAP = 50.0

BF16 = jnp.bfloat16
F32 = jnp.float32


def rms_norm(values, gain):
    return values * lax.rsqrt(jnp.mean(values * values, axis=-1, keepdims=True) + EPSILON) * gain


def matmul(left, right):
    return jnp.dot(left, right, preferred_element_type=F32)


def matmul_nt(left, right):
    return lax.dot_general(left, right, (((1,), (1,)), ((), ())), preferred_element_type=F32)


def swap(rows):
    return lax.ppermute(rows, "tensor", [(0, 1), (1, 0)])


def flip(array, bit, dp):
    return lax.ppermute(array, "dp", [(i, i ^ (1 << bit)) for i in range(dp)])


def gather_small(piece, dp):
    other = swap(piece)
    whole = jnp.where(
        lax.axis_index("tensor") == 0,
        jnp.concatenate([piece, other], axis=1),
        jnp.concatenate([other, piece], axis=1),
    )
    bit = 0
    while (1 << bit) < dp:
        other = flip(whole, bit, dp)
        high = (lax.axis_index("dp") >> bit) & 1
        whole = jnp.where(
            high == 0,
            jnp.concatenate([whole, other], axis=1),
            jnp.concatenate([other, whole], axis=1),
        )
        bit += 1
    return whole


def scatter_small(partial, dp):
    bit = dp.bit_length() - 2
    while bit >= 0:
        half = partial.shape[1] // 2
        low, high = partial[:, :half], partial[:, half:]
        mine = (lax.axis_index("dp") >> bit) & 1
        keep = jnp.where(mine == 0, low, high)
        give = jnp.where(mine == 0, high, low)
        partial = keep + flip(give, bit, dp)
        bit -= 1
    half = partial.shape[1] // 2
    low, high = partial[:, :half], partial[:, half:]
    mine = lax.axis_index("tensor")
    keep = jnp.where(mine == 0, low, high)
    give = jnp.where(mine == 0, high, low)
    return keep + swap(give)


def pick(array, index, axis):
    return lax.dynamic_index_in_dim(array, index, axis, keepdims=False)


def scatter_grad(left_t, right, dp):
    width, tokens = left_t.shape
    columns = right.shape[1]
    rest, rows = dp // 4, width // dp
    me = lax.axis_index("dp")
    core, side, place = me & 1, (me >> 1) & 1, me >> 2
    blocks = left_t.reshape(rest, 2, 2, rows, tokens)

    def product(part):
        flat = part.reshape(-1, tokens)
        return matmul(flat, right).reshape(part.shape[:-1] + (columns,))

    give = product(pick(blocks, 1 - core, 2)).astype(BF16)
    from_core = flip(give, 0, dp)
    mine = pick(blocks, core, 2)
    give = (
        product(pick(mine, 1 - side, 1)) + pick(from_core, 1 - side, 1).astype(F32)
    ).astype(BF16)
    from_side = flip(give, 1, dp)
    total = (
        product(pick(mine, side, 1))
        + pick(from_core, side, 1).astype(F32)
        + from_side.astype(F32)
    ).astype(BF16)
    result = pick(total, place, 0).astype(F32)
    for shift in range(1, rest):
        give = pick(total, (place + shift) % rest, 0)
        pairs = [(i, (i + 4 * shift) % dp) for i in range(dp)]
        result = result + lax.ppermute(give, "dp", pairs).astype(F32)
    return result


def causal_allowed(block_rows, end_row, begin_row):
    key_place = lax.broadcasted_iota(jnp.int32, (block_rows, end_row), 1)
    query_place = lax.broadcasted_iota(jnp.int32, (block_rows, end_row), 0) + begin_row
    return key_place <= query_place


def attend(query_matrix_rows, key_matrix_rows, value_matrix_rows):
    sequence_length = query_matrix_rows.shape[1]
    head_size = query_matrix_rows.shape[4]
    block_rows = min(512, sequence_length)
    score_scale = head_size ** (-0.5)
    out_parts = []
    total_parts = []
    for block_index in range(sequence_length // block_rows):
        begin_row = block_index * block_rows
        end_row = begin_row + block_rows
        query_block = query_matrix_rows[:, begin_row:end_row]
        key_block = key_matrix_rows[:, :end_row]
        value_block = value_matrix_rows[:, :end_row]
        scores = (
            jnp.einsum("sqhgd,skhd->shgqk", query_block, key_block, preferred_element_type=F32)
            * score_scale
        )
        capped = LOGIT_CAP * jnp.tanh(scores / LOGIT_CAP)
        capped = jnp.where(causal_allowed(block_rows, end_row, begin_row), capped, -jnp.inf)
        row_top = jnp.max(capped, axis=-1, keepdims=True)
        exp_terms = jnp.exp(capped - row_top)
        row_total = jnp.sum(exp_terms, axis=-1, keepdims=True)
        soft_low = (exp_terms / row_total).astype(BF16)
        attended = jnp.einsum(
            "shgqk,skhd->sqhgd", soft_low, value_block, preferred_element_type=F32
        )
        out_parts.append(attended.astype(BF16))
        total_parts.append(row_top + jnp.log(row_total))
    return (jnp.concatenate(out_parts, axis=1), jnp.concatenate(total_parts, axis=3))


def attend_back(query_matrix_rows, key_matrix_rows, value_matrix_rows, log_total, d_attended):
    sequence_length = query_matrix_rows.shape[1]
    head_size = query_matrix_rows.shape[4]
    block_rows = min(512, sequence_length)
    score_scale = head_size ** (-0.5)
    d_query_parts = []
    d_key = jnp.zeros(key_matrix_rows.shape, F32)
    d_value = jnp.zeros(value_matrix_rows.shape, F32)
    for block_index in range(sequence_length // block_rows):
        begin_row = block_index * block_rows
        end_row = begin_row + block_rows
        query_block = query_matrix_rows[:, begin_row:end_row]
        key_block = key_matrix_rows[:, :end_row]
        value_block = value_matrix_rows[:, :end_row]
        d_block = d_attended[:, begin_row:end_row]
        scores = (
            jnp.einsum("sqhgd,skhd->shgqk", query_block, key_block, preferred_element_type=F32)
            * score_scale
        )
        tangent = jnp.tanh(scores / LOGIT_CAP)
        capped = jnp.where(
            causal_allowed(block_rows, end_row, begin_row), LOGIT_CAP * tangent, -jnp.inf
        )
        soft_weights = jnp.exp(capped - log_total[:, :, :, begin_row:end_row])
        soft_low = soft_weights.astype(BF16)
        d_soft = jnp.einsum(
            "sqhgd,skhd->shgqk", d_block, value_block, preferred_element_type=F32
        )
        d_capped = soft_weights * (d_soft - jnp.sum(soft_weights * d_soft, axis=-1, keepdims=True))
        d_scores = (d_capped * (1.0 - tangent * tangent)).astype(BF16)
        d_query_parts.append(
            jnp.einsum("shgqk,skhd->sqhgd", d_scores, key_block, preferred_element_type=F32)
            * score_scale
        )
        padding = ((0, 0), (0, sequence_length - end_row), (0, 0), (0, 0))
        key_term = (
            jnp.einsum("shgqk,sqhgd->skhd", d_scores, query_block, preferred_element_type=F32)
            * score_scale
        )
        value_term = jnp.einsum(
            "shgqk,sqhgd->skhd", soft_low, d_block, preferred_element_type=F32
        )
        d_key = d_key + jnp.pad(key_term, padding)
        d_value = d_value + jnp.pad(value_term, padding)
    return (jnp.concatenate(d_query_parts, axis=1), d_key, d_value)


def gelu_product(gate, up_rows):
    return jax.nn.gelu(gate, approximate=True) * up_rows


def make_body(dp):
    def in_order(rows):
        other = swap(rows)
        return jnp.where(
            lax.axis_index("tensor") == 0,
            jnp.concatenate([rows, other], axis=0),
            jnp.concatenate([other, rows], axis=0),
        )

    def own_first(rows):
        return jnp.concatenate([rows, swap(rows)], axis=0)

    def collect_in_order(partial):
        half = partial.shape[0] // 2
        first = lax.axis_index("tensor") == 0
        low, high = partial[:half], partial[half:]
        give = jnp.where(first, high, low).astype(BF16)
        return jnp.where(first, low, high) + swap(give).astype(F32)

    def collect_own_first(partial):
        half = partial.shape[0] // 2
        return partial[:half] + swap(partial[half:].astype(BF16)).astype(F32)

    def body(
        layer_input,
        query_weight,
        key_weight,
        value_weight,
        w_output,
        w_gate,
        w_up,
        w_down,
        gain_attn_in,
        gain_attn_out,
        gain_ffn_in,
        gain_ffn_out,
        cotangent,
    ):
        gains = gather_small(
            jnp.stack([gain_attn_in, gain_attn_out, gain_ffn_in, gain_ffn_out]), dp
        )
        gain_a, gain_b, gain_c, gain_d = gains[0], gains[1], gains[2], gains[3]
        query_cols, key_cols = query_weight.shape[1], key_weight.shape[1]
        ff_local = w_gate.shape[1]
        qkv_cols = query_cols + 2 * key_cols
        full_attn = lax.all_gather(
            jnp.concatenate([query_weight, key_weight, value_weight, w_output.T], axis=1),
            "dp",
            axis=0,
            tiled=True,
        )
        full_qkv, full_output_t = full_attn[:, :qkv_cols], full_attn[:, qkv_cols:]
        full_gate = lax.all_gather(w_gate, "dp", axis=0, tiled=True)
        full_up = lax.all_gather(w_up, "dp", axis=0, tiled=True)
        full_down_t = lax.all_gather(w_down.T, "dp", axis=0, tiled=True)

        residual_in = layer_input.astype(F32)
        normalized_input = in_order(rms_norm(residual_in, gain_a).astype(BF16))
        all_rows = normalized_input.shape[0]
        seq_count = all_rows // SEQ_LEN
        kv_local = key_cols // HEAD_WIDTH
        head_group = QUERY_HEADS // KEY_VALUE_HEADS
        qkv = matmul(normalized_input, full_qkv).astype(BF16)
        query_matrix_rows = qkv[:, :query_cols].reshape(
            seq_count, SEQ_LEN, kv_local, head_group, HEAD_WIDTH
        )
        key_matrix_rows = qkv[:, query_cols : query_cols + key_cols].reshape(
            seq_count, SEQ_LEN, kv_local, HEAD_WIDTH
        )
        value_matrix_rows = qkv[:, query_cols + key_cols :].reshape(
            seq_count, SEQ_LEN, kv_local, HEAD_WIDTH
        )
        attended, log_total = attend(query_matrix_rows, key_matrix_rows, value_matrix_rows)
        attended = attended.reshape(all_rows, query_cols)
        branch_attn = collect_in_order(matmul_nt(attended, full_output_t))
        middle, pull_attn_out = jax.vjp(
            lambda values, gain: residual_in + rms_norm(values, gain), branch_attn, gain_b
        )
        normed_mid_local, pull_ffn_in = jax.vjp(rms_norm, middle, gain_c)
        normed_mid = own_first(normed_mid_local.astype(BF16))
        gate = matmul(normed_mid, full_gate)
        up_rows = matmul(normed_mid, full_up)
        hidden_f, pull_glu = jax.vjp(gelu_product, gate, up_rows)
        hidden = hidden_f.astype(BF16)
        branch_ffn = collect_own_first(matmul_nt(hidden, full_down_t))
        ffn_out, pull_ffn_out = jax.vjp(rms_norm, branch_ffn, gain_d)
        layer_output = (middle + ffn_out).astype(BF16)
        upstream = cotangent.astype(F32)
        d_ffn, grad_d = pull_ffn_out(upstream)
        d_ffn_rows = own_first(d_ffn.astype(BF16))
        grad_down = scatter_grad(d_ffn_rows.T, hidden, dp).T
        d_hidden = matmul(d_ffn_rows, full_down_t)
        d_gate_f, d_up_f = pull_glu(d_hidden)
        d_gate = d_gate_f.astype(BF16)
        d_up = d_up_f.astype(BF16)
        d_normed_mid = matmul_nt(d_gate, full_gate) + matmul_nt(d_up, full_up)
        normed_mid_t = normed_mid.T
        grad_gate = scatter_grad(normed_mid_t, d_gate, dp)
        grad_up = scatter_grad(normed_mid_t, d_up, dp)
        d_mid_norm, grad_c = pull_ffn_in(collect_own_first(d_normed_mid))
        d_middle = upstream + d_mid_norm
        d_branch, grad_b = pull_attn_out(d_middle)
        d_branch_rows = in_order(d_branch.astype(BF16))
        grad_output = scatter_grad(d_branch_rows.T, attended, dp).T
        d_attended = matmul(d_branch_rows, full_output_t).astype(BF16)
        d_attended = d_attended.reshape(seq_count, SEQ_LEN, kv_local, head_group, HEAD_WIDTH)
        d_query_f, d_key_f, d_value_f = attend_back(
            query_matrix_rows, key_matrix_rows, value_matrix_rows, log_total, d_attended
        )
        d_qkv = jnp.concatenate(
            [
                d_query_f.reshape(all_rows, query_cols).astype(BF16),
                d_key_f.reshape(all_rows, key_cols).astype(BF16),
                d_value_f.reshape(all_rows, key_cols).astype(BF16),
            ],
            axis=1,
        )
        grad_qkv = scatter_grad(normalized_input.T, d_qkv, dp)
        d_normed_in = matmul_nt(d_qkv, full_qkv)
        grad_query = grad_qkv[:, :query_cols]
        grad_key = grad_qkv[:, query_cols : query_cols + key_cols]
        grad_value = grad_qkv[:, query_cols + key_cols :]
        _, pull_attn_in = jax.vjp(rms_norm, residual_in, gain_a)
        d_input_norm, grad_a = pull_attn_in(collect_in_order(d_normed_in))
        input_grad = d_middle + d_input_norm
        small = scatter_small(jnp.stack([grad_a, grad_b, grad_c, grad_d]), dp)
        return (
            layer_output,
            input_grad,
            grad_query,
            grad_key,
            grad_value,
            grad_output,
            grad_gate,
            grad_up,
            grad_down,
            small[0],
            small[1],
            small[2],
            small[3],
        )

    return body


def solution(mesh):
    rows = P(("dp", "tensor"), None)
    gain = P(("dp", "tensor"))
    into, out_of = P("dp", "tensor"), P("tensor", "dp")
    return jax.shard_map(
        make_body(mesh.shape["dp"]),
        mesh=mesh,
        in_specs=(rows, into, into, into, out_of, into, into, out_of, gain, gain, gain, gain, rows),
        out_specs=(rows, rows, into, into, into, out_of, into, into, out_of, gain, gain, gain, gain),
        check_vma=False,
    )
```

```python
import jax
import jax.numpy as jnp
from jax import lax
from jax.sharding import PartitionSpec as P

QUERY_HEADS = 8
KEY_VALUE_HEADS = 4
HEAD_WIDTH = 256
SEQ_LEN = 1024


EPSILON = 1e-06
LOGIT_CAP = 50.0

BF16 = jnp.bfloat16
F32 = jnp.float32


def rms_norm(values, gain):
    return values * lax.rsqrt(jnp.mean(values * values, axis=-1, keepdims=True) + EPSILON) * gain


def matmul(left, right):
    return jnp.dot(left, right, preferred_element_type=F32)


def matmul_nt(left, right):
    return lax.dot_general(left, right, (((1,), (1,)), ((), ())), preferred_element_type=F32)


def swap(rows):
    return lax.ppermute(rows, "tensor", [(0, 1), (1, 0)])


def flip(array, bit, dp):
    return lax.ppermute(array, "dp", [(i, i ^ (1 << bit)) for i in range(dp)])


def gather_small(piece, dp):
    other = swap(piece)
    whole = jnp.where(
        lax.axis_index("tensor") == 0,
        jnp.concatenate([piece, other], axis=1),
        jnp.concatenate([other, piece], axis=1),
    )
    bit = 0
    while (1 << bit) < dp:
        other = flip(whole, bit, dp)
        high = (lax.axis_index("dp") >> bit) & 1
        whole = jnp.where(
            high == 0,
            jnp.concatenate([whole, other], axis=1),
            jnp.concatenate([other, whole], axis=1),
        )
        bit += 1
    return whole


def scatter_small(partial, dp):
    bit = dp.bit_length() - 2
    while bit >= 0:
        half = partial.shape[1] // 2
        low, high = partial[:, :half], partial[:, half:]
        mine = (lax.axis_index("dp") >> bit) & 1
        keep = jnp.where(mine == 0, low, high)
        give = jnp.where(mine == 0, high, low)
        partial = keep + flip(give, bit, dp)
        bit -= 1
    half = partial.shape[1] // 2
    low, high = partial[:, :half], partial[:, half:]
    mine = lax.axis_index("tensor")
    keep = jnp.where(mine == 0, low, high)
    give = jnp.where(mine == 0, high, low)
    return keep + swap(give)


def tied(*arrays):
    return lax.optimization_barrier(arrays)


def pick(array, index, axis):
    return lax.dynamic_index_in_dim(array, index, axis, keepdims=False)


class Scatter:
    def __init__(self, dp, chunks):
        self.dp, self.chunks = dp, chunks
        me = lax.axis_index("dp")
        self.core, self.side = me & 1, (me >> 1) & 1
        self.taken = []

    def product(self, part, right):
        flat = part.reshape(-1, part.shape[-1])
        return matmul(flat, right).reshape(part.shape[:-1] + (right.shape[1],))

    def give(self, left_t, right):
        width, tokens = left_t.shape
        self.left, self.right = left_t.reshape(self.dp // 4, 2, 2, width // self.dp, tokens), right
        self.given = self.product(pick(self.left, 1 - self.core, 2), right).astype(BF16)
        return self.given

    def to_core(self):
        return self.given, lambda array: flip(array, 0, self.dp)

    def add(self, line, taken):
        product = self.product(pick(self.left, self.core, 2), line.next(self.right))
        self.sums = (product + taken.astype(F32)).astype(BF16)
        return self.sums

    def to_side(self, chunk):
        size = self.sums.shape[0] // self.chunks
        part = self.sums[chunk * size : (chunk + 1) * size]
        return pick(part, 1 - self.side, 1), lambda array: flip(array, 1, self.dp)

    def total(self, line):
        mine = pick(line.next(self.sums), self.side, 1).astype(F32)
        taken = jnp.concatenate(self.taken, axis=0) if self.chunks > 1 else self.taken[0]
        total = line.mark((mine + taken.astype(F32)).astype(BF16))
        rest = self.dp // 4
        groups = [[low + 4 * high for high in range(rest)] for low in range(4)]
        self.scattered = lax.psum_scatter(
            total.reshape(-1, total.shape[-1]),
            "dp",
            scatter_dimension=0,
            axis_index_groups=groups,
            tiled=True,
        )

    def result(self):
        return self.scattered.astype(F32)


def causal_allowed(block_rows, end_row, begin_row):
    key_place = lax.broadcasted_iota(jnp.int32, (block_rows, end_row), 1)
    query_place = lax.broadcasted_iota(jnp.int32, (block_rows, end_row), 0) + begin_row
    return key_place <= query_place


def attend(query_matrix_rows, key_matrix_rows, value_matrix_rows):
    sequence_length = query_matrix_rows.shape[1]
    head_size = query_matrix_rows.shape[4]
    block_rows = min(512, sequence_length)
    score_scale = head_size ** (-0.5)
    out_parts = []
    total_parts = []
    for block_index in range(sequence_length // block_rows):
        begin_row = block_index * block_rows
        end_row = begin_row + block_rows
        query_block = query_matrix_rows[:, begin_row:end_row]
        key_block = key_matrix_rows[:, :end_row]
        value_block = value_matrix_rows[:, :end_row]
        scores = (
            jnp.einsum("sqhgd,skhd->shgqk", query_block, key_block, preferred_element_type=F32)
            * score_scale
        )
        capped = LOGIT_CAP * jnp.tanh(scores / LOGIT_CAP)
        capped = jnp.where(causal_allowed(block_rows, end_row, begin_row), capped, -jnp.inf)
        row_top = jnp.max(capped, axis=-1, keepdims=True)
        exp_terms = jnp.exp(capped - row_top)
        row_total = jnp.sum(exp_terms, axis=-1, keepdims=True)
        soft_low = (exp_terms / row_total).astype(BF16)
        attended = jnp.einsum(
            "shgqk,skhd->sqhgd", soft_low, value_block, preferred_element_type=F32
        )
        out_parts.append(attended.astype(BF16))
        total_parts.append(row_top + jnp.log(row_total))
    return (jnp.concatenate(out_parts, axis=1), jnp.concatenate(total_parts, axis=3))


def attend_back(line, query_matrix_rows, key_matrix_rows, value_matrix_rows, log_total, d_attended, block_index):
    sequence_length = query_matrix_rows.shape[1]
    head_size = query_matrix_rows.shape[4]
    block_rows = min(512, sequence_length)
    score_scale = head_size ** (-0.5)
    begin_row = block_index * block_rows
    end_row = begin_row + block_rows
    query_block = query_matrix_rows[:, begin_row:end_row]
    key_block = key_matrix_rows[:, :end_row]
    value_block = value_matrix_rows[:, :end_row]
    d_block = line.next(d_attended)[:, begin_row:end_row]
    scores = (
        jnp.einsum("sqhgd,skhd->shgqk", query_block, key_block, preferred_element_type=F32)
        * score_scale
    )
    tangent = jnp.tanh(scores / LOGIT_CAP)
    capped = jnp.where(
        causal_allowed(block_rows, end_row, begin_row), LOGIT_CAP * tangent, -jnp.inf
    )
    soft_weights = jnp.exp(capped - log_total[:, :, :, begin_row:end_row])
    soft_low = soft_weights.astype(BF16)
    d_soft = jnp.einsum("sqhgd,skhd->shgqk", d_block, value_block, preferred_element_type=F32)
    d_capped = soft_weights * (d_soft - jnp.sum(soft_weights * d_soft, axis=-1, keepdims=True))
    d_scores = (d_capped * (1.0 - tangent * tangent)).astype(BF16)
    d_query = (
        jnp.einsum("shgqk,skhd->sqhgd", d_scores, key_block, preferred_element_type=F32)
        * score_scale
    )
    padding = ((0, 0), (0, sequence_length - end_row), (0, 0), (0, 0))
    key_term = (
        jnp.einsum("shgqk,sqhgd->skhd", d_scores, query_block, preferred_element_type=F32)
        * score_scale
    )
    value_term = jnp.einsum("shgqk,sqhgd->skhd", soft_low, d_block, preferred_element_type=F32)
    line.mark(d_scores)
    return d_query, jnp.pad(key_term, padding), jnp.pad(value_term, padding)


def gelu_and_slope(gate):
    return jax.jvp(lambda u: jax.nn.gelu(u, approximate=True), (gate,), (jnp.ones_like(gate),))


class Line:
    def __init__(self):
        self.last = None

    def next(self, array):
        if self.last is not None:
            array, _ = tied(array, self.last)
        return array

    def mark(self, array):
        self.last = array
        return array

    def open(self, *transfers):
        self.flying = [send(self.next(array)) for array, send in transfers]

    def close(self):
        *taken, self.last = tied(*self.flying, self.last)
        return taken


def make_body(dp):
    def in_order(own, other):
        return jnp.where(
            lax.axis_index("tensor") == 0,
            jnp.concatenate([own, other], axis=0),
            jnp.concatenate([other, own], axis=0),
        )

    def halves(rows):
        half = rows.shape[0] // 2
        low, high = rows[:half], rows[half:]
        first = lax.axis_index("tensor") == 0
        return jnp.where(first, low, high), jnp.where(first, high, low)

    def body(
        layer_input,
        query_weight,
        key_weight,
        value_weight,
        w_output,
        w_gate,
        w_up,
        w_down,
        gain_attn_in,
        gain_attn_out,
        gain_ffn_in,
        gain_ffn_out,
        cotangent,
    ):
        line = Line()
        query_cols, key_cols = query_weight.shape[1], key_weight.shape[1]
        qkv_cols = query_cols + 2 * key_cols
        attn_cols = qkv_cols + query_cols
        full_first = lax.all_gather(
            jnp.concatenate([query_weight, key_weight, value_weight, w_output.T, w_gate], axis=1),
            "dp",
            axis=0,
            tiled=True,
        )
        full_qkv = full_first[:, :qkv_cols]
        full_output_t = full_first[:, qkv_cols:attn_cols]
        full_gate = full_first[:, attn_cols:]
        full_up = lax.all_gather(w_up, "dp", axis=0, tiled=True)
        full_down_t = lax.all_gather(w_down.T, "dp", axis=0, tiled=True)
        gains = gather_small(
            jnp.stack([gain_attn_in, gain_attn_out, gain_ffn_in, gain_ffn_out]), dp
        )
        gain_a, gain_b, gain_c, gain_d = gains[0], gains[1], gains[2], gains[3]

        residual_in = layer_input.astype(F32)
        own = rms_norm(residual_in, gain_a).astype(BF16)
        normalized_input = in_order(own, swap(own))
        all_rows = normalized_input.shape[0]
        half = all_rows // 2
        seq_count = all_rows // SEQ_LEN
        kv_local = key_cols // HEAD_WIDTH
        head_group = QUERY_HEADS // KEY_VALUE_HEADS
        qkv = matmul(normalized_input, full_qkv).astype(BF16)
        query_matrix_rows = qkv[:, :query_cols].reshape(
            seq_count, SEQ_LEN, kv_local, head_group, HEAD_WIDTH
        )
        key_matrix_rows = qkv[:, query_cols : query_cols + key_cols].reshape(
            seq_count, SEQ_LEN, kv_local, HEAD_WIDTH
        )
        value_matrix_rows = qkv[:, query_cols + key_cols :].reshape(
            seq_count, SEQ_LEN, kv_local, HEAD_WIDTH
        )
        attended, log_total = attend(query_matrix_rows, key_matrix_rows, value_matrix_rows)
        attended = attended.reshape(all_rows, query_cols)
        attended_own, attended_other = halves(attended)
        give = line.mark(matmul_nt(attended_other, full_output_t).astype(BF16))
        taken = swap(give)
        kept = line.mark(matmul_nt(line.next(attended_own), full_output_t))
        branch_attn = kept + taken.astype(F32)
        middle, pull_attn_out = jax.vjp(
            lambda values, gain: residual_in + rms_norm(values, gain), branch_attn, gain_b
        )
        normed_mid_f, pull_ffn_in = jax.vjp(rms_norm, middle, gain_c)
        mid_own = normed_mid_f.astype(BF16)
        mid_other = swap(mid_own)

        def feed(mid):
            gate = line.mark(matmul(line.next(mid), full_gate))
            up_rows = matmul(line.next(mid), full_up)
            active, slope = gelu_and_slope(gate)
            hidden = line.mark((active * up_rows).astype(BF16))
            return hidden, active.astype(BF16), (slope * up_rows).astype(BF16)

        hidden_own, active_own, slope_own = feed(mid_own)
        hidden_other, active_other, slope_other = feed(mid_other)
        mid_t = line.mark(jnp.concatenate([mid_own, line.next(mid_other)], axis=0).T)
        input_t = line.mark(line.next(normalized_input).T)
        hidden = line.mark(jnp.concatenate([hidden_own, line.next(hidden_other)], axis=0))

        quarter = half // 2
        to_other = lambda array: (array, swap)

        def feed_out(rows):
            return matmul_nt(line.next(rows), full_down_t)

        upstream = cotangent.astype(F32)

        def ffn_back(kept, taken, middle, upstream):
            branch = kept + taken.astype(F32)
            ffn_out, pull = jax.vjp(rms_norm, branch, gain_d)
            d_ffn, grad_gain = pull(upstream)
            return (middle + ffn_out).astype(BF16), line.mark(d_ffn.astype(BF16)), grad_gain

        def hidden_back(d_rows, active, slope):
            d_hidden = matmul(line.next(d_rows), full_down_t)
            d_gate = line.mark((d_hidden * slope.astype(F32)).astype(BF16))
            return d_gate, (d_hidden * active.astype(F32)).astype(BF16)

        give_1 = line.mark(feed_out(hidden_other[:quarter]).astype(BF16))
        line.open(to_other(give_1))
        give_2 = line.mark(feed_out(hidden_other[quarter:]).astype(BF16))
        kept_1 = line.mark(feed_out(hidden_own[:quarter]))
        kept_2 = line.mark(feed_out(hidden_own[quarter:]))
        (taken_1,) = line.close()
        line.open(to_other(give_2))
        output_1, d_ffn_1, grad_d_1 = ffn_back(
            line.next(kept_1), taken_1, middle[:quarter], upstream[:quarter]
        )
        (taken_2,) = line.close()
        line.open(to_other(d_ffn_1))
        output_2, d_ffn_2, grad_d_2 = ffn_back(
            line.next(kept_2), taken_2, middle[quarter:], upstream[quarter:]
        )
        d_gate_1, d_up_1 = hidden_back(d_ffn_1, active_own[:quarter], slope_own[:quarter])
        (d_ffn_3,) = line.close()
        line.open(to_other(d_ffn_2))
        d_gate_2, d_up_2 = hidden_back(d_ffn_2, active_own[quarter:], slope_own[quarter:])
        d_gate_3, d_up_3 = hidden_back(d_ffn_3, active_other[:quarter], slope_other[:quarter])
        (d_ffn_4,) = line.close()
        layer_output = jnp.concatenate([output_1, output_2], axis=0)
        grad_d = grad_d_1 + grad_d_2

        chunks = 4
        down = Scatter(dp, chunks)
        gate_grad = Scatter(dp, chunks)
        up_grad = Scatter(dp, chunks)
        output_grad = Scatter(dp, 1)
        query_grad = Scatter(dp, 1)
        pair_grad = Scatter(dp, 1)
        d_ffn_t = line.mark(
            jnp.concatenate([d_ffn_1, d_ffn_2, d_ffn_3, line.next(d_ffn_4)], axis=0).T
        )
        line.mark(down.give(line.next(d_ffn_t), hidden))
        line.open(down.to_core())
        d_gate_4, d_up_4 = hidden_back(d_ffn_4, active_other[quarter:], slope_other[quarter:])
        d_gate_other = jnp.concatenate([d_gate_3, line.next(d_gate_4)], axis=0)
        d_up_other = jnp.concatenate([d_up_3, d_up_4], axis=0)
        (taken,) = line.close()
        line.mark(down.add(line, taken))

        def mid_back(d_gate, d_up):
            return matmul_nt(line.next(d_gate), full_gate) + matmul_nt(d_up, full_up)

        line.open(down.to_side(0))
        give = line.mark(mid_back(d_gate_other, d_up_other).astype(BF16))
        down.taken += line.close()

        line.open(down.to_side(1), to_other(give[:quarter]))
        d_gate = jnp.concatenate([line.next(d_gate_1), d_gate_2, d_gate_3, d_gate_4], axis=0)
        line.mark(gate_grad.give(mid_t, d_gate))
        side, taken_1 = line.close()
        down.taken.append(side)

        line.open(down.to_side(2), to_other(give[quarter:]), gate_grad.to_core())
        d_gate_own = jnp.concatenate([d_gate_1, d_gate_2], axis=0)
        d_up_own = jnp.concatenate([d_up_1, d_up_2], axis=0)
        kept = line.mark(mid_back(d_gate_own, d_up_own))
        side, taken_2, core = line.close()
        down.taken.append(side)

        line.open(down.to_side(3))
        taken = jnp.concatenate([taken_1, taken_2], axis=0)
        d_mid_norm, grad_c = pull_ffn_in(line.next(kept) + taken.astype(F32))
        d_middle = upstream + d_mid_norm
        d_branch, grad_b = pull_attn_out(d_middle)
        d_branch_own = line.mark(d_branch.astype(BF16))
        line.mark(gate_grad.add(line, core))
        down.taken += line.close()

        line.open(gate_grad.to_side(0), to_other(d_branch_own[:quarter]))
        down.total(line)
        d_up = jnp.concatenate([line.next(d_up_1), d_up_2, d_up_3, d_up_4], axis=0)
        line.mark(up_grad.give(mid_t, d_up))
        side, taken_1 = line.close()
        gate_grad.taken.append(side)

        line.open(gate_grad.to_side(1), to_other(d_branch_own[quarter:]), up_grad.to_core())
        side, taken_2, core = line.close()
        gate_grad.taken.append(side)

        line.open(gate_grad.to_side(2))
        d_branch_other = jnp.concatenate([taken_1, line.next(taken_2)], axis=0)
        d_branch_rows = in_order(d_branch_own, d_branch_other)
        d_attended = line.mark(matmul(d_branch_rows, full_output_t).astype(BF16))
        line.mark(up_grad.add(line, core))
        gate_grad.taken += line.close()

        line.open(gate_grad.to_side(3))
        d_branch_t = line.mark(line.next(d_branch_rows).T)
        line.mark(output_grad.give(line.next(d_branch_t), attended))
        d_attended = d_attended.reshape(seq_count, SEQ_LEN, kv_local, head_group, HEAD_WIDTH)
        back_args = query_matrix_rows, key_matrix_rows, value_matrix_rows, log_total, d_attended
        d_query_1, d_key_1, d_value_1 = attend_back(line, *back_args, 0)
        gate_grad.taken += line.close()

        line.open(up_grad.to_side(0), output_grad.to_core())
        gate_grad.total(line)
        d_query_2, d_key_2, d_value_2 = attend_back(line, *back_args, 1)
        d_qkv = line.mark(
            jnp.concatenate(
                [
                    jnp.concatenate([d_query_1, d_query_2], axis=1)
                    .reshape(all_rows, query_cols)
                    .astype(BF16),
                    (d_key_1 + d_key_2).reshape(all_rows, key_cols).astype(BF16),
                    (d_value_1 + d_value_2).reshape(all_rows, key_cols).astype(BF16),
                ],
                axis=1,
            )
        )
        side, core = line.close()
        up_grad.taken.append(side)

        line.open(up_grad.to_side(1))
        d_qkv_own, d_qkv_other = halves(line.next(d_qkv))
        give = line.mark(matmul_nt(d_qkv_other, full_qkv).astype(BF16))
        line.mark(query_grad.give(input_t, line.next(d_qkv)[:, :query_cols]))
        line.mark(pair_grad.give(input_t, line.next(d_qkv)[:, query_cols:]))
        line.mark(output_grad.add(line, core))
        up_grad.taken += line.close()

        line.open(
            up_grad.to_side(2), query_grad.to_core(), pair_grad.to_core(), to_other(give[:quarter])
        )
        kept = line.mark(matmul_nt(line.next(d_qkv_own), full_qkv))
        side, query_core, pair_core, taken_1 = line.close()
        up_grad.taken.append(side)

        line.open(up_grad.to_side(3), to_other(give[quarter:]))
        line.mark(query_grad.add(line, query_core))
        line.mark(pair_grad.add(line, pair_core))
        side, taken_2 = line.close()
        up_grad.taken.append(side)

        line.open(output_grad.to_side(0))
        up_grad.total(line)
        _, pull_attn_in = jax.vjp(rms_norm, residual_in, gain_a)
        taken = jnp.concatenate([taken_1, taken_2], axis=0)
        d_input_norm, grad_a = pull_attn_in(line.next(kept) + taken.astype(F32))
        input_grad = line.mark(d_middle + d_input_norm)
        output_grad.taken += line.close()
        small = scatter_small(jnp.stack([grad_a, grad_b, grad_c, grad_d]), dp)

        line.open(query_grad.to_side(0))
        output_grad.total(line)
        query_grad.taken += line.close()

        line.open(pair_grad.to_side(0))
        query_grad.total(line)
        pair_grad.taken += line.close()
        pair_grad.total(line)
        grad_pair = pair_grad.result()
        return (
            layer_output,
            input_grad,
            query_grad.result(),
            grad_pair[:, :key_cols],
            grad_pair[:, key_cols:],
            output_grad.result().T,
            gate_grad.result(),
            up_grad.result(),
            down.result().T,
            small[0],
            small[1],
            small[2],
            small[3],
        )

    return body


def solution(mesh):
    rows = P(("dp", "tensor"), None)
    gain = P(("dp", "tensor"))
    into, out_of = P("dp", "tensor"), P("tensor", "dp")
    return jax.shard_map(
        make_body(mesh.shape["dp"]),
        mesh=mesh,
        in_specs=(rows, into, into, into, out_of, into, into, out_of, gain, gain, gain, gain, rows),
        out_specs=(rows, rows, into, into, into, out_of, into, into, out_of, gain, gain, gain, gain),
        check_vma=False,
    )
```

```python
import jax
import jax.numpy as jnp
from jax import lax
from jax.experimental import pallas as pl
from jax.experimental.pallas import tpu as pltpu
from jax.sharding import PartitionSpec as P

QUERY_HEADS = 8
KEY_VALUE_HEADS = 4
HEAD_WIDTH = 256
SEQ_LEN = 1024

EPSILON = 1e-06
LOGIT_CAP = 50.0

BF16 = jnp.bfloat16
F32 = jnp.float32
VMEM_BYTES = 56 * 1024 * 1024


def rms_norm(values, gain):
    return values * lax.rsqrt(jnp.mean(values * values, axis=-1, keepdims=True) + EPSILON) * gain


def swap(rows):
    return lax.ppermute(rows, "tensor", [(0, 1), (1, 0)])


def flip(array, bit, dp):
    return lax.ppermute(array, "dp", [(i, i ^ (1 << bit)) for i in range(dp)])


def gather_small(piece, dp):
    other = swap(piece)
    whole = jnp.where(
        lax.axis_index("tensor") == 0,
        jnp.concatenate([piece, other], axis=1),
        jnp.concatenate([other, piece], axis=1),
    )
    bit = 0
    while (1 << bit) < dp:
        other = flip(whole, bit, dp)
        high = (lax.axis_index("dp") >> bit) & 1
        whole = jnp.where(
            high == 0,
            jnp.concatenate([whole, other], axis=1),
            jnp.concatenate([other, whole], axis=1),
        )
        bit += 1
    return whole


def scatter_small(partial, dp):
    bit = dp.bit_length() - 2
    while bit >= 0:
        half = partial.shape[1] // 2
        low, high = partial[:, :half], partial[:, half:]
        mine = (lax.axis_index("dp") >> bit) & 1
        keep = jnp.where(mine == 0, low, high)
        give = jnp.where(mine == 0, high, low)
        partial = keep + flip(give, bit, dp)
        bit -= 1
    half = partial.shape[1] // 2
    low, high = partial[:, :half], partial[:, half:]
    mine = lax.axis_index("tensor")
    keep = jnp.where(mine == 0, low, high)
    give = jnp.where(mine == 0, high, low)
    return keep + swap(give)


def dot(left, right):
    return lax.dot_general(left, right, (((1,), (0,)), ((), ())), preferred_element_type=F32)


def dot_nt(left, right):
    return lax.dot_general(left, right, (((1,), (1,)), ((), ())), preferred_element_type=F32)


def call(kernel, steps, scalars, inputs, outputs, scratch=()):
    in_specs = [
        pl.BlockSpec(block, index, pipeline_mode=pl.Buffered(1) if whole else None)
        for _, block, index, whole in inputs
    ]
    out_specs = [pl.BlockSpec(block, index) for _, _, block, index in outputs]
    shapes = [jax.ShapeDtypeStruct(shape, dtype) for shape, dtype, _, _ in outputs]
    return pl.pallas_call(
        kernel,
        grid_spec=pltpu.PrefetchScalarGridSpec(
            num_scalar_prefetch=1,
            grid=(steps,),
            in_specs=in_specs,
            out_specs=out_specs,
            scratch_shapes=list(scratch),
        ),
        out_shape=shapes,
        compiler_params=pltpu.CompilerParams(vmem_limit_bytes=VMEM_BYTES),
        cost_estimate=pl.CostEstimate(flops=1, bytes_accessed=1, transcendentals=0),
    )(jnp.stack(scalars).astype(jnp.int32), *(array for array, *_ in inputs))


def tile_of(extent, most=512):
    tile = most
    while extent % tile:
        tile //= 2
    return tile


def turned(pieces, scalars):
    rows = [piece.shape[0] for piece in pieces]
    width = pieces[0].shape[1]
    tile = tile_of(width, 768)

    def kernel(_, *refs):
        *ins, out = refs
        row = lax.broadcasted_iota(jnp.int32, (tile, tile), 0)
        column = lax.broadcasted_iota(jnp.int32, (tile, tile), 1)
        same = (row == column).astype(F32).astype(BF16)
        at = 0
        for ref, count in zip(ins, rows):
            out[:, at : at + count] = dot_nt(same, ref[...]).astype(BF16)
            at += count

    (out,) = call(
        kernel,
        width // tile,
        scalars,
        [(piece, (count, tile), lambda j, s: (0, j), False) for piece, count in zip(pieces, rows)],
        [((width, sum(rows)), BF16, (tile, sum(rows)), lambda j, s: (j, 0))],
    )
    return out


def feed(mid, full_first, gate_at, full_up, scalars):
    rows, width = mid.shape
    columns = full_up.shape[1]
    tile = tile_of(columns)

    def kernel(_, mid_ref, gate_ref, up_ref, hidden_ref, active_ref, slope_ref):
        gate = dot(mid_ref[...], gate_ref[...])
        up = dot(mid_ref[...], up_ref[...])
        inner = 0.7978845608028654 * (gate + 0.044715 * gate * gate * gate)
        bent = jnp.tanh(inner)
        half = 0.5 * (1.0 + bent)
        active = gate * half
        slope = half + gate * (0.5 * (1.0 - bent * bent)) * (
            0.7978845608028654 * (1.0 + 3 * 0.044715 * gate * gate)
        )
        hidden_ref[...] = (active * up).astype(BF16)
        active_ref[...] = active.astype(BF16)
        slope_ref[...] = (slope * up).astype(BF16)

    out = ((rows, columns), BF16, (rows, tile), lambda j, s: (0, j))
    first = gate_at // tile
    return call(
        kernel,
        columns // tile,
        scalars,
        [
            (mid, (rows, width), lambda j, s: (0, 0), True),
            (full_first, (width, tile), lambda j, s: (0, first + j), False),
            (full_up, (width, tile), lambda j, s: (0, j), False),
        ],
        [out] * 3,
    )


def feed_out(hidden, block, size, full_down_t, dtype, scalars):
    inner = hidden.shape[1]
    width = full_down_t.shape[0]
    tile = tile_of(width, 256)

    def kernel(_, hidden_ref, down_ref, out):
        out[...] = dot_nt(hidden_ref[...], down_ref[...]).astype(dtype)

    (out,) = call(
        kernel,
        width // tile,
        scalars,
        [
            (hidden, (size, inner), lambda j, s: (block, 0), True),
            (full_down_t, (tile, inner), lambda j, s: (j, 0), False),
        ],
        [((size, width), dtype, (size, tile), lambda j, s: (0, j))],
    )
    return out


def hidden_back(line, pieces, full_down_t, scalars):
    width, columns = full_down_t.shape
    tile = tile_of(columns)
    count = len(pieces)
    sizes = [piece[0].shape[0] for piece in pieces]

    def kernel(_, *refs):
        down = refs[3 * count][...]
        for index in range(count):
            rows_ref, active_ref, slope_ref = refs[index::count][:3]
            gate_ref, up_ref = refs[3 * count + 1 + index :: count][:2]
            d_hidden = dot(rows_ref[...], down)
            gate_ref[...] = (d_hidden * slope_ref[...].astype(F32)).astype(BF16)
            up_ref[...] = (d_hidden * active_ref[...].astype(F32)).astype(BF16)

    rows = [line.next(piece[0]) if index == 0 else piece[0] for index, piece in enumerate(pieces)]
    place = lambda j, s: (0, j)
    factors = [
        (piece[factor], (size, tile), lambda j, s, block=piece[3]: (block, j), False)
        for factor in (1, 2)
        for piece, size in zip(pieces, sizes)
    ]
    outs = line.mark(
        call(
            kernel,
            columns // tile,
            scalars,
            [(array, array.shape, lambda j, s: (0, 0), True) for array in rows]
            + factors
            + [(full_down_t, (width, tile), lambda j, s: (0, j), False)],
            [((size, columns), BF16, (size, tile), place) for size in sizes] * 2,
        )
    )
    return outs[:count], outs[count:]


def mid_back(d_gate, d_up, full_first, gate_at, full_up, dtype, scalars):
    inner = d_gate[0].shape[1]
    width = full_up.shape[0]
    tile = tile_of(width, 256)
    part = 1536
    parts = inner // part
    count = len(d_gate)

    def kernel(_, *refs):
        gates, ups, refs = refs[:count], refs[count : 2 * count], refs[2 * count :]
        for gate_ref, up_ref, out in zip(gates, ups, refs[parts + 1 :]):
            total = dot_nt(up_ref[...], refs[parts][...])
            for index in range(parts):
                here = slice(index * part, (index + 1) * part)
                total += dot_nt(gate_ref[:, here], refs[index][...])
            out[...] = total.astype(dtype)

    return call(
        kernel,
        width // tile,
        scalars,
        [(piece, piece.shape, lambda j, s: (0, 0), True) for piece in [*d_gate, *d_up]]
        + [
            (full_first, (tile, part), lambda j, s, index=index: (j, gate_at // part + index), False)
            for index in range(parts)
        ]
        + [(full_up, (tile, inner), lambda j, s: (j, 0), False)],
        [
            ((piece.shape[0], width), dtype, (piece.shape[0], tile), lambda j, s: (0, j))
            for piece in d_gate
        ],
    )


def dot_tn(left, right):
    return lax.dot_general(left, right, (((0,), (0,)), ((), ())), preferred_element_type=F32)


def soft(query, keys, start):
    scores = dot_nt(query, keys)
    tangent = jnp.tanh(scores * (HEAD_WIDTH**-0.5 / LOGIT_CAP))
    row = lax.broadcasted_iota(jnp.int32, scores.shape, 0) + start
    column = lax.broadcasted_iota(jnp.int32, scores.shape, 1)
    capped = jnp.where(column <= row, LOGIT_CAP * tangent, -jnp.inf)
    terms = jnp.exp(capped - jnp.max(capped, axis=1, keepdims=True))
    return terms / jnp.sum(terms, axis=1, keepdims=True), tangent


def attend(qkv, heads, group, length, scalars, block=256):
    total = qkv.shape[0]
    block = min(block, length)
    seqs = total // length

    def kernel(_, query_ref, key_ref, value_ref, out_ref):
        for start in range(0, length, block):
            end = start + block
            weights, _ = soft(query_ref[start:end, :], key_ref[:end, :], start)
            out_ref[start:end, :] = dot(weights.astype(BF16), value_ref[:end, :]).astype(BF16)

    shape = (length, HEAD_WIDTH)
    (out,) = call(
        kernel,
        seqs * heads,
        scalars,
        [
            (qkv, shape, lambda j, s: (j // heads, j % heads), False),
            (qkv, shape, lambda j, s: (j // heads, heads + 2 * (j % heads // group)), False),
            (qkv, shape, lambda j, s: (j // heads, heads + 2 * (j % heads // group) + 1), False),
        ],
        [((total, heads * HEAD_WIDTH), BF16, shape, lambda j, s: (j // heads, j % heads))],
    )
    return out


def attend_back(qkv, d_attended, heads, group, length, scalars, block=256):
    total = qkv.shape[0]
    block = min(block, length)
    seqs = total // length
    key_heads = heads // group
    scale = HEAD_WIDTH**-0.5

    def kernel(_, query_ref, pair_ref, d_ref, d_query_ref, d_pair_ref, d_key, d_value):
        d_key[...] = jnp.zeros_like(d_key)
        d_value[...] = jnp.zeros_like(d_value)
        for member in range(group):
            columns = slice(member * HEAD_WIDTH, (member + 1) * HEAD_WIDTH)
            for start in range(0, length, block):
                end = start + block
                query = query_ref[start:end, columns]
                d_rows = d_ref[start:end, columns]
                keys, values = pair_ref[:end, :HEAD_WIDTH], pair_ref[:end, HEAD_WIDTH:]
                weights, tangent = soft(query, keys, start)
                d_soft = dot_nt(d_rows, values)
                d_capped = weights * (
                    d_soft - jnp.sum(weights * d_soft, axis=1, keepdims=True)
                )
                d_scores = (d_capped * (1.0 - tangent * tangent)).astype(BF16)
                d_query_ref[start:end, columns] = (dot(d_scores, keys) * scale).astype(BF16)
                d_key[:end, :] += dot_tn(d_scores, query)
                d_value[:end, :] += dot_tn(weights.astype(BF16), d_rows)
        d_pair_ref[:, :HEAD_WIDTH] = (d_key[...] * scale).astype(BF16)
        d_pair_ref[:, HEAD_WIDTH:] = d_value[...].astype(BF16)

    wide, pair = (length, group * HEAD_WIDTH), (length, 2 * HEAD_WIDTH)
    first_pair = heads // 2
    place = lambda j, s: (j // key_heads, j % key_heads)
    return call(
        kernel,
        seqs * key_heads,
        scalars,
        [
            (qkv, wide, place, False),
            (qkv, pair, lambda j, s: (j // key_heads, first_pair + j % key_heads), False),
            (d_attended, wide, place, False),
        ],
        [
            ((total, heads * HEAD_WIDTH), BF16, wide, place),
            ((total, key_heads * 2 * HEAD_WIDTH), BF16, pair, place),
        ],
        scratch=[pltpu.VMEM((length, HEAD_WIDTH), F32)] * 2,
    )


class Grad:
    def __init__(self, dp, chunks, lefts, rights, first_column, columns, scalars):
        self.dp, self.chunks, self.scalars = dp, chunks, scalars
        width = lefts[0].shape[0]
        self.rest, self.rows = dp // 4, width // dp
        self.lefts = [left.reshape(self.rest, 2, 2, self.rows, left.shape[1]) for left in lefts]
        self.rights = rights
        self.columns, self.tile = columns, tile_of(columns)
        self.first = first_column // self.tile
        self.count = len(lefts) + len(rights)

    def inputs(self, block, place):
        return [
            (
                left,
                (self.rest, block, None, *left.shape[3:]),
                lambda j, s: (0, *place(s), 0, 0),
                True,
            )
            for left in self.lefts
        ] + [
            (array, (size, self.tile), lambda j, s, row=row: (row(s), self.first + j), False)
            for array, size, row in self.rights
        ]

    def product(self, refs):
        return sum_of_products(refs[: len(self.lefts)], refs[len(self.lefts) : self.count])

    def run(self, kernel, inputs, outputs):
        return call(kernel, self.columns // self.tile, self.scalars, inputs, outputs)

    def give(self):
        def kernel(_, *refs):
            refs[-1][...] = self.product(refs).astype(BF16)

        shape = (self.rest, 2, self.rows)
        (self.given,) = self.run(
            kernel,
            self.inputs(2, lambda s: (0, 1 - s[0])),
            [((*shape, self.columns), BF16, (*shape, self.tile), lambda j, s: (0, 0, 0, j))],
        )
        return self.given

    def to_core(self):
        return self.given, lambda array: flip(array, 0, self.dp)

    def side(self, from_core):
        self.from_core = from_core
        size = self.rest // self.chunks

        def kernel(_, *refs):
            core = refs[self.count]
            result = (self.product(refs) + core[...].astype(F32)).astype(BF16)
            for index, out in enumerate(refs[self.count + 1 :]):
                out[...] = result[index * size : (index + 1) * size]

        self.give_side = self.run(
            kernel,
            self.inputs(None, lambda s: (1 - s[1], s[0]))
            + [
                (
                    from_core,
                    (self.rest, None, self.rows, self.tile),
                    lambda j, s: (0, 1 - s[1], 0, j),
                    False,
                )
            ],
            [
                (
                    (size, self.rows, self.columns),
                    BF16,
                    (size, self.rows, self.tile),
                    lambda j, s: (0, 0, j),
                )
            ]
            * self.chunks,
        )
        return self.give_side[0]

    def to_side(self, chunk):
        return self.give_side[chunk], lambda array: flip(array, 1, self.dp)

    def own(self, *from_side):
        size = self.rest // self.chunks

        def kernel(_, *refs):
            core, sides, out = refs[self.count], refs[self.count + 1 : -1], refs[-1]
            result = self.product(refs) + core[...].astype(F32)
            for index, ref in enumerate(sides):
                here = slice(index * size, (index + 1) * size)
                out[here] = (result[here] + ref[...].astype(F32)).astype(BF16)

        place = lambda j, s: (0, 0, j)
        (self.total,) = self.run(
            kernel,
            self.inputs(None, lambda s: (s[1], s[0]))
            + [
                (
                    self.from_core,
                    (self.rest, None, self.rows, self.tile),
                    lambda j, s: (0, s[1], 0, j),
                    False,
                )
            ]
            + [(part, (size, self.rows, self.tile), place, False) for part in from_side],
            [
                (
                    (self.rest, self.rows, self.columns),
                    BF16,
                    (self.rest, self.rows, self.tile),
                    place,
                )
            ],
        )
        return self.total

    def along_rest(self, line):
        groups = [[low + 4 * high for high in range(self.rest)] for low in range(4)]
        self.sums = lax.psum_scatter(
            line.next(self.total).reshape(-1, self.columns),
            "dp",
            scatter_dimension=0,
            axis_index_groups=groups,
            tiled=True,
        )

    def arrive(self, line):
        (self.sums,) = line.land(self.sums)

    def result(self):
        return self.sums.astype(F32)


def sum_of_products(lefts, rights):
    *lead, rows, _ = lefts[0].shape
    columns = rights[0].shape[1]
    count = 1
    for extent in lead:
        count *= extent
    rights = [right[...] for right in rights]
    pairs, index = [], 0
    for left in lefts:
        left, at = left[...], 0
        while at < left.shape[-1]:
            size = rights[index].shape[0]
            pairs.append((left[..., at : at + size], rights[index]))
            at += size
            index += 1

    def total(pick_block):
        result = None
        for left, right in pairs:
            term = dot(pick_block(left), right)
            result = term if result is None else result + term
        return result

    if rows % 16 == 0:
        blocks = total(lambda left: left.reshape(count * rows, left.shape[-1]))
    else:
        blocks = jnp.stack(
            [
                total(lambda left, block=block: left.reshape(count, rows, -1)[block])
                for block in range(count)
            ]
        )
    return blocks.reshape(*lead, rows, columns)


def tied(*arrays):
    return lax.optimization_barrier(arrays)


class Line:
    def __init__(self):
        self.last = None

    def next(self, array):
        if self.last is not None:
            array, _ = tied(array, self.last)
        return array

    def mark(self, array):
        self.last = array[0] if isinstance(array, (list, tuple)) else array
        return array

    def send(self, *transfers):
        return [send(self.next(array)) for array, send in transfers]

    def land(self, *flying):
        *taken, self.last = tied(*flying, self.last)
        return taken


def projected(pieces, weights, first_column, columns, scalars):
    count = len(pieces)
    half = sum(piece.shape[0] for piece in pieces) // 2
    width = pieces[0].shape[1]
    tile = tile_of(columns)

    def kernel(scalar_ref, *refs):
        *ins, weight_ref, out = refs
        weight = weight_ref[...]
        at = 0
        for ref in ins:
            owner = scalar_ref[2] if at < half else 1 - scalar_ref[2]
            size = ref.shape[0]
            start = pl.multiple_of(owner * half + at % half, size)
            out[pl.ds(start, size), :] = dot(ref[...], weight).astype(BF16)
            at += size

    (out,) = call(
        kernel,
        columns // tile,
        scalars,
        [(piece, piece.shape, lambda j, s: (0, 0), True) for piece in pieces]
        + [(weights, (width, tile), lambda j, s: (0, first_column // tile + j), False)],
        [((2 * half, columns), BF16, (2 * half, tile), lambda j, s: (0, j))],
    )
    return out


def projected_back(sources, weights, owner, pieces, dtype, scalars):
    half = sources[0][0].shape[0] // 2
    width = weights.shape[0]
    tile = tile_of(width, 256)
    size = half // pieces
    count = len(sources)

    def kernel(_, *refs):
        total = None
        for rows, weight in zip(refs[:count], refs[count : 2 * count]):
            term = dot_nt(rows[...], weight[...])
            total = term if total is None else total + term
        result = total.astype(dtype)
        for index, out in enumerate(refs[2 * count :]):
            out[...] = result[index * size : (index + 1) * size]

    return call(
        kernel,
        width // tile,
        scalars,
        [
            (array, (half, array.shape[1]), lambda j, s: (owner(s), 0), True)
            for array, _ in sources
        ]
        + [
            (weights, (tile, array.shape[1]), lambda j, s, block=block: (j, block), False)
            for array, block in sources
        ],
        [((size, width), dtype, (size, tile), lambda j, s: (0, j))] * pieces,
    )


def make_body(dp):
    def body(
        layer_input,
        query_weight,
        key_weight,
        value_weight,
        w_output,
        w_gate,
        w_up,
        w_down,
        gain_attn_in,
        gain_attn_out,
        gain_ffn_in,
        gain_ffn_out,
        cotangent,
    ):
        line = Line()
        place, turn = lax.axis_index("dp"), lax.axis_index("tensor")
        scalars = [place & 1, (place >> 1) & 1, turn]
        to_other = lambda array: (array, swap)
        mine, theirs = (lambda s: s[2]), (lambda s: 1 - s[2])
        query_cols, key_cols = query_weight.shape[1], key_weight.shape[1]
        qkv_cols = query_cols + 2 * key_cols
        gate_at = qkv_cols + query_cols
        columns = w_gate.shape[1]
        half = layer_input.shape[0]
        quarter = half // 2
        heads = query_cols // HEAD_WIDTH
        group = QUERY_HEADS // KEY_VALUE_HEADS
        pairs = []
        for head in range(key_cols // HEAD_WIDTH):
            here = slice(head * HEAD_WIDTH, (head + 1) * HEAD_WIDTH)
            pairs += [key_weight[:, here], value_weight[:, here]]
        full_first = lax.all_gather(
            jnp.concatenate([query_weight, *pairs, w_output.T, w_gate], axis=1),
            "dp",
            axis=0,
            tiled=True,
        )
        full_up = lax.all_gather(w_up, "dp", axis=0, tiled=True)
        full_down_t = lax.all_gather(w_down.T, "dp", axis=0, tiled=True)
        gains = gather_small(
            jnp.stack([gain_attn_in, gain_attn_out, gain_ffn_in, gain_ffn_out]), dp
        )
        gain_a, gain_b, gain_c, gain_d = gains[0], gains[1], gains[2], gains[3]

        residual_in = layer_input.astype(F32)
        upstream = cotangent.astype(F32)
        input_own = line.mark(rms_norm(residual_in, gain_a).astype(BF16))
        input_other = swap(input_own)
        input_own_t = line.mark(turned([input_own], scalars))
        (input_other,) = line.land(input_other)
        input_other_t = line.mark(turned([input_other], scalars))
        qkv = line.mark(
            projected([input_own, line.next(input_other)], full_first, 0, qkv_cols, scalars)
        )
        attended = line.mark(attend(qkv, heads, group, SEQ_LEN, scalars))
        output_block = qkv_cols // query_cols
        (give,) = line.mark(
            projected_back([(attended, output_block)], full_first, theirs, 1, BF16, scalars)
        )
        (taken,) = line.send(to_other(give))
        (kept,) = line.mark(
            projected_back(
                [(line.next(attended), output_block)], full_first, mine, 1, F32, scalars
            )
        )
        branch_attn = kept + taken.astype(F32)
        middle, pull_attn_out = jax.vjp(
            lambda values, gain: residual_in + rms_norm(values, gain), branch_attn, gain_b
        )
        normed_mid_f, pull_ffn_in = jax.vjp(rms_norm, middle, gain_c)
        mid_own = line.mark(normed_mid_f.astype(BF16))
        (mid_other,) = line.send(to_other(mid_own))
        hidden_own, active_own, slope_own = line.mark(
            feed(mid_own, full_first, gate_at, full_up, scalars)
        )
        mid_own_t = line.mark(turned([line.next(mid_own)], scalars))
        (mid_other,) = line.land(mid_other)
        hidden_other, active_other, slope_other = line.mark(
            feed(line.next(mid_other), full_first, gate_at, full_up, scalars)
        )
        mid_other_t = line.mark(turned([line.next(mid_other)], scalars))

        def ffn_back(kept, taken, middle, upstream):
            branch = kept + taken.astype(F32)
            ffn_out, pull = jax.vjp(rms_norm, branch, gain_d)
            d_ffn, grad_gain = pull(upstream)
            return (middle + ffn_out).astype(BF16), line.mark(d_ffn.astype(BF16)), grad_gain

        low, high = slice(0, quarter), slice(quarter, half)
        give_1 = line.mark(
            feed_out(line.next(hidden_other), 0, quarter, full_down_t, BF16, scalars)
        )
        (taken_1,) = line.send(to_other(give_1))
        give_2 = line.mark(
            feed_out(line.next(hidden_other), 1, quarter, full_down_t, BF16, scalars)
        )
        (taken_1,) = line.land(taken_1)
        (taken_2,) = line.send(to_other(give_2))
        kept = line.mark(feed_out(line.next(hidden_own), 0, half, full_down_t, F32, scalars))
        output_1, d_ffn_1, grad_d_1 = ffn_back(
            line.next(kept)[low], taken_1, middle[low], upstream[low]
        )
        (taken_2,) = line.land(taken_2)
        (d_ffn_3,) = line.send(to_other(d_ffn_1))
        output_2, d_ffn_2, grad_d_2 = ffn_back(
            line.next(kept)[high], taken_2, middle[high], upstream[high]
        )
        d_ffn_own_t = line.mark(turned([line.next(d_ffn_1), d_ffn_2], scalars))
        (d_gate_1,), (d_up_1,) = hidden_back(
            line, [(d_ffn_1, active_own, slope_own, 0)], full_down_t, scalars
        )
        (d_ffn_3,) = line.land(d_ffn_3)
        (d_ffn_4,) = line.send(to_other(d_ffn_2))
        layer_output = jnp.concatenate([output_1, output_2], axis=0)
        grad_d = grad_d_1 + grad_d_2
        (d_gate_2, d_gate_3), (d_up_2, d_up_3) = hidden_back(
            line,
            [(d_ffn_2, active_own, slope_own, 1), (d_ffn_3, active_other, slope_other, 0)],
            full_down_t,
            scalars,
        )
        (d_ffn_4,) = line.land(d_ffn_4)
        d_ffn_other_t = line.mark(turned([line.next(d_ffn_3), d_ffn_4], scalars))

        first = lambda s: 0
        tile = tile_of(columns)
        tiles = columns // tile
        cuts = [0, 2 * tile, 5 * tile, columns]
        split = tile * -(-tiles // 2)
        halves = [(0, split), (split, columns - split)]
        hidden_rights = [(hidden_own, half, first), (hidden_other, half, first)]
        mid_lefts = [mid_own_t, mid_other_t]

        def down_part(part, chunks):
            lefts = [line.next(d_ffn_own_t), d_ffn_other_t]
            start, end = cuts[part], cuts[part + 1]
            return Grad(dp, chunks, lefts, hidden_rights, start, end - start, scalars)

        def mid_part(pieces, part):
            rights = [(line.next(piece), quarter, first) for piece in pieces]
            return Grad(dp, 2, mid_lefts, rights, *halves[part], scalars)

        def mid_back_of(gates, ups, dtype):
            gates = [line.next(gates[0]), *gates[1:]]
            return line.mark(mid_back(gates, ups, full_first, gate_at, full_up, dtype, scalars))

        down_0 = down_part(0, 1)
        line.mark(down_0.give())
        (core_0,) = line.send(down_0.to_core())
        down_1 = down_part(1, 1)
        line.mark(down_1.give())
        (core_0,) = line.land(core_0)
        line.mark(down_0.side(line.next(core_0)))

        down_0_side, core_1 = line.send(down_0.to_side(0), down_1.to_core())
        down_2 = down_part(2, 2)
        line.mark(down_2.give())
        (core_1,) = line.land(core_1)
        line.mark(down_1.side(line.next(core_1)))
        (d_gate_4,), (d_up_4,) = hidden_back(
            line, [(d_ffn_4, active_other, slope_other, 1)], full_down_t, scalars
        )
        (down_0_side,) = line.land(down_0_side)
        d_gates = [d_gate_1, d_gate_2, d_gate_3, d_gate_4]
        d_ups = [d_up_1, d_up_2, d_up_3, d_up_4]

        down_1_side, core_2 = line.send(down_1.to_side(0), down_2.to_core())
        line.mark(down_0.own(line.next(down_0_side)))
        gate_0 = mid_part(d_gates, 0)
        line.mark(gate_0.give())
        (core_2,) = line.land(core_2)
        line.mark(down_2.side(line.next(core_2)))
        gate_1 = mid_part(d_gates, 1)
        line.mark(gate_1.give())
        (down_1_side,) = line.land(down_1_side)

        side_0, core_0, core_1 = line.send(
            down_2.to_side(0), gate_0.to_core(), gate_1.to_core()
        )
        down_0.along_rest(line)
        line.mark(down_1.own(line.next(down_1_side)))
        core_0, core_1 = line.land(core_0, core_1)
        line.mark(gate_0.side(line.next(core_0)))
        (side_0,) = line.land(side_0)
        down_0.arrive(line)

        (side_1,) = line.send(down_2.to_side(1))
        down_1.along_rest(line)
        give_1, give_2 = mid_back_of(d_gates[2:], d_ups[2:], BF16)
        (side_1,) = line.land(side_1)

        gate_0_side_0, taken_1 = line.send(gate_0.to_side(0), to_other(give_1))
        line.mark(down_2.own(line.next(side_0), side_1))
        line.mark(gate_1.side(line.next(core_1)))
        up_0 = mid_part(d_ups, 0)
        line.mark(up_0.give())
        gate_0_side_0, taken_1 = line.land(gate_0_side_0, taken_1)
        down_1.arrive(line)

        gate_0_side_1, taken_2, core_0 = line.send(
            gate_0.to_side(1), to_other(give_2), up_0.to_core()
        )
        down_2.along_rest(line)
        kept_1, kept_2 = mid_back_of(d_gates[:2], d_ups[:2], F32)
        gate_0_side_1, taken_2, core_0 = line.land(gate_0_side_1, taken_2, core_0)

        (gate_1_side_0,) = line.send(gate_1.to_side(0))
        line.mark(gate_0.own(line.next(gate_0_side_0), gate_0_side_1))
        taken = jnp.concatenate([taken_1, taken_2], axis=0).astype(F32)
        d_mid_norm, grad_c = pull_ffn_in(
            jnp.concatenate([line.next(kept_1), kept_2], axis=0) + taken
        )
        d_middle = upstream + d_mid_norm
        d_branch, grad_b = pull_attn_out(d_middle)
        d_branch_own = line.mark(d_branch.astype(BF16))
        (gate_1_side_0,) = line.land(gate_1_side_0)
        down_2.arrive(line)

        gate_1_side_1, d_branch_3 = line.send(gate_1.to_side(1), to_other(d_branch_own[low]))
        gate_0.along_rest(line)
        line.mark(up_0.side(line.next(core_0)))
        up_1 = mid_part(d_ups, 1)
        line.mark(up_1.give())
        gate_1_side_1, d_branch_3 = line.land(gate_1_side_1, d_branch_3)

        up_0_side_0, core_1, d_branch_4 = line.send(
            up_0.to_side(0), up_1.to_core(), to_other(d_branch_own[high])
        )
        line.mark(gate_1.own(line.next(gate_1_side_0), gate_1_side_1))
        d_branch_own_t = line.mark(turned([line.next(d_branch_own)], scalars))
        (core_1,) = line.land(core_1)
        line.mark(up_1.side(line.next(core_1)))
        up_0_side_0, d_branch_4 = line.land(up_0_side_0, d_branch_4)
        gate_0.arrive(line)

        (up_0_side_1,) = line.send(up_0.to_side(1))
        gate_1.along_rest(line)
        d_attended = line.mark(
            projected(
                [line.next(d_branch_own), d_branch_3, d_branch_4],
                full_first,
                qkv_cols,
                query_cols,
                scalars,
            )
        )
        d_branch_other_t = line.mark(turned([line.next(d_branch_3), d_branch_4], scalars))
        output = Grad(
            dp,
            1,
            [d_branch_own_t, line.next(d_branch_other_t)],
            [(attended, half, mine), (attended, half, theirs)],
            0,
            query_cols,
            scalars,
        )
        line.mark(output.give())
        (up_0_side_1,) = line.land(up_0_side_1)

        up_1_side_0, core = line.send(up_1.to_side(0), output.to_core())
        line.mark(up_0.own(line.next(up_0_side_0), up_0_side_1))
        d_query, d_pair = line.mark(
            attend_back(qkv, line.next(d_attended), heads, group, SEQ_LEN, scalars)
        )
        up_1_side_0, core = line.land(up_1_side_0, core)
        gate_1.arrive(line)

        (up_1_side_1,) = line.send(up_1.to_side(1))
        up_0.along_rest(line)
        line.mark(output.side(line.next(core)))

        def input_part(array, width):
            rights = [(line.next(array), half, mine), (array, half, theirs)]
            return Grad(dp, 1, [input_own_t, input_other_t], rights, 0, width, scalars)

        query = input_part(d_query, query_cols)
        line.mark(query.give())
        pair = input_part(d_pair, 2 * key_cols)
        line.mark(pair.give())
        (up_1_side_1,) = line.land(up_1_side_1)

        output_side, query_core, pair_core = line.send(
            output.to_side(0), query.to_core(), pair.to_core()
        )
        line.mark(up_1.own(line.next(up_1_side_0), up_1_side_1))
        query_core, pair_core = line.land(query_core, pair_core)
        line.mark(query.side(line.next(query_core)))
        line.mark(pair.side(line.next(pair_core)))
        (output_side,) = line.land(output_side)
        up_0.arrive(line)

        (query_side,) = line.send(query.to_side(0))
        up_1.along_rest(line)
        line.mark(output.own(line.next(output_side)))
        give_1, give_2 = line.mark(
            projected_back(
                [(line.next(d_query), 0), (d_pair, 1)], full_first, theirs, 2, BF16, scalars
            )
        )
        (query_side,) = line.land(query_side)

        pair_side, taken_1, taken_2 = line.send(
            pair.to_side(0), to_other(give_1), to_other(give_2)
        )
        line.mark(query.own(line.next(query_side)))
        (kept,) = line.mark(
            projected_back(
                [(line.next(d_query), 0), (d_pair, 1)], full_first, mine, 1, F32, scalars
            )
        )
        (pair_side,) = line.land(pair_side)
        line.mark(pair.own(line.next(pair_side)))
        up_1.arrive(line)
        output.along_rest(line)
        output.arrive(line)
        query.along_rest(line)
        taken_1, taken_2 = line.land(taken_1, taken_2)
        _, pull_attn_in = jax.vjp(rms_norm, residual_in, gain_a)
        taken = jnp.concatenate([taken_1, taken_2], axis=0).astype(F32)
        d_input_norm, grad_a = pull_attn_in(line.next(kept) + taken)
        input_grad = line.mark(d_middle + d_input_norm)
        query.arrive(line)
        pair.along_rest(line)
        small = scatter_small(jnp.stack([grad_a, grad_b, grad_c, grad_d]), dp)

        down, gate, up = [down_0, down_1, down_2], [gate_0, gate_1], [up_0, up_1]
        grad_pair = pair.result().reshape(-1, key_cols // HEAD_WIDTH, 2, HEAD_WIDTH)
        grad_down = jnp.concatenate([part.result() for part in down], axis=1).T
        return (
            layer_output,
            input_grad,
            query.result(),
            grad_pair[:, :, 0].reshape(-1, key_cols),
            grad_pair[:, :, 1].reshape(-1, key_cols),
            output.result().T,
            jnp.concatenate([part.result() for part in gate], axis=1),
            jnp.concatenate([part.result() for part in up], axis=1),
            grad_down,
            small[0],
            small[1],
            small[2],
            small[3],
        )

    return body


def solution(mesh):
    rows = P(("dp", "tensor"), None)
    gain = P(("dp", "tensor"))
    into, out_of = P("dp", "tensor"), P("tensor", "dp")
    return jax.shard_map(
        make_body(mesh.shape["dp"]),
        mesh=mesh,
        in_specs=(rows, into, into, into, out_of, into, into, out_of, gain, gain, gain, gain, rows),
        out_specs=(rows, rows, into, into, into, out_of, into, into, out_of, gain, gain, gain, gain),
        check_vma=False,
    )
```

```python
import jax
import jax.numpy as jnp
from jax import lax
from jax.experimental import pallas as pl
from jax.experimental.pallas import tpu as pltpu
from jax.sharding import PartitionSpec as P

QUERY_HEADS = 8
KEY_VALUE_HEADS = 4
HEAD_WIDTH = 256
SEQ_LEN = 1024

EPSILON = 1e-06
LOGIT_CAP = 50.0

BF16 = jnp.bfloat16
F32 = jnp.float32
VMEM_BYTES = 56 * 1024 * 1024


def rms_norm(values, gain):
    return values * lax.rsqrt(jnp.mean(values * values, axis=-1, keepdims=True) + EPSILON) * gain


def swap(rows):
    return lax.ppermute(rows, "tensor", [(0, 1), (1, 0)])


def flip(array, bit, dp):
    return lax.ppermute(array, "dp", [(i, i ^ (1 << bit)) for i in range(dp)])


def gather_small(piece, dp):
    other = swap(piece)
    whole = jnp.where(
        lax.axis_index("tensor") == 0,
        jnp.concatenate([piece, other], axis=1),
        jnp.concatenate([other, piece], axis=1),
    )
    bit = 0
    while (1 << bit) < dp:
        other = flip(whole, bit, dp)
        high = (lax.axis_index("dp") >> bit) & 1
        whole = jnp.where(
            high == 0,
            jnp.concatenate([whole, other], axis=1),
            jnp.concatenate([other, whole], axis=1),
        )
        bit += 1
    return whole


def dot(left, right):
    return lax.dot_general(left, right, (((1,), (0,)), ((), ())), preferred_element_type=F32)


def dot_nt(left, right):
    return lax.dot_general(left, right, (((1,), (1,)), ((), ())), preferred_element_type=F32)


def call(kernel, steps, scalars, inputs, outputs, scratch=()):
    in_specs = [
        pl.BlockSpec(block, index, pipeline_mode=pl.Buffered(1) if whole else None)
        for _, block, index, whole in inputs
    ]
    out_specs = [pl.BlockSpec(block, index) for _, _, block, index in outputs]
    shapes = [jax.ShapeDtypeStruct(shape, dtype) for shape, dtype, _, _ in outputs]
    return pl.pallas_call(
        kernel,
        grid_spec=pltpu.PrefetchScalarGridSpec(
            num_scalar_prefetch=1,
            grid=(steps,),
            in_specs=in_specs,
            out_specs=out_specs,
            scratch_shapes=list(scratch),
        ),
        out_shape=shapes,
        compiler_params=pltpu.CompilerParams(vmem_limit_bytes=VMEM_BYTES),
        cost_estimate=pl.CostEstimate(flops=1, bytes_accessed=1, transcendentals=0),
    )(jnp.stack(scalars).astype(jnp.int32), *(array for array, *_ in inputs))


def tile_of(extent, most=512):
    tile = most
    while extent % tile:
        tile //= 2
    return tile


def turned(pieces, scalars):
    rows = [piece.shape[0] for piece in pieces]
    width = pieces[0].shape[1]
    tile = tile_of(width, 768)

    def kernel(_, *refs):
        *ins, out = refs
        row = lax.broadcasted_iota(jnp.int32, (tile, tile), 0)
        column = lax.broadcasted_iota(jnp.int32, (tile, tile), 1)
        same = (row == column).astype(F32).astype(BF16)
        at = 0
        for ref, count in zip(ins, rows):
            out[:, at : at + count] = dot_nt(same, ref[...]).astype(BF16)
            at += count

    (out,) = call(
        kernel,
        width // tile,
        scalars,
        [(piece, (count, tile), lambda j, s: (0, j), False) for piece, count in zip(pieces, rows)],
        [((width, sum(rows)), BF16, (tile, sum(rows)), lambda j, s: (j, 0))],
    )
    return out


def feed(mid, full_first, gate_at, full_up, scalars):
    rows, width = mid.shape
    columns = full_up.shape[1]
    tile = tile_of(columns)

    def kernel(_, mid_ref, gate_ref, up_ref, hidden_ref, active_ref, slope_ref):
        gate = dot(mid_ref[...], gate_ref[...])
        up = dot(mid_ref[...], up_ref[...])
        inner = 0.7978845608028654 * (gate + 0.044715 * gate * gate * gate)
        bent = jnp.tanh(inner)
        half = 0.5 * (1.0 + bent)
        active = gate * half
        slope = half + gate * (0.5 * (1.0 - bent * bent)) * (
            0.7978845608028654 * (1.0 + 3 * 0.044715 * gate * gate)
        )
        hidden_ref[...] = (active * up).astype(BF16)
        active_ref[...] = active.astype(BF16)
        slope_ref[...] = (slope * up).astype(BF16)

    out = ((rows, columns), BF16, (rows, tile), lambda j, s: (0, j))
    first = gate_at // tile
    return call(
        kernel,
        columns // tile,
        scalars,
        [
            (mid, (rows, width), lambda j, s: (0, 0), True),
            (full_first, (width, tile), lambda j, s: (0, first + j), False),
            (full_up, (width, tile), lambda j, s: (0, j), False),
        ],
        [out] * 3,
    )


def feed_out(hidden, block, size, full_down_t, dtype, scalars):
    inner = hidden.shape[1]
    width = full_down_t.shape[0]
    tile = tile_of(width, 256)

    def kernel(_, hidden_ref, down_ref, out):
        out[...] = dot_nt(hidden_ref[...], down_ref[...]).astype(dtype)

    (out,) = call(
        kernel,
        width // tile,
        scalars,
        [
            (hidden, (size, inner), lambda j, s: (block, 0), True),
            (full_down_t, (tile, inner), lambda j, s: (j, 0), False),
        ],
        [((size, width), dtype, (size, tile), lambda j, s: (0, j))],
    )
    return out


def hidden_back(line, pieces, full_down_t, scalars):
    width, columns = full_down_t.shape
    tile = tile_of(columns)
    count = len(pieces)
    sizes = [piece[0].shape[0] for piece in pieces]

    def kernel(_, *refs):
        down = refs[3 * count][...]
        for index in range(count):
            rows_ref, active_ref, slope_ref = refs[index::count][:3]
            gate_ref, up_ref = refs[3 * count + 1 + index :: count][:2]
            d_hidden = dot(rows_ref[...], down)
            gate_ref[...] = (d_hidden * slope_ref[...].astype(F32)).astype(BF16)
            up_ref[...] = (d_hidden * active_ref[...].astype(F32)).astype(BF16)

    rows = [line.next(piece[0]) if index == 0 else piece[0] for index, piece in enumerate(pieces)]
    place = lambda j, s: (0, j)
    factors = [
        (piece[factor], (size, tile), lambda j, s, block=piece[3]: (block, j), False)
        for factor in (1, 2)
        for piece, size in zip(pieces, sizes)
    ]
    outs = line.mark(
        call(
            kernel,
            columns // tile,
            scalars,
            [(array, array.shape, lambda j, s: (0, 0), True) for array in rows]
            + factors
            + [(full_down_t, (width, tile), lambda j, s: (0, j), False)],
            [((size, columns), BF16, (size, tile), place) for size in sizes] * 2,
        )
    )
    return outs[:count], outs[count:]


def mid_back(d_gate, d_up, full_first, gate_at, full_up, dtype, scalars):
    inner = d_gate[0].shape[1]
    width = full_up.shape[0]
    tile = tile_of(width, 256)
    part = 1536
    parts = inner // part
    count = len(d_gate)

    def kernel(_, *refs):
        gates, ups, refs = refs[:count], refs[count : 2 * count], refs[2 * count :]
        for gate_ref, up_ref, out in zip(gates, ups, refs[parts + 1 :]):
            total = dot_nt(up_ref[...], refs[parts][...])
            for index in range(parts):
                here = slice(index * part, (index + 1) * part)
                total += dot_nt(gate_ref[:, here], refs[index][...])
            out[...] = total.astype(dtype)

    return call(
        kernel,
        width // tile,
        scalars,
        [(piece, piece.shape, lambda j, s: (0, 0), True) for piece in [*d_gate, *d_up]]
        + [
            (full_first, (tile, part), lambda j, s, index=index: (j, gate_at // part + index), False)
            for index in range(parts)
        ]
        + [(full_up, (tile, inner), lambda j, s: (j, 0), False)],
        [
            ((piece.shape[0], width), dtype, (piece.shape[0], tile), lambda j, s: (0, j))
            for piece in d_gate
        ],
    )


def dot_tn(left, right):
    return lax.dot_general(left, right, (((0,), (0,)), ((), ())), preferred_element_type=F32)


def soft(query, keys, start):
    scores = dot_nt(query, keys)
    tangent = jnp.tanh(scores * (HEAD_WIDTH**-0.5 / LOGIT_CAP))
    row = lax.broadcasted_iota(jnp.int32, scores.shape, 0) + start
    column = lax.broadcasted_iota(jnp.int32, scores.shape, 1)
    capped = jnp.where(column <= row, LOGIT_CAP * tangent, -jnp.inf)
    terms = jnp.exp(capped - jnp.max(capped, axis=1, keepdims=True))
    return terms / jnp.sum(terms, axis=1, keepdims=True), tangent


def attend(qkv, heads, group, length, scalars, block=256):
    total = qkv.shape[0]
    block = min(block, length)
    seqs = total // length

    def kernel(_, query_ref, key_ref, value_ref, out_ref):
        for start in range(0, length, block):
            end = start + block
            weights, _ = soft(query_ref[start:end, :], key_ref[:end, :], start)
            out_ref[start:end, :] = dot(weights.astype(BF16), value_ref[:end, :]).astype(BF16)

    shape = (length, HEAD_WIDTH)
    (out,) = call(
        kernel,
        seqs * heads,
        scalars,
        [
            (qkv, shape, lambda j, s: (j // heads, j % heads), False),
            (qkv, shape, lambda j, s: (j // heads, heads + 2 * (j % heads // group)), False),
            (qkv, shape, lambda j, s: (j // heads, heads + 2 * (j % heads // group) + 1), False),
        ],
        [((total, heads * HEAD_WIDTH), BF16, shape, lambda j, s: (j // heads, j % heads))],
    )
    return out


def attend_back(qkv, d_attended, heads, group, length, scalars, block=256):
    total = qkv.shape[0]
    block = min(block, length)
    seqs = total // length
    key_heads = heads // group
    scale = HEAD_WIDTH**-0.5

    def kernel(_, query_ref, pair_ref, d_ref, d_query_ref, d_pair_ref, d_key, d_value):
        d_key[...] = jnp.zeros_like(d_key)
        d_value[...] = jnp.zeros_like(d_value)
        for member in range(group):
            columns = slice(member * HEAD_WIDTH, (member + 1) * HEAD_WIDTH)
            for start in range(0, length, block):
                end = start + block
                query = query_ref[start:end, columns]
                d_rows = d_ref[start:end, columns]
                keys, values = pair_ref[:end, :HEAD_WIDTH], pair_ref[:end, HEAD_WIDTH:]
                weights, tangent = soft(query, keys, start)
                d_soft = dot_nt(d_rows, values)
                d_capped = weights * (
                    d_soft - jnp.sum(weights * d_soft, axis=1, keepdims=True)
                )
                d_scores = (d_capped * (1.0 - tangent * tangent)).astype(BF16)
                d_query_ref[start:end, columns] = (dot(d_scores, keys) * scale).astype(BF16)
                d_key[:end, :] += dot_tn(d_scores, query)
                d_value[:end, :] += dot_tn(weights.astype(BF16), d_rows)
        d_pair_ref[:, :HEAD_WIDTH] = (d_key[...] * scale).astype(BF16)
        d_pair_ref[:, HEAD_WIDTH:] = d_value[...].astype(BF16)

    wide, pair = (length, group * HEAD_WIDTH), (length, 2 * HEAD_WIDTH)
    first_pair = heads // 2
    place = lambda j, s: (j // key_heads, j % key_heads)
    return call(
        kernel,
        seqs * key_heads,
        scalars,
        [
            (qkv, wide, place, False),
            (qkv, pair, lambda j, s: (j // key_heads, first_pair + j % key_heads), False),
            (d_attended, wide, place, False),
        ],
        [
            ((total, heads * HEAD_WIDTH), BF16, wide, place),
            ((total, key_heads * 2 * HEAD_WIDTH), BF16, pair, place),
        ],
        scratch=[pltpu.VMEM((length, HEAD_WIDTH), F32)] * 2,
    )


class Grad:
    def __init__(self, dp, chunks, lefts, rights, first_column, columns, scalars):
        self.dp, self.chunks, self.scalars = dp, chunks, scalars
        width = lefts[0].shape[0]
        self.rest, self.rows = dp // 4, width // dp
        self.lefts = [left.reshape(self.rest, 2, 2, self.rows, left.shape[1]) for left in lefts]
        self.rights = rights
        self.columns, self.tile = columns, tile_of(columns)
        self.first = first_column // self.tile
        self.count = len(lefts) + len(rights)

    def inputs(self, block, place):
        return [
            (
                left,
                (self.rest, block, None, *left.shape[3:]),
                lambda j, s: (0, *place(s), 0, 0),
                True,
            )
            for left in self.lefts
        ] + [
            (array, (size, self.tile), lambda j, s, row=row: (row(s), self.first + j), False)
            for array, size, row in self.rights
        ]

    def product(self, refs):
        return sum_of_products(refs[: len(self.lefts)], refs[len(self.lefts) : self.count])

    def run(self, kernel, inputs, outputs):
        return call(kernel, self.columns // self.tile, self.scalars, inputs, outputs)

    def give(self):
        def kernel(_, *refs):
            refs[-1][...] = self.product(refs).astype(BF16)

        shape = (self.rest, 2, self.rows)
        (self.given,) = self.run(
            kernel,
            self.inputs(2, lambda s: (0, 1 - s[0])),
            [((*shape, self.columns), BF16, (*shape, self.tile), lambda j, s: (0, 0, 0, j))],
        )
        return self.given

    def to_core(self):
        return self.given, lambda array: flip(array, 0, self.dp)

    def side(self, from_core):
        self.from_core = from_core
        size = self.rest // self.chunks

        def kernel(_, *refs):
            core = refs[self.count]
            result = (self.product(refs) + core[...].astype(F32)).astype(BF16)
            for index, out in enumerate(refs[self.count + 1 :]):
                out[...] = result[index * size : (index + 1) * size]

        self.give_side = self.run(
            kernel,
            self.inputs(None, lambda s: (1 - s[1], s[0]))
            + [
                (
                    from_core,
                    (self.rest, None, self.rows, self.tile),
                    lambda j, s: (0, 1 - s[1], 0, j),
                    False,
                )
            ],
            [
                (
                    (size, self.rows, self.columns),
                    BF16,
                    (size, self.rows, self.tile),
                    lambda j, s: (0, 0, j),
                )
            ]
            * self.chunks,
        )
        return self.give_side[0]

    def to_side(self, chunk):
        return self.give_side[chunk], lambda array: flip(array, 1, self.dp)

    def own(self, *from_side):
        size = self.rest // self.chunks

        def kernel(_, *refs):
            core, sides, out = refs[self.count], refs[self.count + 1 : -1], refs[-1]
            result = self.product(refs) + core[...].astype(F32)
            for index, ref in enumerate(sides):
                here = slice(index * size, (index + 1) * size)
                out[here] = (result[here] + ref[...].astype(F32)).astype(BF16)

        place = lambda j, s: (0, 0, j)
        (self.total,) = self.run(
            kernel,
            self.inputs(None, lambda s: (s[1], s[0]))
            + [
                (
                    self.from_core,
                    (self.rest, None, self.rows, self.tile),
                    lambda j, s: (0, s[1], 0, j),
                    False,
                )
            ]
            + [(part, (size, self.rows, self.tile), place, False) for part in from_side],
            [
                (
                    (self.rest, self.rows, self.columns),
                    BF16,
                    (self.rest, self.rows, self.tile),
                    place,
                )
            ],
        )
        return self.total

    def along_rest(self, line):
        groups = [[low + 4 * high for high in range(self.rest)] for low in range(4)]
        self.sums = lax.psum_scatter(
            line.next(self.total).reshape(-1, self.columns),
            "dp",
            scatter_dimension=0,
            axis_index_groups=groups,
            tiled=True,
        )

    def to_owner(self):
        place = lax.axis_index("dp") >> 2
        transfers = []
        for shift in range(1, self.rest):
            pairs = [(i, (i + 4 * shift) % self.dp) for i in range(self.dp)]
            part = lax.dynamic_index_in_dim(
                self.total, (place + shift) % self.rest, 0, keepdims=False
            )
            transfers.append((part, lambda array, pairs=pairs: lax.ppermute(array, "dp", pairs)))
        return transfers

    def gather(self, parts):
        place = lax.axis_index("dp") >> 2
        total = lax.dynamic_index_in_dim(self.total, place, 0, keepdims=False).astype(F32)
        self.sums = sum((part.astype(F32) for part in parts), total)

    def arrive(self, line):
        (self.sums,) = line.land(self.sums)

    def result(self):
        return self.sums.astype(F32)


def sum_of_products(lefts, rights):
    *lead, rows, _ = lefts[0].shape
    columns = rights[0].shape[1]
    count = 1
    for extent in lead:
        count *= extent
    rights = [right[...] for right in rights]
    pairs, index = [], 0
    for left in lefts:
        left, at = left[...], 0
        while at < left.shape[-1]:
            size = rights[index].shape[0]
            pairs.append((left[..., at : at + size], rights[index]))
            at += size
            index += 1

    def total(pick_block):
        result = None
        for left, right in pairs:
            term = dot(pick_block(left), right)
            result = term if result is None else result + term
        return result

    if rows % 16 == 0:
        blocks = total(lambda left: left.reshape(count * rows, left.shape[-1]))
    else:
        blocks = jnp.stack(
            [
                total(lambda left, block=block: left.reshape(count, rows, -1)[block])
                for block in range(count)
            ]
        )
    return blocks.reshape(*lead, rows, columns)


def tied(*arrays):
    return lax.optimization_barrier(arrays)


class Line:
    def __init__(self):
        self.last = None

    def next(self, array):
        if self.last is not None:
            array, _ = tied(array, self.last)
        return array

    def mark(self, array):
        self.last = array[0] if isinstance(array, (list, tuple)) else array
        return array

    def send(self, *transfers):
        return [send(self.next(array)) for array, send in transfers]

    def land(self, *flying):
        *taken, self.last = tied(*flying, self.last)
        return taken


def projected(pieces, weights, first_column, columns, scalars):
    count = len(pieces)
    half = sum(piece.shape[0] for piece in pieces) // 2
    width = pieces[0].shape[1]
    tile = tile_of(columns)

    def kernel(scalar_ref, *refs):
        *ins, weight_ref, out = refs
        weight = weight_ref[...]
        at = 0
        for ref in ins:
            owner = scalar_ref[2] if at < half else 1 - scalar_ref[2]
            size = ref.shape[0]
            start = pl.multiple_of(owner * half + at % half, size)
            out[pl.ds(start, size), :] = dot(ref[...], weight).astype(BF16)
            at += size

    (out,) = call(
        kernel,
        columns // tile,
        scalars,
        [(piece, piece.shape, lambda j, s: (0, 0), True) for piece in pieces]
        + [(weights, (width, tile), lambda j, s: (0, first_column // tile + j), False)],
        [((2 * half, columns), BF16, (2 * half, tile), lambda j, s: (0, j))],
    )
    return out


def projected_back(sources, weights, owner, pieces, dtype, scalars):
    half = sources[0][0].shape[0] // 2
    width = weights.shape[0]
    tile = tile_of(width, 256)
    size = half // pieces
    count = len(sources)

    def kernel(_, *refs):
        total = None
        for rows, weight in zip(refs[:count], refs[count : 2 * count]):
            term = dot_nt(rows[...], weight[...])
            total = term if total is None else total + term
        result = total.astype(dtype)
        for index, out in enumerate(refs[2 * count :]):
            out[...] = result[index * size : (index + 1) * size]

    return call(
        kernel,
        width // tile,
        scalars,
        [
            (array, (half, array.shape[1]), lambda j, s: (owner(s), 0), True)
            for array, _ in sources
        ]
        + [
            (weights, (tile, array.shape[1]), lambda j, s, block=block: (j, block), False)
            for array, block in sources
        ],
        [((size, width), dtype, (size, tile), lambda j, s: (0, j))] * pieces,
    )


def norms_back(line, sums, middle, gain_mid, upstream, branch, gain_branch, scalars):
    rows, width = middle.shape
    count = len(sums)
    size = sums[0][0].shape[0]
    block = 64
    steps, each = rows // block, size // block
    given = [(middle, gain_mid)] + ([] if branch is None else [(branch, gain_branch)])
    norms = len(given)
    outs = 1 if branch is None else 1 + count

    def back(values, gain, d_normed):
        values = values.astype(F32)
        scale = lax.rsqrt(jnp.mean(values * values, axis=1, keepdims=True) + EPSILON)
        normed = values * scale
        weighted = d_normed * gain
        inner = jnp.mean(weighted * normed, axis=1, keepdims=True)
        grad = scale * (weighted - normed * inner)
        return grad, jnp.sum(d_normed * normed, axis=0, keepdims=True)

    def kernel(_, *refs):
        parts, upstream_ref, refs = refs[: 2 * count], refs[2 * count], refs[2 * count + 1 :]
        values_refs, gain_refs, refs = refs[:norms], refs[norms : 2 * norms], refs[2 * norms :]
        grad_refs, gain_grad_refs = refs[:outs], refs[outs:]
        step = pl.program_id(0)

        @pl.when(step == 0)
        def _():
            for ref in gain_grad_refs:
                ref[...] = jnp.zeros_like(ref)

        for index in range(count):

            @pl.when(step // each == index)
            def _(index=index):
                d_normed = parts[2 * index][...] + parts[2 * index + 1][...].astype(F32)
                grad, grad_gain = back(values_refs[0][...], gain_refs[0][...], d_normed)
                gain_grad_refs[0][...] += grad_gain
                total = upstream_ref[...].astype(F32) + grad
                grad_refs[0][...] = total
                if norms > 1:
                    grad, grad_gain = back(values_refs[1][...], gain_refs[1][...], total)
                    gain_grad_refs[1][...] += grad_gain
                    grad_refs[1 + index][...] = grad.astype(BF16)

    def piece(index):
        return lambda j, s: (jnp.clip(j - index * each, 0, each - 1), 0)

    shape = (block, width)
    every = lambda j, s: (j, 0)
    once = lambda j, s: (0, 0)
    (first, *others), *later = sums
    sums = [(line.next(first), *others), *later]
    return line.mark(
        call(
            kernel,
            steps,
            scalars,
            [
                (array, shape, piece(index), False)
                for index, pair in enumerate(sums)
                for array in pair
            ]
            + [(array, shape, every, False) for array in (upstream, *(v for v, _ in given))]
            + [(gain[None], (1, width), once, True) for _, gain in given],
            [((rows, width), F32, shape, every)]
            + [((size, width), BF16, shape, piece(index)) for index in range(outs - 1)]
            + [((1, width), F32, (1, width), once)] * norms,
        )
    )


def to_owners(partial):
    count, width = partial.shape
    devices = lax.axis_size("dp") * lax.axis_size("tensor")
    parts = partial.reshape(count, devices, width // devices).transpose(1, 0, 2)
    return lax.all_to_all(parts, ("dp", "tensor"), 0, 0, tiled=True)


def make_body(dp):
    def body(
        layer_input,
        query_weight,
        key_weight,
        value_weight,
        w_output,
        w_gate,
        w_up,
        w_down,
        gain_attn_in,
        gain_attn_out,
        gain_ffn_in,
        gain_ffn_out,
        cotangent,
    ):
        line = Line()
        place, turn = lax.axis_index("dp"), lax.axis_index("tensor")
        scalars = [place & 1, (place >> 1) & 1, turn]
        to_other = lambda array: (array, swap)
        mine, theirs = (lambda s: s[2]), (lambda s: 1 - s[2])
        query_cols, key_cols = query_weight.shape[1], key_weight.shape[1]
        qkv_cols = query_cols + 2 * key_cols
        gate_at = qkv_cols + query_cols
        columns = w_gate.shape[1]
        half = layer_input.shape[0]
        quarter = half // 2
        heads = query_cols // HEAD_WIDTH
        group = QUERY_HEADS // KEY_VALUE_HEADS
        pairs = []
        for head in range(key_cols // HEAD_WIDTH):
            here = slice(head * HEAD_WIDTH, (head + 1) * HEAD_WIDTH)
            pairs += [key_weight[:, here], value_weight[:, here]]
        full_first = lax.all_gather(
            jnp.concatenate([query_weight, *pairs, w_output.T, w_gate], axis=1),
            "dp",
            axis=0,
            tiled=True,
        )
        full_up = lax.all_gather(w_up, "dp", axis=0, tiled=True)
        full_down_t = lax.all_gather(w_down.T, "dp", axis=0, tiled=True)
        gains = gather_small(
            jnp.stack([gain_attn_in, gain_attn_out, gain_ffn_in, gain_ffn_out]), dp
        )
        gain_a, gain_b, gain_c, gain_d = gains[0], gains[1], gains[2], gains[3]

        residual_in = layer_input.astype(F32)
        upstream = cotangent.astype(F32)
        input_own = line.mark(rms_norm(residual_in, gain_a).astype(BF16))
        input_other = swap(input_own)
        input_own_t = line.mark(turned([input_own], scalars))
        (input_other,) = line.land(input_other)
        input_other_t = line.mark(turned([input_other], scalars))
        qkv = line.mark(
            projected([input_own, line.next(input_other)], full_first, 0, qkv_cols, scalars)
        )
        attended = line.mark(attend(qkv, heads, group, SEQ_LEN, scalars))
        output_block = qkv_cols // query_cols
        (give,) = line.mark(
            projected_back([(attended, output_block)], full_first, theirs, 1, BF16, scalars)
        )
        (taken,) = line.send(to_other(give))
        (kept,) = line.mark(
            projected_back(
                [(line.next(attended), output_block)], full_first, mine, 1, F32, scalars
            )
        )
        branch_attn = kept + taken.astype(F32)
        middle = residual_in + rms_norm(branch_attn, gain_b)
        mid_own = line.mark(rms_norm(middle, gain_c).astype(BF16))
        (mid_other,) = line.send(to_other(mid_own))
        hidden_own, active_own, slope_own = line.mark(
            feed(mid_own, full_first, gate_at, full_up, scalars)
        )
        mid_own_t = line.mark(turned([line.next(mid_own)], scalars))
        (mid_other,) = line.land(mid_other)
        hidden_other, active_other, slope_other = line.mark(
            feed(line.next(mid_other), full_first, gate_at, full_up, scalars)
        )
        mid_other_t = line.mark(turned([line.next(mid_other)], scalars))

        def ffn_back(kept, taken, middle, upstream):
            branch = kept + taken.astype(F32)
            ffn_out, pull = jax.vjp(rms_norm, branch, gain_d)
            d_ffn, grad_gain = pull(upstream)
            return (middle + ffn_out).astype(BF16), line.mark(d_ffn.astype(BF16)), grad_gain

        low, high = slice(0, quarter), slice(quarter, half)
        give_1 = line.mark(
            feed_out(line.next(hidden_other), 0, quarter, full_down_t, BF16, scalars)
        )
        (taken_1,) = line.send(to_other(give_1))
        give_2 = line.mark(
            feed_out(line.next(hidden_other), 1, quarter, full_down_t, BF16, scalars)
        )
        (taken_1,) = line.land(taken_1)
        (taken_2,) = line.send(to_other(give_2))
        kept = line.mark(feed_out(line.next(hidden_own), 0, half, full_down_t, F32, scalars))
        output_1, d_ffn_1, grad_d_1 = ffn_back(
            line.next(kept)[low], taken_1, middle[low], upstream[low]
        )
        (taken_2,) = line.land(taken_2)
        (d_ffn_3,) = line.send(to_other(d_ffn_1))
        output_2, d_ffn_2, grad_d_2 = ffn_back(
            line.next(kept)[high], taken_2, middle[high], upstream[high]
        )
        d_ffn_own_t = line.mark(turned([line.next(d_ffn_1), d_ffn_2], scalars))
        (d_gate_1,), (d_up_1,) = hidden_back(
            line, [(d_ffn_1, active_own, slope_own, 0)], full_down_t, scalars
        )
        (d_ffn_3,) = line.land(d_ffn_3)
        (d_ffn_4,) = line.send(to_other(d_ffn_2))
        layer_output = jnp.concatenate([output_1, output_2], axis=0)
        grad_d = grad_d_1 + grad_d_2
        (d_gate_2, d_gate_3), (d_up_2, d_up_3) = hidden_back(
            line,
            [(d_ffn_2, active_own, slope_own, 1), (d_ffn_3, active_other, slope_other, 0)],
            full_down_t,
            scalars,
        )
        (d_ffn_4,) = line.land(d_ffn_4)
        d_ffn_other_t = line.mark(turned([line.next(d_ffn_3), d_ffn_4], scalars))

        first = lambda s: 0
        tile = tile_of(columns)
        tiles = columns // tile
        cuts = [0, 2 * tile, 5 * tile, columns]
        split = tile * -(-tiles // 2)
        halves = [(0, split), (split, columns - split)]
        hidden_rights = [(hidden_own, half, first), (hidden_other, half, first)]
        mid_lefts = [mid_own_t, mid_other_t]

        def down_part(part, chunks):
            lefts = [line.next(d_ffn_own_t), d_ffn_other_t]
            start, end = cuts[part], cuts[part + 1]
            return Grad(dp, chunks, lefts, hidden_rights, start, end - start, scalars)

        def mid_part(pieces, part):
            rights = [(line.next(piece), quarter, first) for piece in pieces]
            return Grad(dp, 2, mid_lefts, rights, *halves[part], scalars)

        def mid_back_of(gates, ups, dtype):
            gates = [line.next(gates[0]), *gates[1:]]
            return line.mark(mid_back(gates, ups, full_first, gate_at, full_up, dtype, scalars))

        down_0 = down_part(0, 1)
        line.mark(down_0.give())
        (core_0,) = line.send(down_0.to_core())
        down_1 = down_part(1, 1)
        line.mark(down_1.give())
        (core_0,) = line.land(core_0)
        line.mark(down_0.side(line.next(core_0)))

        down_0_side, core_1 = line.send(down_0.to_side(0), down_1.to_core())
        down_2 = down_part(2, 2)
        line.mark(down_2.give())
        (core_1,) = line.land(core_1)
        line.mark(down_1.side(line.next(core_1)))
        (down_0_side,) = line.land(down_0_side)

        down_1_side, core_2 = line.send(down_1.to_side(0), down_2.to_core())
        (d_gate_4,), (d_up_4,) = hidden_back(
            line, [(d_ffn_4, active_other, slope_other, 1)], full_down_t, scalars
        )
        d_gates = [d_gate_1, d_gate_2, d_gate_3, d_gate_4]
        d_ups = [d_up_1, d_up_2, d_up_3, d_up_4]
        line.mark(down_0.own(line.next(down_0_side)))
        gate_0 = mid_part(d_gates, 0)
        line.mark(gate_0.give())
        (core_2,) = line.land(core_2)
        line.mark(down_2.side(line.next(core_2)))
        (down_1_side,) = line.land(down_1_side)

        side_0, core_0 = line.send(down_2.to_side(0), gate_0.to_core())
        down_0.along_rest(line)
        line.mark(down_1.own(line.next(down_1_side)))
        gate_1 = mid_part(d_gates, 1)
        line.mark(gate_1.give())
        (core_0,) = line.land(core_0)
        line.mark(gate_0.side(line.next(core_0)))
        (side_0,) = line.land(side_0)
        down_0.arrive(line)

        side_1, core_1 = line.send(down_2.to_side(1), gate_1.to_core())
        down_1.along_rest(line)
        give_1, give_2 = mid_back_of(d_gates[2:], d_ups[2:], BF16)
        side_1, core_1 = line.land(side_1, core_1)

        gate_0_side_0, taken_1 = line.send(gate_0.to_side(0), to_other(give_1))
        line.mark(down_2.own(line.next(side_0), side_1))
        line.mark(gate_1.side(line.next(core_1)))
        up_0 = mid_part(d_ups, 0)
        line.mark(up_0.give())
        gate_0_side_0, taken_1 = line.land(gate_0_side_0, taken_1)
        down_1.arrive(line)

        gate_0_side_1, taken_2, core_0 = line.send(
            gate_0.to_side(1), to_other(give_2), up_0.to_core()
        )
        down_2.along_rest(line)
        kept_1, kept_2 = mid_back_of(d_gates[:2], d_ups[:2], F32)
        gate_0_side_1, taken_2, core_0 = line.land(gate_0_side_1, taken_2, core_0)

        (gate_1_side_0,) = line.send(gate_1.to_side(0))
        line.mark(gate_0.own(line.next(gate_0_side_0), gate_0_side_1))
        d_middle, d_branch_1, d_branch_2, grad_c, grad_b = norms_back(
            line,
            [(kept_1, taken_1), (kept_2, taken_2)],
            middle,
            gain_c,
            cotangent,
            branch_attn,
            gain_b,
            scalars,
        )
        (gate_1_side_0,) = line.land(gate_1_side_0)
        down_2.arrive(line)

        gate_1_side_1, d_branch_3 = line.send(gate_1.to_side(1), to_other(d_branch_1))
        gate_0.along_rest(line)
        line.mark(up_0.side(line.next(core_0)))
        up_1 = mid_part(d_ups, 1)
        line.mark(up_1.give())
        gate_1_side_1, d_branch_3 = line.land(gate_1_side_1, d_branch_3)

        up_0_side_0, core_1, d_branch_4 = line.send(
            up_0.to_side(0), up_1.to_core(), to_other(d_branch_2)
        )
        line.mark(gate_1.own(line.next(gate_1_side_0), gate_1_side_1))
        d_branch_own_t = line.mark(turned([line.next(d_branch_1), d_branch_2], scalars))
        (core_1,) = line.land(core_1)
        line.mark(up_1.side(line.next(core_1)))
        up_0_side_0, d_branch_4 = line.land(up_0_side_0, d_branch_4)
        gate_0.arrive(line)

        (up_0_side_1,) = line.send(up_0.to_side(1))
        gate_1.along_rest(line)
        d_attended = line.mark(
            projected(
                [line.next(d_branch_1), d_branch_2, d_branch_3, d_branch_4],
                full_first,
                qkv_cols,
                query_cols,
                scalars,
            )
        )
        d_branch_other_t = line.mark(turned([line.next(d_branch_3), d_branch_4], scalars))
        output = Grad(
            dp,
            1,
            [d_branch_own_t, line.next(d_branch_other_t)],
            [(attended, half, mine), (attended, half, theirs)],
            0,
            query_cols,
            scalars,
        )
        line.mark(output.give())
        (up_0_side_1,) = line.land(up_0_side_1)

        up_1_side_0, core = line.send(up_1.to_side(0), output.to_core())
        line.mark(up_0.own(line.next(up_0_side_0), up_0_side_1))
        d_query, d_pair = line.mark(
            attend_back(qkv, line.next(d_attended), heads, group, SEQ_LEN, scalars)
        )
        up_1_side_0, core = line.land(up_1_side_0, core)
        gate_1.arrive(line)

        (up_1_side_1,) = line.send(up_1.to_side(1))
        up_0.along_rest(line)
        line.mark(output.side(line.next(core)))

        def input_part(array, width):
            rights = [(line.next(array), half, mine), (array, half, theirs)]
            return Grad(dp, 1, [input_own_t, input_other_t], rights, 0, width, scalars)

        query = input_part(d_query, query_cols)
        line.mark(query.give())
        pair = input_part(d_pair, 2 * key_cols)
        line.mark(pair.give())
        give_1, give_2 = line.mark(
            projected_back(
                [(line.next(d_query), 0), (d_pair, 1)], full_first, theirs, 2, BF16, scalars
            )
        )
        (up_1_side_1,) = line.land(up_1_side_1)

        output_side, query_core, pair_core, taken_1 = line.send(
            output.to_side(0), query.to_core(), pair.to_core(), to_other(give_1)
        )
        line.mark(up_1.own(line.next(up_1_side_0), up_1_side_1))
        query_core, pair_core = line.land(query_core, pair_core)
        line.mark(query.side(line.next(query_core)))
        line.mark(pair.side(line.next(pair_core)))
        output_side, taken_1 = line.land(output_side, taken_1)
        up_0.arrive(line)

        query_side, taken_2 = line.send(query.to_side(0), to_other(give_2))
        up_1.along_rest(line)
        line.mark(output.own(line.next(output_side)))
        kept_1, kept_2 = line.mark(
            projected_back(
                [(line.next(d_query), 0), (d_pair, 1)], full_first, mine, 2, F32, scalars
            )
        )
        query_side, taken_2 = line.land(query_side, taken_2)
        line.mark(query.own(line.next(query_side)))

        pair_side, *query_parts = line.send(pair.to_side(0), *query.to_owner())
        input_grad, grad_a = norms_back(
            line,
            [(kept_1, taken_1), (kept_2, taken_2)],
            layer_input,
            gain_a,
            d_middle,
            None,
            None,
            scalars,
        )
        (pair_side,) = line.land(pair_side)
        up_1.arrive(line)
        line.mark(pair.own(line.next(pair_side)))
        query_parts = line.land(*query_parts)

        gain_grads = jnp.stack([grad_a[0], grad_b[0], grad_c[0], grad_d])
        gain_parts, *pair_parts = line.send((gain_grads, to_owners), *pair.to_owner())
        output.along_rest(line)
        small = jnp.sum(gain_parts, axis=0)
        query.gather(query_parts)
        pair.gather(pair_parts)

        down, gate, up = [down_0, down_1, down_2], [gate_0, gate_1], [up_0, up_1]
        grad_pair = pair.result().reshape(-1, key_cols // HEAD_WIDTH, 2, HEAD_WIDTH)
        grad_down = jnp.concatenate([part.result() for part in down], axis=1).T
        return (
            layer_output,
            input_grad,
            query.result(),
            grad_pair[:, :, 0].reshape(-1, key_cols),
            grad_pair[:, :, 1].reshape(-1, key_cols),
            output.result().T,
            jnp.concatenate([part.result() for part in gate], axis=1),
            jnp.concatenate([part.result() for part in up], axis=1),
            grad_down,
            small[0],
            small[1],
            small[2],
            small[3],
        )

    return body


def solution(mesh):
    rows = P(("dp", "tensor"), None)
    gain = P(("dp", "tensor"))
    into, out_of = P("dp", "tensor"), P("tensor", "dp")
    return jax.shard_map(
        make_body(mesh.shape["dp"]),
        mesh=mesh,
        in_specs=(rows, into, into, into, out_of, into, into, out_of, gain, gain, gain, gain, rows),
        out_specs=(rows, rows, into, into, into, out_of, into, into, out_of, gain, gain, gain, gain),
        check_vma=False,
    )
```

```python
import jax
import jax.numpy as jnp
from jax import lax
from jax.experimental import pallas as pl
from jax.experimental.pallas import tpu as pltpu
from jax.sharding import PartitionSpec as P

QUERY_HEADS = 8
KEY_VALUE_HEADS = 4
HEAD_WIDTH = 256
SEQ_LEN = 1024

EPSILON = 1e-06
LOGIT_CAP = 50.0

BF16 = jnp.bfloat16
F32 = jnp.float32
VMEM_BYTES = 56 * 1024 * 1024


def rms_norm(values, gain):
    return values * lax.rsqrt(jnp.mean(values * values, axis=-1, keepdims=True) + EPSILON) * gain


def swap(rows):
    return lax.ppermute(rows, "tensor", [(0, 1), (1, 0)])


def flip(array, bit, dp):
    return lax.ppermute(array, "dp", [(i, i ^ (1 << bit)) for i in range(dp)])


def gather_small(piece, dp):
    other = swap(piece)
    whole = jnp.where(
        lax.axis_index("tensor") == 0,
        jnp.concatenate([piece, other], axis=1),
        jnp.concatenate([other, piece], axis=1),
    )
    bit = 0
    while (1 << bit) < dp:
        other = flip(whole, bit, dp)
        high = (lax.axis_index("dp") >> bit) & 1
        whole = jnp.where(
            high == 0,
            jnp.concatenate([whole, other], axis=1),
            jnp.concatenate([other, whole], axis=1),
        )
        bit += 1
    return whole


def dot(left, right):
    return lax.dot_general(left, right, (((1,), (0,)), ((), ())), preferred_element_type=F32)


def dot_nt(left, right):
    return lax.dot_general(left, right, (((1,), (1,)), ((), ())), preferred_element_type=F32)


def call(kernel, steps, scalars, inputs, outputs, scratch=()):
    in_specs = [
        pl.BlockSpec(block, index, pipeline_mode=pl.Buffered(1) if whole else None)
        for _, block, index, whole in inputs
    ]
    out_specs = [pl.BlockSpec(block, index) for _, _, block, index in outputs]
    shapes = [jax.ShapeDtypeStruct(shape, dtype) for shape, dtype, _, _ in outputs]
    return pl.pallas_call(
        kernel,
        grid_spec=pltpu.PrefetchScalarGridSpec(
            num_scalar_prefetch=1,
            grid=(steps,),
            in_specs=in_specs,
            out_specs=out_specs,
            scratch_shapes=list(scratch),
        ),
        out_shape=shapes,
        compiler_params=pltpu.CompilerParams(vmem_limit_bytes=VMEM_BYTES),
        cost_estimate=pl.CostEstimate(flops=1, bytes_accessed=1, transcendentals=0),
    )(jnp.stack(scalars).astype(jnp.int32), *(array for array, *_ in inputs))


def tile_of(extent, most=512):
    tile = most
    while extent % tile:
        tile //= 2
    return tile


def turned(pieces, scalars):
    rows = [piece.shape[0] for piece in pieces]
    width = pieces[0].shape[1]
    tile = tile_of(width, 768)

    def kernel(_, *refs):
        *ins, out = refs
        row = lax.broadcasted_iota(jnp.int32, (tile, tile), 0)
        column = lax.broadcasted_iota(jnp.int32, (tile, tile), 1)
        same = (row == column).astype(F32).astype(BF16)
        at = 0
        for ref, count in zip(ins, rows):
            out[:, at : at + count] = dot_nt(same, ref[...]).astype(BF16)
            at += count

    (out,) = call(
        kernel,
        width // tile,
        scalars,
        [(piece, (count, tile), lambda j, s: (0, j), False) for piece, count in zip(pieces, rows)],
        [((width, sum(rows)), BF16, (tile, sum(rows)), lambda j, s: (j, 0))],
    )
    return out


def feed(mid, full_first, gate_at, full_up, scalars):
    rows, width = mid.shape
    columns = full_up.shape[1]
    tile = tile_of(columns)

    def kernel(_, mid_ref, gate_ref, up_ref, hidden_ref, active_ref, slope_ref):
        gate = dot(mid_ref[...], gate_ref[...])
        up = dot(mid_ref[...], up_ref[...])
        inner = 0.7978845608028654 * (gate + 0.044715 * gate * gate * gate)
        bent = jnp.tanh(inner)
        half = 0.5 * (1.0 + bent)
        active = gate * half
        slope = half + gate * (0.5 * (1.0 - bent * bent)) * (
            0.7978845608028654 * (1.0 + 3 * 0.044715 * gate * gate)
        )
        hidden_ref[...] = (active * up).astype(BF16)
        active_ref[...] = active.astype(BF16)
        slope_ref[...] = (slope * up).astype(BF16)

    out = ((rows, columns), BF16, (rows, tile), lambda j, s: (0, j))
    first = gate_at // tile
    return call(
        kernel,
        columns // tile,
        scalars,
        [
            (mid, (rows, width), lambda j, s: (0, 0), True),
            (full_first, (width, tile), lambda j, s: (0, first + j), False),
            (full_up, (width, tile), lambda j, s: (0, j), False),
        ],
        [out] * 3,
    )


def feed_out(hidden, block, size, full_down_t, dtype, scalars):
    inner = hidden.shape[1]
    width = full_down_t.shape[0]
    tile = tile_of(width, 256)

    def kernel(_, hidden_ref, down_ref, out):
        out[...] = dot_nt(hidden_ref[...], down_ref[...]).astype(dtype)

    (out,) = call(
        kernel,
        width // tile,
        scalars,
        [
            (hidden, (size, inner), lambda j, s: (block, 0), True),
            (full_down_t, (tile, inner), lambda j, s: (j, 0), False),
        ],
        [((size, width), dtype, (size, tile), lambda j, s: (0, j))],
    )
    return out


def hidden_back(line, pieces, full_down_t, scalars):
    width, columns = full_down_t.shape
    tile = tile_of(columns)
    count = len(pieces)
    sizes = [piece[0].shape[0] for piece in pieces]

    def kernel(_, *refs):
        down = refs[3 * count][...]
        for index in range(count):
            rows_ref, active_ref, slope_ref = refs[index::count][:3]
            gate_ref, up_ref = refs[3 * count + 1 + index :: count][:2]
            d_hidden = dot(rows_ref[...], down)
            gate_ref[...] = (d_hidden * slope_ref[...].astype(F32)).astype(BF16)
            up_ref[...] = (d_hidden * active_ref[...].astype(F32)).astype(BF16)

    rows = [line.next(piece[0]) if index == 0 else piece[0] for index, piece in enumerate(pieces)]
    place = lambda j, s: (0, j)
    factors = [
        (piece[factor], (size, tile), lambda j, s, block=piece[3]: (block, j), False)
        for factor in (1, 2)
        for piece, size in zip(pieces, sizes)
    ]
    outs = line.mark(
        call(
            kernel,
            columns // tile,
            scalars,
            [(array, array.shape, lambda j, s: (0, 0), True) for array in rows]
            + factors
            + [(full_down_t, (width, tile), lambda j, s: (0, j), False)],
            [((size, columns), BF16, (size, tile), place) for size in sizes] * 2,
        )
    )
    return outs[:count], outs[count:]


def mid_back(d_gate, d_up, full_first, gate_at, full_up, dtype, scalars):
    inner = d_gate[0].shape[1]
    width = full_up.shape[0]
    tile = tile_of(width, 256)
    part = 1536
    parts = inner // part
    count = len(d_gate)

    def kernel(_, *refs):
        gates, ups, refs = refs[:count], refs[count : 2 * count], refs[2 * count :]
        for gate_ref, up_ref, out in zip(gates, ups, refs[parts + 1 :]):
            total = dot_nt(up_ref[...], refs[parts][...])
            for index in range(parts):
                here = slice(index * part, (index + 1) * part)
                total += dot_nt(gate_ref[:, here], refs[index][...])
            out[...] = total.astype(dtype)

    return call(
        kernel,
        width // tile,
        scalars,
        [(piece, piece.shape, lambda j, s: (0, 0), True) for piece in [*d_gate, *d_up]]
        + [
            (full_first, (tile, part), lambda j, s, index=index: (j, gate_at // part + index), False)
            for index in range(parts)
        ]
        + [(full_up, (tile, inner), lambda j, s: (j, 0), False)],
        [
            ((piece.shape[0], width), dtype, (piece.shape[0], tile), lambda j, s: (0, j))
            for piece in d_gate
        ],
    )


def dot_tn(left, right):
    return lax.dot_general(left, right, (((0,), (0,)), ((), ())), preferred_element_type=F32)


def soft(query, keys, start):
    scores = dot_nt(query, keys)
    tangent = jnp.tanh(scores * (HEAD_WIDTH**-0.5 / LOGIT_CAP))
    row = lax.broadcasted_iota(jnp.int32, scores.shape, 0) + start
    column = lax.broadcasted_iota(jnp.int32, scores.shape, 1)
    capped = jnp.where(column <= row, LOGIT_CAP * tangent, -jnp.inf)
    terms = jnp.exp(capped - jnp.max(capped, axis=1, keepdims=True))
    return terms / jnp.sum(terms, axis=1, keepdims=True), tangent


def attend(qkv, heads, group, length, scalars, block=256):
    total = qkv.shape[0]
    block = min(block, length)
    seqs = total // length

    def kernel(_, query_ref, key_ref, value_ref, out_ref):
        for start in range(0, length, block):
            end = start + block
            weights, _ = soft(query_ref[start:end, :], key_ref[:end, :], start)
            out_ref[start:end, :] = dot(weights.astype(BF16), value_ref[:end, :]).astype(BF16)

    shape = (length, HEAD_WIDTH)
    (out,) = call(
        kernel,
        seqs * heads,
        scalars,
        [
            (qkv, shape, lambda j, s: (j // heads, j % heads), False),
            (qkv, shape, lambda j, s: (j // heads, heads + 2 * (j % heads // group)), False),
            (qkv, shape, lambda j, s: (j // heads, heads + 2 * (j % heads // group) + 1), False),
        ],
        [((total, heads * HEAD_WIDTH), BF16, shape, lambda j, s: (j // heads, j % heads))],
    )
    return out


def attend_back(qkv, d_attended, heads, group, length, scalars, block=256):
    total = qkv.shape[0]
    block = min(block, length)
    seqs = total // length
    key_heads = heads // group
    scale = HEAD_WIDTH**-0.5

    def kernel(_, query_ref, pair_ref, d_ref, d_query_ref, d_pair_ref, d_key, d_value):
        d_key[...] = jnp.zeros_like(d_key)
        d_value[...] = jnp.zeros_like(d_value)
        for member in range(group):
            columns = slice(member * HEAD_WIDTH, (member + 1) * HEAD_WIDTH)
            for start in range(0, length, block):
                end = start + block
                query = query_ref[start:end, columns]
                d_rows = d_ref[start:end, columns]
                keys, values = pair_ref[:end, :HEAD_WIDTH], pair_ref[:end, HEAD_WIDTH:]
                weights, tangent = soft(query, keys, start)
                d_soft = dot_nt(d_rows, values)
                d_capped = weights * (
                    d_soft - jnp.sum(weights * d_soft, axis=1, keepdims=True)
                )
                d_scores = (d_capped * (1.0 - tangent * tangent)).astype(BF16)
                d_query_ref[start:end, columns] = (dot(d_scores, keys) * scale).astype(BF16)
                d_key[:end, :] += dot_tn(d_scores, query)
                d_value[:end, :] += dot_tn(weights.astype(BF16), d_rows)
        d_pair_ref[:, :HEAD_WIDTH] = (d_key[...] * scale).astype(BF16)
        d_pair_ref[:, HEAD_WIDTH:] = d_value[...].astype(BF16)

    wide, pair = (length, group * HEAD_WIDTH), (length, 2 * HEAD_WIDTH)
    first_pair = heads // 2
    place = lambda j, s: (j // key_heads, j % key_heads)
    return call(
        kernel,
        seqs * key_heads,
        scalars,
        [
            (qkv, wide, place, False),
            (qkv, pair, lambda j, s: (j // key_heads, first_pair + j % key_heads), False),
            (d_attended, wide, place, False),
        ],
        [
            ((total, heads * HEAD_WIDTH), BF16, wide, place),
            ((total, key_heads * 2 * HEAD_WIDTH), BF16, pair, place),
        ],
        scratch=[pltpu.VMEM((length, HEAD_WIDTH), F32)] * 2,
    )


class Grad:
    def __init__(self, dp, chunks, lefts, rights, first_column, columns, scalars):
        self.dp, self.chunks, self.scalars = dp, chunks, scalars
        width = lefts[0].shape[0]
        self.rest, self.rows = dp // 4, width // dp
        self.lefts = [left.reshape(self.rest, 2, 2, self.rows, left.shape[1]) for left in lefts]
        self.rights = rights
        self.columns, self.tile = columns, tile_of(columns)
        self.first = first_column // self.tile
        self.count = len(lefts) + len(rights)

    def inputs(self, block, place):
        return [
            (
                left,
                (self.rest, block, None, *left.shape[3:]),
                lambda j, s: (0, *place(s), 0, 0),
                True,
            )
            for left in self.lefts
        ] + [
            (array, (size, self.tile), lambda j, s, row=row: (row(s), self.first + j), False)
            for array, size, row in self.rights
        ]

    def product(self, refs):
        return sum_of_products(refs[: len(self.lefts)], refs[len(self.lefts) : self.count])

    def run(self, kernel, inputs, outputs):
        return call(kernel, self.columns // self.tile, self.scalars, inputs, outputs)

    def give(self):
        def kernel(_, *refs):
            refs[-1][...] = self.product(refs).astype(BF16)

        shape = (self.rest, 2, self.rows)
        (self.given,) = self.run(
            kernel,
            self.inputs(2, lambda s: (0, 1 - s[0])),
            [((*shape, self.columns), BF16, (*shape, self.tile), lambda j, s: (0, 0, 0, j))],
        )
        return self.given

    def to_core(self):
        return self.given, lambda array: flip(array, 0, self.dp)

    def side(self, from_core):
        self.from_core = from_core
        size = self.rest // self.chunks

        def kernel(_, *refs):
            core = refs[self.count]
            result = (self.product(refs) + core[...].astype(F32)).astype(BF16)
            for index, out in enumerate(refs[self.count + 1 :]):
                out[...] = result[index * size : (index + 1) * size]

        self.give_side = self.run(
            kernel,
            self.inputs(None, lambda s: (1 - s[1], s[0]))
            + [
                (
                    from_core,
                    (self.rest, None, self.rows, self.tile),
                    lambda j, s: (0, 1 - s[1], 0, j),
                    False,
                )
            ],
            [
                (
                    (size, self.rows, self.columns),
                    BF16,
                    (size, self.rows, self.tile),
                    lambda j, s: (0, 0, j),
                )
            ]
            * self.chunks,
        )
        return self.give_side[0]

    def both(self, from_core):
        def kernel(_, *refs):
            result = self.product(refs) + refs[self.count][...].astype(F32)
            refs[-1][...] = result.astype(BF16)

        shape = (self.rest, 2, self.rows)
        place = lambda j, s: (0, 0, 0, j)
        (self.total,) = self.run(
            kernel,
            self.inputs(2, lambda s: (0, s[0]))
            + [(from_core, (*shape, self.tile), place, False)],
            [((*shape, self.columns), BF16, (*shape, self.tile), place)],
        )
        return self.total

    def to_side_last(self):
        side = (lax.axis_index("dp") >> 1) & 1
        parts = self.sums.reshape(2, self.rows, self.columns)
        self.sums = pick(parts, side)
        return pick(parts, 1 - side), lambda array: flip(array, 1, self.dp)

    def add_side(self, part):
        self.sums = self.sums.astype(F32) + part.astype(F32)

    def to_side(self, chunk):
        return self.give_side[chunk], lambda array: flip(array, 1, self.dp)

    def own(self, *from_side):
        size = self.rest // self.chunks

        def kernel(_, *refs):
            core, sides, out = refs[self.count], refs[self.count + 1 : -1], refs[-1]
            result = self.product(refs) + core[...].astype(F32)
            for index, ref in enumerate(sides):
                here = slice(index * size, (index + 1) * size)
                out[here] = (result[here] + ref[...].astype(F32)).astype(BF16)

        place = lambda j, s: (0, 0, j)
        (self.total,) = self.run(
            kernel,
            self.inputs(None, lambda s: (s[1], s[0]))
            + [
                (
                    self.from_core,
                    (self.rest, None, self.rows, self.tile),
                    lambda j, s: (0, s[1], 0, j),
                    False,
                )
            ]
            + [(part, (size, self.rows, self.tile), place, False) for part in from_side],
            [
                (
                    (self.rest, self.rows, self.columns),
                    BF16,
                    (self.rest, self.rows, self.tile),
                    place,
                )
            ],
        )
        return self.total

    def along_rest(self, line):
        groups = [[low + 4 * high for high in range(self.rest)] for low in range(4)]
        self.sums = lax.psum_scatter(
            line.next(self.total).reshape(-1, self.columns),
            "dp",
            scatter_dimension=0,
            axis_index_groups=groups,
            tiled=True,
        )

    def to_owner(self):
        place = lax.axis_index("dp") >> 2
        transfers = []
        for shift in range(1, self.rest):
            pairs = [(i, (i + 4 * shift) % self.dp) for i in range(self.dp)]
            part = pick(self.total, (place + shift) % self.rest)
            transfers.append((part, lambda array, pairs=pairs: lax.ppermute(array, "dp", pairs)))
        return transfers

    def gather(self, parts):
        place = lax.axis_index("dp") >> 2
        total = pick(self.total, place).astype(F32)
        self.sums = sum((part.astype(F32) for part in parts), total)

    def result(self):
        return self.sums.astype(F32)


def pick(array, index):
    return lax.dynamic_index_in_dim(array, index, 0, keepdims=False)


def sum_of_products(lefts, rights):
    *lead, rows, _ = lefts[0].shape
    columns = rights[0].shape[1]
    count = 1
    for extent in lead:
        count *= extent
    rights = [right[...] for right in rights]
    pairs, index = [], 0
    for left in lefts:
        left, at = left[...], 0
        while at < left.shape[-1]:
            size = rights[index].shape[0]
            pairs.append((left[..., at : at + size], rights[index]))
            at += size
            index += 1

    def total(pick_block):
        result = None
        for left, right in pairs:
            term = dot(pick_block(left), right)
            result = term if result is None else result + term
        return result

    if rows % 16 == 0:
        blocks = total(lambda left: left.reshape(count * rows, left.shape[-1]))
    else:
        blocks = jnp.stack(
            [
                total(lambda left, block=block: left.reshape(count, rows, -1)[block])
                for block in range(count)
            ]
        )
    return blocks.reshape(*lead, rows, columns)


def tied(*arrays):
    return lax.optimization_barrier(arrays)


class Line:
    def __init__(self):
        self.last = None

    def next(self, array):
        if self.last is not None:
            array, _ = tied(array, self.last)
        return array

    def mark(self, array):
        self.last = array[0] if isinstance(array, (list, tuple)) else array
        return array

    def send(self, *transfers):
        return [send(self.next(array)) for array, send in transfers]

    def land(self, *flying, sums=()):
        count = len(flying)
        *taken, self.last = tied(*flying, *(grad.sums for grad in sums), self.last)
        for grad, value in zip(sums, taken[count:]):
            grad.sums = value
        return taken[:count]


def projected(pieces, weights, first_column, columns, scalars):
    count = len(pieces)
    half = sum(piece.shape[0] for piece in pieces) // 2
    width = pieces[0].shape[1]
    tile = tile_of(columns)

    def kernel(scalar_ref, *refs):
        *ins, weight_ref, out = refs
        weight = weight_ref[...]
        at = 0
        for ref in ins:
            owner = scalar_ref[2] if at < half else 1 - scalar_ref[2]
            size = ref.shape[0]
            start = pl.multiple_of(owner * half + at % half, size)
            out[pl.ds(start, size), :] = dot(ref[...], weight).astype(BF16)
            at += size

    (out,) = call(
        kernel,
        columns // tile,
        scalars,
        [(piece, piece.shape, lambda j, s: (0, 0), True) for piece in pieces]
        + [(weights, (width, tile), lambda j, s: (0, first_column // tile + j), False)],
        [((2 * half, columns), BF16, (2 * half, tile), lambda j, s: (0, j))],
    )
    return out


def projected_back(sources, weights, owner, pieces, dtype, scalars):
    half = sources[0][0].shape[0] // 2
    width = weights.shape[0]
    tile = tile_of(width, 256)
    size = half // pieces
    count = len(sources)

    def kernel(_, *refs):
        total = None
        for rows, weight in zip(refs[:count], refs[count : 2 * count]):
            term = dot_nt(rows[...], weight[...])
            total = term if total is None else total + term
        result = total.astype(dtype)
        for index, out in enumerate(refs[2 * count :]):
            out[...] = result[index * size : (index + 1) * size]

    return call(
        kernel,
        width // tile,
        scalars,
        [
            (array, (half, array.shape[1]), lambda j, s: (owner(s), 0), True)
            for array, _ in sources
        ]
        + [
            (weights, (tile, array.shape[1]), lambda j, s, block=block: (j, block), False)
            for array, block in sources
        ],
        [((size, width), dtype, (size, tile), lambda j, s: (0, j))] * pieces,
    )


def norms_back(line, sums, middle, gain_mid, upstream, branch, gain_branch, scalars):
    rows, width = middle.shape
    count = len(sums)
    size = sums[0][0].shape[0]
    block = 64
    steps, each = rows // block, size // block
    given = [(middle, gain_mid)] + ([] if branch is None else [(branch, gain_branch)])
    norms = len(given)
    outs = 1 if branch is None else 1 + count

    def back(values, gain, d_normed):
        values = values.astype(F32)
        scale = lax.rsqrt(jnp.mean(values * values, axis=1, keepdims=True) + EPSILON)
        normed = values * scale
        weighted = d_normed * gain
        inner = jnp.mean(weighted * normed, axis=1, keepdims=True)
        grad = scale * (weighted - normed * inner)
        return grad, jnp.sum(d_normed * normed, axis=0, keepdims=True)

    def kernel(_, *refs):
        parts, upstream_ref, refs = refs[: 2 * count], refs[2 * count], refs[2 * count + 1 :]
        values_refs, gain_refs, refs = refs[:norms], refs[norms : 2 * norms], refs[2 * norms :]
        grad_refs, gain_grad_refs = refs[:outs], refs[outs:]
        step = pl.program_id(0)

        @pl.when(step == 0)
        def _():
            for ref in gain_grad_refs:
                ref[...] = jnp.zeros_like(ref)

        for index in range(count):

            @pl.when(step // each == index)
            def _(index=index):
                d_normed = parts[2 * index][...] + parts[2 * index + 1][...].astype(F32)
                grad, grad_gain = back(values_refs[0][...], gain_refs[0][...], d_normed)
                gain_grad_refs[0][...] += grad_gain
                total = upstream_ref[...].astype(F32) + grad
                grad_refs[0][...] = total
                if norms > 1:
                    grad, grad_gain = back(values_refs[1][...], gain_refs[1][...], total)
                    gain_grad_refs[1][...] += grad_gain
                    grad_refs[1 + index][...] = grad.astype(BF16)

    def piece(index):
        return lambda j, s: (jnp.clip(j - index * each, 0, each - 1), 0)

    shape = (block, width)
    every = lambda j, s: (j, 0)
    once = lambda j, s: (0, 0)
    (first, *others), *later = sums
    sums = [(line.next(first), *others), *later]
    return line.mark(
        call(
            kernel,
            steps,
            scalars,
            [
                (array, shape, piece(index), False)
                for index, pair in enumerate(sums)
                for array in pair
            ]
            + [(array, shape, every, False) for array in (upstream, *(v for v, _ in given))]
            + [(gain[None], (1, width), once, True) for _, gain in given],
            [((rows, width), F32, shape, every)]
            + [((size, width), BF16, shape, piece(index)) for index in range(outs - 1)]
            + [((1, width), F32, (1, width), once)] * norms,
        )
    )


def to_owners(partial):
    count, width = partial.shape
    devices = lax.axis_size("dp") * lax.axis_size("tensor")
    parts = partial.reshape(count, devices, width // devices).transpose(1, 0, 2)
    return lax.all_to_all(parts, ("dp", "tensor"), 0, 0, tiled=True)


def make_body(dp):
    def body(
        layer_input,
        query_weight,
        key_weight,
        value_weight,
        w_output,
        w_gate,
        w_up,
        w_down,
        gain_attn_in,
        gain_attn_out,
        gain_ffn_in,
        gain_ffn_out,
        cotangent,
    ):
        line = Line()
        place, turn = lax.axis_index("dp"), lax.axis_index("tensor")
        scalars = [place & 1, (place >> 1) & 1, turn]
        to_other = lambda array: (array, swap)
        mine, theirs = (lambda s: s[2]), (lambda s: 1 - s[2])
        query_cols, key_cols = query_weight.shape[1], key_weight.shape[1]
        qkv_cols = query_cols + 2 * key_cols
        gate_at = qkv_cols + query_cols
        columns = w_gate.shape[1]
        half = layer_input.shape[0]
        quarter = half // 2
        heads = query_cols // HEAD_WIDTH
        group = QUERY_HEADS // KEY_VALUE_HEADS
        pairs = []
        for head in range(key_cols // HEAD_WIDTH):
            here = slice(head * HEAD_WIDTH, (head + 1) * HEAD_WIDTH)
            pairs += [key_weight[:, here], value_weight[:, here]]
        full_first = lax.all_gather(
            jnp.concatenate([query_weight, *pairs, w_output.T, w_gate], axis=1),
            "dp",
            axis=0,
            tiled=True,
        )
        full_up = lax.all_gather(w_up, "dp", axis=0, tiled=True)
        full_down_t = lax.all_gather(w_down.T, "dp", axis=0, tiled=True)
        gains = gather_small(
            jnp.stack([gain_attn_in, gain_attn_out, gain_ffn_in, gain_ffn_out]), dp
        )
        gain_a, gain_b, gain_c, gain_d = gains[0], gains[1], gains[2], gains[3]

        residual_in = layer_input.astype(F32)
        upstream = cotangent.astype(F32)
        input_own = line.mark(rms_norm(residual_in, gain_a).astype(BF16))
        input_other = swap(input_own)
        input_own_t = line.mark(turned([input_own], scalars))
        (input_other,) = line.land(input_other)
        input_other_t = line.mark(turned([input_other], scalars))
        qkv = line.mark(
            projected([input_own, line.next(input_other)], full_first, 0, qkv_cols, scalars)
        )
        attended = line.mark(attend(qkv, heads, group, SEQ_LEN, scalars))
        output_block = qkv_cols // query_cols
        (give,) = line.mark(
            projected_back([(attended, output_block)], full_first, theirs, 1, BF16, scalars)
        )
        (taken,) = line.send(to_other(give))
        (kept,) = line.mark(
            projected_back(
                [(line.next(attended), output_block)], full_first, mine, 1, F32, scalars
            )
        )
        branch_attn = kept + taken.astype(F32)
        middle = residual_in + rms_norm(branch_attn, gain_b)
        mid_own = line.mark(rms_norm(middle, gain_c).astype(BF16))
        (mid_other,) = line.send(to_other(mid_own))
        hidden_own, active_own, slope_own = line.mark(
            feed(mid_own, full_first, gate_at, full_up, scalars)
        )
        mid_own_t = line.mark(turned([line.next(mid_own)], scalars))
        (mid_other,) = line.land(mid_other)
        hidden_other, active_other, slope_other = line.mark(
            feed(line.next(mid_other), full_first, gate_at, full_up, scalars)
        )
        mid_other_t = line.mark(turned([line.next(mid_other)], scalars))

        def ffn_back(kept, taken, middle, upstream):
            branch = kept + taken.astype(F32)
            ffn_out, pull = jax.vjp(rms_norm, branch, gain_d)
            d_ffn, grad_gain = pull(upstream)
            return (middle + ffn_out).astype(BF16), line.mark(d_ffn.astype(BF16)), grad_gain

        low, high = slice(0, quarter), slice(quarter, half)
        give_1 = line.mark(
            feed_out(line.next(hidden_other), 0, quarter, full_down_t, BF16, scalars)
        )
        (taken_1,) = line.send(to_other(give_1))
        give_2 = line.mark(
            feed_out(line.next(hidden_other), 1, quarter, full_down_t, BF16, scalars)
        )
        (taken_1,) = line.land(taken_1)
        (taken_2,) = line.send(to_other(give_2))
        kept = line.mark(feed_out(line.next(hidden_own), 0, half, full_down_t, F32, scalars))
        output_1, d_ffn_1, grad_d_1 = ffn_back(
            line.next(kept)[low], taken_1, middle[low], upstream[low]
        )
        (taken_2,) = line.land(taken_2)
        (d_ffn_3,) = line.send(to_other(d_ffn_1))
        output_2, d_ffn_2, grad_d_2 = ffn_back(
            line.next(kept)[high], taken_2, middle[high], upstream[high]
        )
        d_ffn_own_t = line.mark(turned([line.next(d_ffn_1), d_ffn_2], scalars))
        (d_gate_1,), (d_up_1,) = hidden_back(
            line, [(d_ffn_1, active_own, slope_own, 0)], full_down_t, scalars
        )
        (d_ffn_3,) = line.land(d_ffn_3)
        (d_ffn_4,) = line.send(to_other(d_ffn_2))
        layer_output = jnp.concatenate([output_1, output_2], axis=0)
        grad_d = grad_d_1 + grad_d_2
        (d_gate_2, d_gate_3), (d_up_2, d_up_3) = hidden_back(
            line,
            [(d_ffn_2, active_own, slope_own, 1), (d_ffn_3, active_other, slope_other, 0)],
            full_down_t,
            scalars,
        )
        (d_ffn_4,) = line.land(d_ffn_4)
        d_ffn_other_t = line.mark(turned([line.next(d_ffn_3), d_ffn_4], scalars))

        first = lambda s: 0
        tile = tile_of(columns)
        tiles = columns // tile
        cuts = [0, 2 * tile, 4 * tile, columns]
        split = tile * -(-tiles // 2)
        halves = [(0, split), (split, columns - split)]
        hidden_rights = [(hidden_own, half, first), (hidden_other, half, first)]
        mid_lefts = [mid_own_t, mid_other_t]

        def down_part(part, chunks):
            lefts = [line.next(d_ffn_own_t), d_ffn_other_t]
            start, end = cuts[part], cuts[part + 1]
            return Grad(dp, chunks, lefts, hidden_rights, start, end - start, scalars)

        def mid_part(pieces, part):
            rights = [(line.next(piece), quarter, first) for piece in pieces]
            return Grad(dp, 2, mid_lefts, rights, *halves[part], scalars)

        def mid_back_of(gates, ups, dtype):
            gates = [line.next(gates[0]), *gates[1:]]
            return line.mark(mid_back(gates, ups, full_first, gate_at, full_up, dtype, scalars))

        down_0 = down_part(0, 1)
        line.mark(down_0.give())
        (core_0,) = line.send(down_0.to_core())
        down_2 = down_part(2, 2)
        line.mark(down_2.give())
        (core_0,) = line.land(core_0)
        line.mark(down_0.side(line.next(core_0)))

        down_0_side, core_2 = line.send(down_0.to_side(0), down_2.to_core())
        down_1 = down_part(1, 1)
        line.mark(down_1.give())
        (d_gate_4,), (d_up_4,) = hidden_back(
            line, [(d_ffn_4, active_other, slope_other, 1)], full_down_t, scalars
        )
        d_gates = [d_gate_1, d_gate_2, d_gate_3, d_gate_4]
        d_ups = [d_up_1, d_up_2, d_up_3, d_up_4]
        (core_2,) = line.land(core_2)
        line.mark(down_2.side(line.next(core_2)))
        (down_0_side,) = line.land(down_0_side)

        side_0, core_1 = line.send(down_2.to_side(0), down_1.to_core())
        line.mark(down_0.own(line.next(down_0_side)))
        gate_0 = mid_part(d_gates, 0)
        line.mark(gate_0.give())
        (core_1,) = line.land(core_1)
        line.mark(down_1.both(line.next(core_1)))
        gate_1 = mid_part(d_gates, 1)
        line.mark(gate_1.give())
        (side_0,) = line.land(side_0)

        side_1, core_0, core_1 = line.send(
            down_2.to_side(1), gate_0.to_core(), gate_1.to_core()
        )
        down_0.along_rest(line)
        give_1, give_2 = mid_back_of(d_gates[2:], d_ups[2:], BF16)
        core_0, core_1 = line.land(core_0, core_1)
        line.mark(gate_0.side(line.next(core_0)))
        (side_1,) = line.land(
            side_1, sums=[down_0]
        )

        gate_0_side_0, gate_0_side_1, taken_1, taken_2 = line.send(
            gate_0.to_side(0), gate_0.to_side(1), to_other(give_1), to_other(give_2)
        )
        down_1.along_rest(line)
        line.mark(down_2.own(line.next(side_0), side_1))
        line.mark(gate_1.side(line.next(core_1)))
        up_0 = mid_part(d_ups, 0)
        line.mark(up_0.give())
        kept_1, kept_2 = mid_back_of(d_gates[:2], d_ups[:2], F32)
        gate_0_side_0, gate_0_side_1, taken_1, taken_2 = line.land(
            gate_0_side_0, gate_0_side_1, taken_1, taken_2, sums=[down_1]
        )

        gate_1_side_0, core_0 = line.send(gate_1.to_side(0), up_0.to_core())
        down_2.along_rest(line)
        d_middle, d_branch_1, d_branch_2, grad_c, grad_b = norms_back(
            line,
            [(kept_1, taken_1), (kept_2, taken_2)],
            middle,
            gain_c,
            cotangent,
            branch_attn,
            gain_b,
            scalars,
        )
        (core_0,) = line.land(core_0)
        line.mark(up_0.side(line.next(core_0)))
        (gate_1_side_0,) = line.land(gate_1_side_0)

        gate_1_side_1, d_branch_3, down_1_side = line.send(
            gate_1.to_side(1), to_other(d_branch_1), down_1.to_side_last()
        )
        line.mark(gate_0.own(line.next(gate_0_side_0), gate_0_side_1))
        up_1 = mid_part(d_ups, 1)
        line.mark(up_1.give())
        d_branch_own_t = line.mark(turned([line.next(d_branch_1), d_branch_2], scalars))
        gate_1_side_1, d_branch_3, down_1_side = line.land(
            gate_1_side_1, d_branch_3, down_1_side, sums=[down_2]
        )
        down_1.add_side(down_1_side)

        up_0_side_0, core_1, d_branch_4 = line.send(
            up_0.to_side(0), up_1.to_core(), to_other(d_branch_2)
        )
        gate_0.along_rest(line)
        line.mark(gate_1.own(line.next(gate_1_side_0), gate_1_side_1))
        (core_1,) = line.land(core_1)
        line.mark(up_1.side(line.next(core_1)))
        up_0_side_0, d_branch_4 = line.land(up_0_side_0, d_branch_4)

        (up_0_side_1,) = line.send(up_0.to_side(1))
        gate_1.along_rest(line)
        d_attended = line.mark(
            projected(
                [line.next(d_branch_1), d_branch_2, d_branch_3, d_branch_4],
                full_first,
                qkv_cols,
                query_cols,
                scalars,
            )
        )
        d_branch_other_t = line.mark(turned([line.next(d_branch_3), d_branch_4], scalars))
        d_query, d_pair = line.mark(
            attend_back(qkv, line.next(d_attended), heads, group, SEQ_LEN, scalars)
        )
        (up_0_side_1,) = line.land(
            up_0_side_1, sums=[gate_0]
        )

        (up_1_side_0,) = line.send(up_1.to_side(0))
        line.mark(up_0.own(line.next(up_0_side_0), up_0_side_1))
        output = Grad(
            dp,
            1,
            [d_branch_own_t, line.next(d_branch_other_t)],
            [(attended, half, mine), (attended, half, theirs)],
            0,
            query_cols,
            scalars,
        )
        line.mark(output.give())

        def input_part(array, width):
            rights = [(line.next(array), half, mine), (array, half, theirs)]
            return Grad(dp, 1, [input_own_t, input_other_t], rights, 0, width, scalars)

        query = input_part(d_query, query_cols)
        line.mark(query.give())
        pair = input_part(d_pair, 2 * key_cols)
        line.mark(pair.give())
        (up_1_side_0,) = line.land(up_1_side_0)

        up_1_side_1, core, query_core, pair_core = line.send(
            up_1.to_side(1), output.to_core(), query.to_core(), pair.to_core()
        )
        up_0.along_rest(line)
        give_1, give_2 = line.mark(
            projected_back(
                [(line.next(d_query), 0), (d_pair, 1)], full_first, theirs, 2, BF16, scalars
            )
        )
        core, query_core, pair_core = line.land(core, query_core, pair_core)
        line.mark(output.side(line.next(core)))
        line.mark(query.side(line.next(query_core)))
        line.mark(pair.side(line.next(pair_core)))
        (up_1_side_1,) = line.land(up_1_side_1, sums=[gate_1])

        output_side, taken_1 = line.send(output.to_side(0), to_other(give_1))
        line.mark(up_1.own(line.next(up_1_side_0), up_1_side_1))
        kept_1, kept_2 = line.mark(
            projected_back(
                [(line.next(d_query), 0), (d_pair, 1)], full_first, mine, 2, F32, scalars
            )
        )
        output_side, taken_1 = line.land(output_side, taken_1)

        query_side, taken_2 = line.send(query.to_side(0), to_other(give_2))
        up_1.along_rest(line)
        line.mark(output.own(line.next(output_side)))
        query_side, taken_2 = line.land(query_side, taken_2, sums=[up_0])
        line.mark(query.own(line.next(query_side)))

        pair_side, *query_parts = line.send(pair.to_side(0), *query.to_owner())
        input_grad, grad_a = norms_back(
            line,
            [(kept_1, taken_1), (kept_2, taken_2)],
            layer_input,
            gain_a,
            d_middle,
            None,
            None,
            scalars,
        )
        (pair_side,) = line.land(pair_side)
        line.mark(pair.own(line.next(pair_side)))
        query_parts = line.land(*query_parts, sums=[up_1])
        gain_grads = jnp.stack([grad_a[0], grad_b[0], grad_c[0], grad_d])
        *pair_parts, gain_parts = line.send(*pair.to_owner(), (gain_grads, to_owners))
        output.along_rest(line)
        pair_parts = line.land(*pair_parts)
        (gain_parts,) = line.land(gain_parts)
        small = jnp.sum(gain_parts, axis=0)
        query.gather(query_parts)
        pair.gather(pair_parts)

        down, gate, up = [down_0, down_1, down_2], [gate_0, gate_1], [up_0, up_1]
        grad_pair = pair.result().reshape(-1, key_cols // HEAD_WIDTH, 2, HEAD_WIDTH)
        grad_down = jnp.concatenate([part.result() for part in down], axis=1).T
        return (
            layer_output,
            input_grad,
            query.result(),
            grad_pair[:, :, 0].reshape(-1, key_cols),
            grad_pair[:, :, 1].reshape(-1, key_cols),
            output.result().T,
            jnp.concatenate([part.result() for part in gate], axis=1),
            jnp.concatenate([part.result() for part in up], axis=1),
            grad_down,
            small[0],
            small[1],
            small[2],
            small[3],
        )

    return body


def solution(mesh):
    rows = P(("dp", "tensor"), None)
    gain = P(("dp", "tensor"))
    into, out_of = P("dp", "tensor"), P("tensor", "dp")
    return jax.shard_map(
        make_body(mesh.shape["dp"]),
        mesh=mesh,
        in_specs=(rows, into, into, into, out_of, into, into, out_of, gain, gain, gain, gain, rows),
        out_specs=(rows, rows, into, into, into, out_of, into, into, out_of, gain, gain, gain, gain),
        check_vma=False,
    )
```

```python
import jax
import jax.numpy as jnp
from jax import lax
from jax.experimental import pallas as pl
from jax.experimental.pallas import tpu as pltpu
from jax.sharding import PartitionSpec as P

QUERY_HEADS = 8
KEY_VALUE_HEADS = 4
HEAD_WIDTH = 256
SEQ_LEN = 1024

EPSILON = 1e-06
LOGIT_CAP = 50.0

BF16 = jnp.bfloat16
F32 = jnp.float32
VMEM_BYTES = 56 * 1024 * 1024


def rms_norm(values, gain):
    return values * lax.rsqrt(jnp.mean(values * values, axis=-1, keepdims=True) + EPSILON) * gain


def swap(rows):
    return lax.ppermute(rows, "tensor", [(0, 1), (1, 0)])


def flip(array, bit, dp):
    return lax.ppermute(array, "dp", [(i, i ^ (1 << bit)) for i in range(dp)])


def gather_small(piece, dp):
    other = swap(piece)
    whole = jnp.where(
        lax.axis_index("tensor") == 0,
        jnp.concatenate([piece, other], axis=1),
        jnp.concatenate([other, piece], axis=1),
    )
    bit = 0
    while (1 << bit) < dp:
        other = flip(whole, bit, dp)
        high = (lax.axis_index("dp") >> bit) & 1
        whole = jnp.where(
            high == 0,
            jnp.concatenate([whole, other], axis=1),
            jnp.concatenate([other, whole], axis=1),
        )
        bit += 1
    return whole


def dot(left, right):
    return lax.dot_general(left, right, (((1,), (0,)), ((), ())), preferred_element_type=F32)


def dot_nt(left, right):
    return lax.dot_general(left, right, (((1,), (1,)), ((), ())), preferred_element_type=F32)


def call(kernel, steps, scalars, inputs, outputs, scratch=()):
    in_specs = [
        pl.BlockSpec(block, index, pipeline_mode=pl.Buffered(1) if whole else None)
        for _, block, index, whole in inputs
    ]
    out_specs = [pl.BlockSpec(block, index) for _, _, block, index in outputs]
    shapes = [jax.ShapeDtypeStruct(shape, dtype) for shape, dtype, _, _ in outputs]
    return pl.pallas_call(
        kernel,
        grid_spec=pltpu.PrefetchScalarGridSpec(
            num_scalar_prefetch=1,
            grid=(steps,),
            in_specs=in_specs,
            out_specs=out_specs,
            scratch_shapes=list(scratch),
        ),
        out_shape=shapes,
        compiler_params=pltpu.CompilerParams(vmem_limit_bytes=VMEM_BYTES),
        cost_estimate=pl.CostEstimate(flops=1, bytes_accessed=1, transcendentals=0),
    )(jnp.stack(scalars).astype(jnp.int32), *(array for array, *_ in inputs))


def tile_of(extent, most=512):
    tile = most
    while extent % tile:
        tile //= 2
    return tile


def turned(pieces, scalars):
    rows = [piece.shape[0] for piece in pieces]
    width = pieces[0].shape[1]
    tile = tile_of(width, 768)

    def kernel(_, *refs):
        *ins, out = refs
        row = lax.broadcasted_iota(jnp.int32, (tile, tile), 0)
        column = lax.broadcasted_iota(jnp.int32, (tile, tile), 1)
        same = (row == column).astype(F32).astype(BF16)
        at = 0
        for ref, count in zip(ins, rows):
            out[:, at : at + count] = dot_nt(same, ref[...]).astype(BF16)
            at += count

    (out,) = call(
        kernel,
        width // tile,
        scalars,
        [(piece, (count, tile), lambda j, s: (0, j), False) for piece, count in zip(pieces, rows)],
        [((width, sum(rows)), BF16, (tile, sum(rows)), lambda j, s: (j, 0))],
    )
    return out


def feed(mid, full_first, gate_at, full_up, scalars):
    rows, width = mid.shape
    columns = full_up.shape[1]
    tile = tile_of(columns)

    def kernel(_, mid_ref, gate_ref, up_ref, hidden_ref, active_ref, slope_ref):
        gate = dot(mid_ref[...], gate_ref[...])
        up = dot(mid_ref[...], up_ref[...])
        inner = 0.7978845608028654 * (gate + 0.044715 * gate * gate * gate)
        bent = jnp.tanh(inner)
        half = 0.5 * (1.0 + bent)
        active = gate * half
        slope = half + gate * (0.5 * (1.0 - bent * bent)) * (
            0.7978845608028654 * (1.0 + 3 * 0.044715 * gate * gate)
        )
        hidden_ref[...] = (active * up).astype(BF16)
        active_ref[...] = active.astype(BF16)
        slope_ref[...] = (slope * up).astype(BF16)

    out = ((rows, columns), BF16, (rows, tile), lambda j, s: (0, j))
    first = gate_at // tile
    return call(
        kernel,
        columns // tile,
        scalars,
        [
            (mid, (rows, width), lambda j, s: (0, 0), True),
            (full_first, (width, tile), lambda j, s: (0, first + j), False),
            (full_up, (width, tile), lambda j, s: (0, j), False),
        ],
        [out] * 3,
    )


def feed_out(hidden, block, size, full_down_t, dtype, scalars):
    inner = hidden.shape[1]
    width = full_down_t.shape[0]
    tile = tile_of(width, 256)

    def kernel(_, hidden_ref, down_ref, out):
        out[...] = dot_nt(hidden_ref[...], down_ref[...]).astype(dtype)

    (out,) = call(
        kernel,
        width // tile,
        scalars,
        [
            (hidden, (size, inner), lambda j, s: (block, 0), True),
            (full_down_t, (tile, inner), lambda j, s: (j, 0), False),
        ],
        [((size, width), dtype, (size, tile), lambda j, s: (0, j))],
    )
    return out


def hidden_back(line, pieces, full_down_t, scalars):
    width, columns = full_down_t.shape
    tile = tile_of(columns)
    count = len(pieces)
    sizes = [piece[0].shape[0] for piece in pieces]

    def kernel(_, *refs):
        down = refs[3 * count][...]
        for index in range(count):
            rows_ref, active_ref, slope_ref = refs[index::count][:3]
            gate_ref, up_ref = refs[3 * count + 1 + index :: count][:2]
            d_hidden = dot(rows_ref[...], down)
            gate_ref[...] = (d_hidden * slope_ref[...].astype(F32)).astype(BF16)
            up_ref[...] = (d_hidden * active_ref[...].astype(F32)).astype(BF16)

    rows = [line.next(piece[0]) if index == 0 else piece[0] for index, piece in enumerate(pieces)]
    place = lambda j, s: (0, j)
    factors = [
        (piece[factor], (size, tile), lambda j, s, block=piece[3]: (block, j), False)
        for factor in (1, 2)
        for piece, size in zip(pieces, sizes)
    ]
    outs = line.mark(
        call(
            kernel,
            columns // tile,
            scalars,
            [(array, array.shape, lambda j, s: (0, 0), True) for array in rows]
            + factors
            + [(full_down_t, (width, tile), lambda j, s: (0, j), False)],
            [((size, columns), BF16, (size, tile), place) for size in sizes] * 2,
        )
    )
    return outs[:count], outs[count:]


def mid_back(d_gate, d_up, full_first, gate_at, full_up, dtype, scalars):
    inner = d_gate[0].shape[1]
    width = full_up.shape[0]
    tile = tile_of(width, 256)
    part = 1536
    parts = inner // part
    count = len(d_gate)

    def kernel(_, *refs):
        gates, ups, refs = refs[:count], refs[count : 2 * count], refs[2 * count :]
        for gate_ref, up_ref, out in zip(gates, ups, refs[parts + 1 :]):
            total = dot_nt(up_ref[...], refs[parts][...])
            for index in range(parts):
                here = slice(index * part, (index + 1) * part)
                total += dot_nt(gate_ref[:, here], refs[index][...])
            out[...] = total.astype(dtype)

    return call(
        kernel,
        width // tile,
        scalars,
        [(piece, piece.shape, lambda j, s: (0, 0), True) for piece in [*d_gate, *d_up]]
        + [
            (full_first, (tile, part), lambda j, s, index=index: (j, gate_at // part + index), False)
            for index in range(parts)
        ]
        + [(full_up, (tile, inner), lambda j, s: (j, 0), False)],
        [
            ((piece.shape[0], width), dtype, (piece.shape[0], tile), lambda j, s: (0, j))
            for piece in d_gate
        ],
    )


def dot_tn(left, right):
    return lax.dot_general(left, right, (((0,), (0,)), ((), ())), preferred_element_type=F32)


def soft(query, keys, start):
    scores = dot_nt(query, keys)
    tangent = jnp.tanh(scores * (HEAD_WIDTH**-0.5 / LOGIT_CAP))
    row = lax.broadcasted_iota(jnp.int32, scores.shape, 0) + start
    column = lax.broadcasted_iota(jnp.int32, scores.shape, 1)
    capped = jnp.where(column <= row, LOGIT_CAP * tangent, -jnp.inf)
    terms = jnp.exp(capped - jnp.max(capped, axis=1, keepdims=True))
    return terms / jnp.sum(terms, axis=1, keepdims=True), tangent


def attend(qkv, heads, group, length, scalars, block=256):
    total = qkv.shape[0]
    block = min(block, length)
    seqs = total // length

    def kernel(_, query_ref, key_ref, value_ref, out_ref):
        for start in range(0, length, block):
            end = start + block
            weights, _ = soft(query_ref[start:end, :], key_ref[:end, :], start)
            out_ref[start:end, :] = dot(weights.astype(BF16), value_ref[:end, :]).astype(BF16)

    shape = (length, HEAD_WIDTH)
    (out,) = call(
        kernel,
        seqs * heads,
        scalars,
        [
            (qkv, shape, lambda j, s: (j // heads, j % heads), False),
            (qkv, shape, lambda j, s: (j // heads, heads + 2 * (j % heads // group)), False),
            (qkv, shape, lambda j, s: (j // heads, heads + 2 * (j % heads // group) + 1), False),
        ],
        [((total, heads * HEAD_WIDTH), BF16, shape, lambda j, s: (j // heads, j % heads))],
    )
    return out


def attend_back(qkv, d_attended, heads, group, length, scalars, block=256):
    total = qkv.shape[0]
    block = min(block, length)
    seqs = total // length
    key_heads = heads // group
    scale = HEAD_WIDTH**-0.5

    def kernel(_, query_ref, pair_ref, d_ref, d_query_ref, d_pair_ref, d_key, d_value):
        d_key[...] = jnp.zeros_like(d_key)
        d_value[...] = jnp.zeros_like(d_value)
        for member in range(group):
            columns = slice(member * HEAD_WIDTH, (member + 1) * HEAD_WIDTH)
            for start in range(0, length, block):
                end = start + block
                query = query_ref[start:end, columns]
                d_rows = d_ref[start:end, columns]
                keys, values = pair_ref[:end, :HEAD_WIDTH], pair_ref[:end, HEAD_WIDTH:]
                weights, tangent = soft(query, keys, start)
                d_soft = dot_nt(d_rows, values)
                d_capped = weights * (
                    d_soft - jnp.sum(weights * d_soft, axis=1, keepdims=True)
                )
                d_scores = (d_capped * (1.0 - tangent * tangent)).astype(BF16)
                d_query_ref[start:end, columns] = (dot(d_scores, keys) * scale).astype(BF16)
                d_key[:end, :] += dot_tn(d_scores, query)
                d_value[:end, :] += dot_tn(weights.astype(BF16), d_rows)
        d_pair_ref[:, :HEAD_WIDTH] = (d_key[...] * scale).astype(BF16)
        d_pair_ref[:, HEAD_WIDTH:] = d_value[...].astype(BF16)

    wide, pair = (length, group * HEAD_WIDTH), (length, 2 * HEAD_WIDTH)
    first_pair = heads // 2
    place = lambda j, s: (j // key_heads, j % key_heads)
    return call(
        kernel,
        seqs * key_heads,
        scalars,
        [
            (qkv, wide, place, False),
            (qkv, pair, lambda j, s: (j // key_heads, first_pair + j % key_heads), False),
            (d_attended, wide, place, False),
        ],
        [
            ((total, heads * HEAD_WIDTH), BF16, wide, place),
            ((total, key_heads * 2 * HEAD_WIDTH), BF16, pair, place),
        ],
        scratch=[pltpu.VMEM((length, HEAD_WIDTH), F32)] * 2,
    )


class Grad:
    def __init__(self, dp, chunks, lefts, rights, first_column, columns, scalars):
        self.dp, self.chunks, self.scalars = dp, chunks, scalars
        width = lefts[0].shape[0]
        self.rest, self.rows = dp // 4, width // dp
        self.lefts = [left.reshape(self.rest, 2, 2, self.rows, left.shape[1]) for left in lefts]
        self.rights = rights
        self.columns, self.tile = columns, tile_of(columns)
        self.first = first_column // self.tile
        self.count = len(lefts) + len(rights)

    def inputs(self, block, place):
        return [
            (
                left,
                (self.rest, block, None, *left.shape[3:]),
                lambda j, s: (0, *place(s), 0, 0),
                True,
            )
            for left in self.lefts
        ] + [
            (array, (size, self.tile), lambda j, s, row=row: (row(s), self.first + j), False)
            for array, size, row in self.rights
        ]

    def product(self, refs):
        return sum_of_products(refs[: len(self.lefts)], refs[len(self.lefts) : self.count])

    def run(self, kernel, inputs, outputs):
        return call(kernel, self.columns // self.tile, self.scalars, inputs, outputs)

    def give(self):
        def kernel(_, *refs):
            refs[-1][...] = self.product(refs).astype(BF16)

        shape = (self.rest, 2, self.rows)
        (self.given,) = self.run(
            kernel,
            self.inputs(2, lambda s: (0, 1 - s[0])),
            [((*shape, self.columns), BF16, (*shape, self.tile), lambda j, s: (0, 0, 0, j))],
        )
        return self.given

    def to_core(self):
        return self.given, lambda array: flip(array, 0, self.dp)

    def side(self, from_core):
        self.from_core = from_core
        size = self.rest // self.chunks

        def kernel(_, *refs):
            core = refs[self.count]
            result = (self.product(refs) + core[...].astype(F32)).astype(BF16)
            for index, out in enumerate(refs[self.count + 1 :]):
                out[...] = result[index * size : (index + 1) * size]

        self.give_side = self.run(
            kernel,
            self.inputs(None, lambda s: (1 - s[1], s[0]))
            + [
                (
                    from_core,
                    (self.rest, None, self.rows, self.tile),
                    lambda j, s: (0, 1 - s[1], 0, j),
                    False,
                )
            ],
            [
                (
                    (size, self.rows, self.columns),
                    BF16,
                    (size, self.rows, self.tile),
                    lambda j, s: (0, 0, j),
                )
            ]
            * self.chunks,
        )
        return self.give_side[0]

    def both(self, from_core):
        def kernel(_, *refs):
            result = self.product(refs) + refs[self.count][...].astype(F32)
            refs[-1][...] = result.astype(BF16)

        shape = (self.rest, 2, self.rows)
        place = lambda j, s: (0, 0, 0, j)
        (self.total,) = self.run(
            kernel,
            self.inputs(2, lambda s: (0, s[0]))
            + [(from_core, (*shape, self.tile), place, False)],
            [((*shape, self.columns), BF16, (*shape, self.tile), place)],
        )
        return self.total

    def to_side_last(self):
        side = (lax.axis_index("dp") >> 1) & 1
        parts = self.sums.reshape(2, self.rows, self.columns)
        self.sums = pick(parts, side)
        return pick(parts, 1 - side), lambda array: flip(array, 1, self.dp)

    def add_side(self, part):
        self.sums = self.sums.astype(F32) + part.astype(F32)

    def to_side(self, chunk):
        return self.give_side[chunk], lambda array: flip(array, 1, self.dp)

    def own(self, *from_side):
        size = self.rest // self.chunks

        def kernel(_, *refs):
            core, sides, out = refs[self.count], refs[self.count + 1 : -1], refs[-1]
            result = self.product(refs) + core[...].astype(F32)
            for index, ref in enumerate(sides):
                here = slice(index * size, (index + 1) * size)
                out[here] = (result[here] + ref[...].astype(F32)).astype(BF16)

        place = lambda j, s: (0, 0, j)
        (self.total,) = self.run(
            kernel,
            self.inputs(None, lambda s: (s[1], s[0]))
            + [
                (
                    self.from_core,
                    (self.rest, None, self.rows, self.tile),
                    lambda j, s: (0, s[1], 0, j),
                    False,
                )
            ]
            + [(part, (size, self.rows, self.tile), place, False) for part in from_side],
            [
                (
                    (self.rest, self.rows, self.columns),
                    BF16,
                    (self.rest, self.rows, self.tile),
                    place,
                )
            ],
        )
        return self.total

    def along_rest(self, line):
        groups = [[low + 4 * high for high in range(self.rest)] for low in range(4)]
        self.sums = lax.psum_scatter(
            line.next(self.total).reshape(-1, self.columns),
            "dp",
            scatter_dimension=0,
            axis_index_groups=groups,
            tiled=True,
        )

    def to_owner(self):
        place = lax.axis_index("dp") >> 2
        transfers = []
        for shift in range(1, self.rest):
            pairs = [(i, (i + 4 * shift) % self.dp) for i in range(self.dp)]
            part = pick(self.total, (place + shift) % self.rest)
            transfers.append((part, lambda array, pairs=pairs: lax.ppermute(array, "dp", pairs)))
        return transfers

    def gather(self, parts):
        place = lax.axis_index("dp") >> 2
        total = pick(self.total, place).astype(F32)
        self.sums = sum((part.astype(F32) for part in parts), total)

    def result(self):
        return self.sums.astype(F32)


def pick(array, index):
    return lax.dynamic_index_in_dim(array, index, 0, keepdims=False)


def sum_of_products(lefts, rights):
    *lead, rows, _ = lefts[0].shape
    columns = rights[0].shape[1]
    count = 1
    for extent in lead:
        count *= extent
    rights = [right[...] for right in rights]
    pairs, index = [], 0
    for left in lefts:
        left, at = left[...], 0
        while at < left.shape[-1]:
            size = rights[index].shape[0]
            pairs.append((left[..., at : at + size], rights[index]))
            at += size
            index += 1

    def total(pick_block):
        result = None
        for left, right in pairs:
            term = dot(pick_block(left), right)
            result = term if result is None else result + term
        return result

    if rows % 16 == 0:
        blocks = total(lambda left: left.reshape(count * rows, left.shape[-1]))
    else:
        blocks = jnp.stack(
            [
                total(lambda left, block=block: left.reshape(count, rows, -1)[block])
                for block in range(count)
            ]
        )
    return blocks.reshape(*lead, rows, columns)


def tied(*arrays):
    return lax.optimization_barrier(arrays)


class Line:
    def __init__(self):
        self.last = None

    def next(self, array):
        if self.last is not None:
            array, _ = tied(array, self.last)
        return array

    def mark(self, array):
        self.last = array[0] if isinstance(array, (list, tuple)) else array
        return array

    def send(self, *transfers):
        return [send(self.next(array)) for array, send in transfers]

    def land(self, *flying, sums=()):
        count = len(flying)
        *taken, self.last = tied(*flying, *(grad.sums for grad in sums), self.last)
        for grad, value in zip(sums, taken[count:]):
            grad.sums = value
        return taken[:count]


def projected(pieces, weights, first_column, columns, scalars):
    count = len(pieces)
    half = sum(piece.shape[0] for piece in pieces) // 2
    width = pieces[0].shape[1]
    tile = tile_of(columns)

    def kernel(scalar_ref, *refs):
        *ins, weight_ref, out = refs
        weight = weight_ref[...]
        at = 0
        for ref in ins:
            owner = scalar_ref[2] if at < half else 1 - scalar_ref[2]
            size = ref.shape[0]
            start = pl.multiple_of(owner * half + at % half, size)
            out[pl.ds(start, size), :] = dot(ref[...], weight).astype(BF16)
            at += size

    (out,) = call(
        kernel,
        columns // tile,
        scalars,
        [(piece, piece.shape, lambda j, s: (0, 0), True) for piece in pieces]
        + [(weights, (width, tile), lambda j, s: (0, first_column // tile + j), False)],
        [((2 * half, columns), BF16, (2 * half, tile), lambda j, s: (0, j))],
    )
    return out


def projected_back(sources, weights, owner, pieces, dtype, scalars):
    half = sources[0][0].shape[0] // 2
    width = weights.shape[0]
    tile = tile_of(width, 256)
    size = half // pieces
    count = len(sources)

    def kernel(_, *refs):
        total = None
        for rows, weight in zip(refs[:count], refs[count : 2 * count]):
            term = dot_nt(rows[...], weight[...])
            total = term if total is None else total + term
        result = total.astype(dtype)
        for index, out in enumerate(refs[2 * count :]):
            out[...] = result[index * size : (index + 1) * size]

    return call(
        kernel,
        width // tile,
        scalars,
        [
            (array, (half, array.shape[1]), lambda j, s: (owner(s), 0), True)
            for array, _ in sources
        ]
        + [
            (weights, (tile, array.shape[1]), lambda j, s, block=block: (j, block), False)
            for array, block in sources
        ],
        [((size, width), dtype, (size, tile), lambda j, s: (0, j))] * pieces,
    )


def norms_back(line, sums, middle, gain_mid, upstream, branch, gain_branch, scalars):
    rows, width = middle.shape
    count = len(sums)
    size = sums[0][0].shape[0]
    block = 64
    steps, each = rows // block, size // block
    given = [(middle, gain_mid)] + ([] if branch is None else [(branch, gain_branch)])
    norms = len(given)
    outs = 1 if branch is None else 1 + count

    def back(values, gain, d_normed):
        values = values.astype(F32)
        scale = lax.rsqrt(jnp.mean(values * values, axis=1, keepdims=True) + EPSILON)
        normed = values * scale
        weighted = d_normed * gain
        inner = jnp.mean(weighted * normed, axis=1, keepdims=True)
        grad = scale * (weighted - normed * inner)
        return grad, jnp.sum(d_normed * normed, axis=0, keepdims=True)

    def kernel(_, *refs):
        parts, upstream_ref, refs = refs[: 2 * count], refs[2 * count], refs[2 * count + 1 :]
        values_refs, gain_refs, refs = refs[:norms], refs[norms : 2 * norms], refs[2 * norms :]
        grad_refs, gain_grad_refs = refs[:outs], refs[outs:]
        step = pl.program_id(0)

        @pl.when(step == 0)
        def _():
            for ref in gain_grad_refs:
                ref[...] = jnp.zeros_like(ref)

        for index in range(count):

            @pl.when(step // each == index)
            def _(index=index):
                d_normed = parts[2 * index][...] + parts[2 * index + 1][...].astype(F32)
                grad, grad_gain = back(values_refs[0][...], gain_refs[0][...], d_normed)
                gain_grad_refs[0][...] += grad_gain
                total = upstream_ref[...].astype(F32) + grad
                grad_refs[0][...] = total
                if norms > 1:
                    grad, grad_gain = back(values_refs[1][...], gain_refs[1][...], total)
                    gain_grad_refs[1][...] += grad_gain
                    grad_refs[1 + index][...] = grad.astype(BF16)

    def piece(index):
        return lambda j, s: (jnp.clip(j - index * each, 0, each - 1), 0)

    shape = (block, width)
    every = lambda j, s: (j, 0)
    once = lambda j, s: (0, 0)
    (first, *others), *later = sums
    sums = [(line.next(first), *others), *later]
    return line.mark(
        call(
            kernel,
            steps,
            scalars,
            [
                (array, shape, piece(index), False)
                for index, pair in enumerate(sums)
                for array in pair
            ]
            + [(array, shape, every, False) for array in (upstream, *(v for v, _ in given))]
            + [(gain[None], (1, width), once, True) for _, gain in given],
            [((rows, width), F32, shape, every)]
            + [((size, width), BF16, shape, piece(index)) for index in range(outs - 1)]
            + [((1, width), F32, (1, width), once)] * norms,
        )
    )


def joined(weights):
    rows = weights[0].shape[0]
    width = sum(weight.shape[1] for weight in weights)

    def kernel(query_ref, key_ref, value_ref, output_ref, gate_ref, out_ref):
        parts = [query_ref[...]]
        for head in range(key_ref.shape[1] // HEAD_WIDTH):
            here = slice(head * HEAD_WIDTH, (head + 1) * HEAD_WIDTH)
            parts += [key_ref[:, here], value_ref[:, here]]
        at = 0
        for part in [*parts, output_ref[...], gate_ref[...]]:
            out_ref[:, at : at + part.shape[1]] = part
            at += part.shape[1]

    return pl.pallas_call(
        kernel,
        out_shape=jax.ShapeDtypeStruct((rows, width), BF16),
        in_specs=[pl.BlockSpec(memory_space=pltpu.VMEM)] * 5,
        out_specs=pl.BlockSpec(memory_space=pltpu.VMEM),
        compiler_params=pltpu.CompilerParams(vmem_limit_bytes=VMEM_BYTES),
    )(*weights)


def owner_parts(partial):
    count, width = partial.shape
    devices = lax.axis_size("dp") * lax.axis_size("tensor")
    return partial.reshape(count, devices, width // devices).transpose(1, 0, 2)


def to_owners(parts):
    return lax.all_to_all(parts, ("dp", "tensor"), 0, 0, tiled=True)


def make_body(dp):
    def body(
        layer_input,
        query_weight,
        key_weight,
        value_weight,
        w_output,
        w_gate,
        w_up,
        w_down,
        gain_attn_in,
        gain_attn_out,
        gain_ffn_in,
        gain_ffn_out,
        cotangent,
    ):
        line = Line()
        place, turn = lax.axis_index("dp"), lax.axis_index("tensor")
        scalars = [place & 1, (place >> 1) & 1, turn]
        to_other = lambda array: (array, swap)
        mine, theirs = (lambda s: s[2]), (lambda s: 1 - s[2])
        query_cols, key_cols = query_weight.shape[1], key_weight.shape[1]
        qkv_cols = query_cols + 2 * key_cols
        gate_at = qkv_cols + query_cols
        columns = w_gate.shape[1]
        half = layer_input.shape[0]
        quarter = half // 2
        heads = query_cols // HEAD_WIDTH
        group = QUERY_HEADS // KEY_VALUE_HEADS
        full_first = lax.all_gather(
            joined([query_weight, key_weight, value_weight, w_output.T, w_gate]),
            "dp",
            axis=0,
            tiled=True,
        )
        full_up = lax.all_gather(w_up, "dp", axis=0, tiled=True)
        full_down_t = lax.all_gather(w_down.T, "dp", axis=0, tiled=True)
        gains = gather_small(
            jnp.stack([gain_attn_in, gain_attn_out, gain_ffn_in, gain_ffn_out]), dp
        )
        gain_a, gain_b, gain_c, gain_d = gains[0], gains[1], gains[2], gains[3]

        residual_in = layer_input.astype(F32)
        upstream = cotangent.astype(F32)
        input_own = line.mark(rms_norm(residual_in, gain_a).astype(BF16))
        input_other = swap(input_own)
        input_own_t = line.mark(turned([input_own], scalars))
        (input_other,) = line.land(input_other)
        input_other_t = line.mark(turned([input_other], scalars))
        qkv = line.mark(
            projected([input_own, line.next(input_other)], full_first, 0, qkv_cols, scalars)
        )
        attended = line.mark(attend(qkv, heads, group, SEQ_LEN, scalars))
        output_block = qkv_cols // query_cols
        (give,) = line.mark(
            projected_back([(attended, output_block)], full_first, theirs, 1, BF16, scalars)
        )
        (taken,) = line.send(to_other(give))
        (kept,) = line.mark(
            projected_back(
                [(line.next(attended), output_block)], full_first, mine, 1, F32, scalars
            )
        )
        branch_attn = kept + taken.astype(F32)
        middle = residual_in + rms_norm(branch_attn, gain_b)
        mid_own = line.mark(rms_norm(middle, gain_c).astype(BF16))
        (mid_other,) = line.send(to_other(mid_own))
        hidden_own, active_own, slope_own = line.mark(
            feed(mid_own, full_first, gate_at, full_up, scalars)
        )
        mid_own_t = line.mark(turned([line.next(mid_own)], scalars))
        (mid_other,) = line.land(mid_other)
        hidden_other, active_other, slope_other = line.mark(
            feed(line.next(mid_other), full_first, gate_at, full_up, scalars)
        )
        mid_other_t = line.mark(turned([line.next(mid_other)], scalars))

        def ffn_back(kept, taken, middle, upstream):
            branch = kept + taken.astype(F32)
            ffn_out, pull = jax.vjp(rms_norm, branch, gain_d)
            d_ffn, grad_gain = pull(upstream)
            return (middle + ffn_out).astype(BF16), line.mark(d_ffn.astype(BF16)), grad_gain

        low, high = slice(0, quarter), slice(quarter, half)
        give_1 = line.mark(
            feed_out(line.next(hidden_other), 0, quarter, full_down_t, BF16, scalars)
        )
        (taken_1,) = line.send(to_other(give_1))
        give_2 = line.mark(
            feed_out(line.next(hidden_other), 1, quarter, full_down_t, BF16, scalars)
        )
        (taken_1,) = line.land(taken_1)
        (taken_2,) = line.send(to_other(give_2))
        kept = line.mark(feed_out(line.next(hidden_own), 0, half, full_down_t, F32, scalars))
        output_1, d_ffn_1, grad_d_1 = ffn_back(
            line.next(kept)[low], taken_1, middle[low], upstream[low]
        )
        (taken_2,) = line.land(taken_2)
        (d_ffn_3,) = line.send(to_other(d_ffn_1))
        output_2, d_ffn_2, grad_d_2 = ffn_back(
            line.next(kept)[high], taken_2, middle[high], upstream[high]
        )
        d_ffn_own_t = line.mark(turned([line.next(d_ffn_1), d_ffn_2], scalars))
        (d_gate_1,), (d_up_1,) = hidden_back(
            line, [(d_ffn_1, active_own, slope_own, 0)], full_down_t, scalars
        )
        (d_ffn_3,) = line.land(d_ffn_3)
        (d_ffn_4,) = line.send(to_other(d_ffn_2))
        layer_output = jnp.concatenate([output_1, output_2], axis=0)
        grad_d = grad_d_1 + grad_d_2
        (d_gate_2, d_gate_3), (d_up_2, d_up_3) = hidden_back(
            line,
            [(d_ffn_2, active_own, slope_own, 1), (d_ffn_3, active_other, slope_other, 0)],
            full_down_t,
            scalars,
        )
        (d_ffn_4,) = line.land(d_ffn_4)
        d_ffn_other_t = line.mark(turned([line.next(d_ffn_3), d_ffn_4], scalars))

        first = lambda s: 0
        tile = tile_of(columns)
        tiles = columns // tile
        cuts = [0, 2 * tile, 4 * tile, columns]
        split = tile * -(-tiles // 2)
        halves = [(0, split), (split, columns - split)]
        hidden_rights = [(hidden_own, half, first), (hidden_other, half, first)]
        mid_lefts = [mid_own_t, mid_other_t]

        def down_part(part, chunks):
            lefts = [line.next(d_ffn_own_t), d_ffn_other_t]
            start, end = cuts[part], cuts[part + 1]
            return Grad(dp, chunks, lefts, hidden_rights, start, end - start, scalars)

        def mid_part(pieces, part):
            rights = [(line.next(piece), quarter, first) for piece in pieces]
            return Grad(dp, 2, mid_lefts, rights, *halves[part], scalars)

        def mid_back_of(gates, ups, dtype):
            gates = [line.next(gates[0]), *gates[1:]]
            return line.mark(mid_back(gates, ups, full_first, gate_at, full_up, dtype, scalars))

        down_0 = down_part(0, 1)
        line.mark(down_0.give())
        (core_0,) = line.send(down_0.to_core())
        down_2 = down_part(2, 2)
        line.mark(down_2.give())
        (core_0,) = line.land(core_0)
        line.mark(down_0.side(line.next(core_0)))

        down_0_side, core_2 = line.send(down_0.to_side(0), down_2.to_core())
        down_1 = down_part(1, 1)
        line.mark(down_1.give())
        (d_gate_4,), (d_up_4,) = hidden_back(
            line, [(d_ffn_4, active_other, slope_other, 1)], full_down_t, scalars
        )
        d_gates = [d_gate_1, d_gate_2, d_gate_3, d_gate_4]
        d_ups = [d_up_1, d_up_2, d_up_3, d_up_4]
        (core_2,) = line.land(core_2)
        line.mark(down_2.side(line.next(core_2)))
        (down_0_side,) = line.land(down_0_side)

        side_0, core_1 = line.send(down_2.to_side(0), down_1.to_core())
        line.mark(down_0.own(line.next(down_0_side)))
        gate_0 = mid_part(d_gates, 0)
        line.mark(gate_0.give())
        (core_1,) = line.land(core_1)
        line.mark(down_1.both(line.next(core_1)))
        gate_1 = mid_part(d_gates, 1)
        line.mark(gate_1.give())
        (side_0,) = line.land(side_0)

        side_1, core_0, core_1 = line.send(
            down_2.to_side(1), gate_0.to_core(), gate_1.to_core()
        )
        down_0.along_rest(line)
        give_1, give_2 = mid_back_of(d_gates[2:], d_ups[2:], BF16)
        core_0, core_1 = line.land(core_0, core_1)
        line.mark(gate_0.side(line.next(core_0)))
        (side_1,) = line.land(
            side_1, sums=[down_0]
        )

        gate_0_side_0, gate_0_side_1, taken_1, taken_2 = line.send(
            gate_0.to_side(0), gate_0.to_side(1), to_other(give_1), to_other(give_2)
        )
        down_1.along_rest(line)
        line.mark(down_2.own(line.next(side_0), side_1))
        line.mark(gate_1.side(line.next(core_1)))
        up_0 = mid_part(d_ups, 0)
        line.mark(up_0.give())
        kept_1, kept_2 = mid_back_of(d_gates[:2], d_ups[:2], F32)
        gate_0_side_0, gate_0_side_1, taken_1, taken_2 = line.land(
            gate_0_side_0, gate_0_side_1, taken_1, taken_2, sums=[down_1]
        )

        gate_1_side_0, core_0 = line.send(gate_1.to_side(0), up_0.to_core())
        down_2.along_rest(line)
        d_middle, d_branch_1, d_branch_2, grad_c, grad_b = norms_back(
            line,
            [(kept_1, taken_1), (kept_2, taken_2)],
            middle,
            gain_c,
            cotangent,
            branch_attn,
            gain_b,
            scalars,
        )
        (core_0,) = line.land(core_0)
        line.mark(up_0.side(line.next(core_0)))
        (gate_1_side_0,) = line.land(gate_1_side_0)

        gate_1_side_1, d_branch_3, down_1_side = line.send(
            gate_1.to_side(1), to_other(d_branch_1), down_1.to_side_last()
        )
        line.mark(gate_0.own(line.next(gate_0_side_0), gate_0_side_1))
        up_1 = mid_part(d_ups, 1)
        line.mark(up_1.give())
        d_branch_own_t = line.mark(turned([line.next(d_branch_1), d_branch_2], scalars))
        gate_1_side_1, d_branch_3, down_1_side = line.land(
            gate_1_side_1, d_branch_3, down_1_side, sums=[down_2]
        )
        down_1.add_side(down_1_side)

        up_0_side_0, core_1, d_branch_4 = line.send(
            up_0.to_side(0), up_1.to_core(), to_other(d_branch_2)
        )
        gate_0.along_rest(line)
        line.mark(gate_1.own(line.next(gate_1_side_0), gate_1_side_1))
        (core_1,) = line.land(core_1)
        line.mark(up_1.side(line.next(core_1)))
        up_0_side_0, d_branch_4 = line.land(up_0_side_0, d_branch_4)

        (up_0_side_1,) = line.send(up_0.to_side(1))
        gate_1.along_rest(line)
        d_attended = line.mark(
            projected(
                [line.next(d_branch_1), d_branch_2, d_branch_3, d_branch_4],
                full_first,
                qkv_cols,
                query_cols,
                scalars,
            )
        )
        d_branch_other_t = line.mark(turned([line.next(d_branch_3), d_branch_4], scalars))
        d_query, d_pair = line.mark(
            attend_back(qkv, line.next(d_attended), heads, group, SEQ_LEN, scalars)
        )
        (up_0_side_1,) = line.land(
            up_0_side_1, sums=[gate_0]
        )

        (up_1_side_0,) = line.send(up_1.to_side(0))
        line.mark(up_0.own(line.next(up_0_side_0), up_0_side_1))
        output = Grad(
            dp,
            1,
            [d_branch_own_t, line.next(d_branch_other_t)],
            [(attended, half, mine), (attended, half, theirs)],
            0,
            query_cols,
            scalars,
        )
        line.mark(output.give())

        def input_part(array, width):
            rights = [(line.next(array), half, mine), (array, half, theirs)]
            return Grad(dp, 1, [input_own_t, input_other_t], rights, 0, width, scalars)

        query = input_part(d_query, query_cols)
        line.mark(query.give())
        pair = input_part(d_pair, 2 * key_cols)
        line.mark(pair.give())
        (up_1_side_0,) = line.land(up_1_side_0)

        up_1_side_1, core, query_core, pair_core = line.send(
            up_1.to_side(1), output.to_core(), query.to_core(), pair.to_core()
        )
        up_0.along_rest(line)
        give_1, give_2 = line.mark(
            projected_back(
                [(line.next(d_query), 0), (d_pair, 1)], full_first, theirs, 2, BF16, scalars
            )
        )
        core, query_core, pair_core = line.land(core, query_core, pair_core)
        line.mark(output.side(line.next(core)))
        line.mark(query.side(line.next(query_core)))
        line.mark(pair.side(line.next(pair_core)))
        (up_1_side_1,) = line.land(up_1_side_1, sums=[gate_1])

        output_side, taken_1 = line.send(output.to_side(0), to_other(give_1))
        line.mark(up_1.own(line.next(up_1_side_0), up_1_side_1))
        kept_1, kept_2 = line.mark(
            projected_back(
                [(line.next(d_query), 0), (d_pair, 1)], full_first, mine, 2, F32, scalars
            )
        )
        output_side, taken_1 = line.land(output_side, taken_1)

        query_side, taken_2 = line.send(query.to_side(0), to_other(give_2))
        up_1.along_rest(line)
        line.mark(output.own(line.next(output_side)))
        query_side, taken_2 = line.land(query_side, taken_2, sums=[up_0])
        line.mark(query.own(line.next(query_side)))

        pair_side, *query_parts = line.send(pair.to_side(0), *query.to_owner())
        input_grad, grad_a = norms_back(
            line,
            [(kept_1, taken_1), (kept_2, taken_2)],
            layer_input,
            gain_a,
            d_middle,
            None,
            None,
            scalars,
        )
        gain_grads = jnp.stack([grad_a[0], grad_b[0], grad_c[0], grad_d])
        gain_grads = line.mark(owner_parts(gain_grads))
        (pair_side,) = line.land(pair_side)
        line.mark(pair.own(line.next(pair_side)))
        query_parts = line.land(*query_parts, sums=[up_1])
        *pair_parts, gain_parts = line.send(*pair.to_owner(), (gain_grads, to_owners))
        output.along_rest(line)
        pair_parts = line.land(*pair_parts)
        (gain_parts,) = line.land(gain_parts)
        small = jnp.sum(gain_parts, axis=0)
        query.gather(query_parts)
        pair.gather(pair_parts)

        down, gate, up = [down_0, down_1, down_2], [gate_0, gate_1], [up_0, up_1]
        grad_pair = pair.result().reshape(-1, key_cols // HEAD_WIDTH, 2, HEAD_WIDTH)
        grad_down = jnp.concatenate([part.result() for part in down], axis=1).T
        return (
            layer_output,
            input_grad,
            query.result(),
            grad_pair[:, :, 0].reshape(-1, key_cols),
            grad_pair[:, :, 1].reshape(-1, key_cols),
            output.result().T,
            jnp.concatenate([part.result() for part in gate], axis=1),
            jnp.concatenate([part.result() for part in up], axis=1),
            grad_down,
            small[0],
            small[1],
            small[2],
            small[3],
        )

    return body


def solution(mesh):
    rows = P(("dp", "tensor"), None)
    gain = P(("dp", "tensor"))
    into, out_of = P("dp", "tensor"), P("tensor", "dp")
    return jax.shard_map(
        make_body(mesh.shape["dp"]),
        mesh=mesh,
        in_specs=(rows, into, into, into, out_of, into, into, out_of, gain, gain, gain, gain, rows),
        out_specs=(rows, rows, into, into, into, out_of, into, into, out_of, gain, gain, gain, gain),
        check_vma=False,
    )
```

```python
import jax
import jax.numpy as jnp
from jax import lax
from jax.experimental import pallas as pl
from jax.experimental.pallas import tpu as pltpu
from jax.sharding import PartitionSpec as P

QUERY_HEADS = 8
KEY_VALUE_HEADS = 4
HEAD_WIDTH = 256
SEQ_LEN = 1024

EPSILON = 1e-06
LOGIT_CAP = 50.0

BF16 = jnp.bfloat16
F32 = jnp.float32
VMEM_BYTES = 56 * 1024 * 1024


def rms_norm(values, gain):
    return values * lax.rsqrt(jnp.mean(values * values, axis=-1, keepdims=True) + EPSILON) * gain


def swap(rows):
    return lax.ppermute(rows, "tensor", [(0, 1), (1, 0)])


def flip(array, bit, dp):
    return lax.ppermute(array, "dp", [(i, i ^ (1 << bit)) for i in range(dp)])


def gather_small(piece, dp):
    other = swap(piece)
    whole = jnp.where(
        lax.axis_index("tensor") == 0,
        jnp.concatenate([piece, other], axis=1),
        jnp.concatenate([other, piece], axis=1),
    )
    bit = 0
    while (1 << bit) < dp:
        other = flip(whole, bit, dp)
        high = (lax.axis_index("dp") >> bit) & 1
        whole = jnp.where(
            high == 0,
            jnp.concatenate([whole, other], axis=1),
            jnp.concatenate([other, whole], axis=1),
        )
        bit += 1
    return whole


def dot(left, right):
    return lax.dot_general(left, right, (((1,), (0,)), ((), ())), preferred_element_type=F32)


def dot_nt(left, right):
    return lax.dot_general(left, right, (((1,), (1,)), ((), ())), preferred_element_type=F32)


def call(kernel, steps, scalars, inputs, outputs, scratch=()):
    in_specs = [
        pl.BlockSpec(block, index, pipeline_mode=pl.Buffered(1) if whole else None)
        for _, block, index, whole in inputs
    ]
    out_specs = [pl.BlockSpec(block, index) for _, _, block, index in outputs]
    shapes = [jax.ShapeDtypeStruct(shape, dtype) for shape, dtype, _, _ in outputs]
    return pl.pallas_call(
        kernel,
        grid_spec=pltpu.PrefetchScalarGridSpec(
            num_scalar_prefetch=1,
            grid=(steps,),
            in_specs=in_specs,
            out_specs=out_specs,
            scratch_shapes=list(scratch),
        ),
        out_shape=shapes,
        compiler_params=pltpu.CompilerParams(vmem_limit_bytes=VMEM_BYTES),
        cost_estimate=pl.CostEstimate(flops=1, bytes_accessed=1, transcendentals=0),
    )(jnp.stack(scalars).astype(jnp.int32), *(array for array, *_ in inputs))


def tile_of(extent, most=512):
    tile = most
    while extent % tile:
        tile //= 2
    return tile


def turned(pieces, scalars):
    rows = [piece.shape[0] for piece in pieces]
    width = pieces[0].shape[1]
    tile = tile_of(width, 768)

    def kernel(_, *refs):
        *ins, out = refs
        row = lax.broadcasted_iota(jnp.int32, (tile, tile), 0)
        column = lax.broadcasted_iota(jnp.int32, (tile, tile), 1)
        same = (row == column).astype(F32).astype(BF16)
        at = 0
        for ref, count in zip(ins, rows):
            out[:, at : at + count] = dot_nt(same, ref[...]).astype(BF16)
            at += count

    (out,) = call(
        kernel,
        width // tile,
        scalars,
        [(piece, (count, tile), lambda j, s: (0, j), False) for piece, count in zip(pieces, rows)],
        [((width, sum(rows)), BF16, (tile, sum(rows)), lambda j, s: (j, 0))],
    )
    return out


def feed(mid, full_first, gate_at, full_up, scalars):
    rows, width = mid.shape
    columns = full_up.shape[1]
    tile = tile_of(columns)

    def kernel(_, mid_ref, gate_ref, up_ref, hidden_ref, active_ref, slope_ref):
        gate = dot(mid_ref[...], gate_ref[...])
        up = dot(mid_ref[...], up_ref[...])
        inner = 0.7978845608028654 * (gate + 0.044715 * gate * gate * gate)
        bent = jnp.tanh(inner)
        half = 0.5 * (1.0 + bent)
        active = gate * half
        slope = half + gate * (0.5 * (1.0 - bent * bent)) * (
            0.7978845608028654 * (1.0 + 3 * 0.044715 * gate * gate)
        )
        hidden_ref[...] = (active * up).astype(BF16)
        active_ref[...] = active.astype(BF16)
        slope_ref[...] = (slope * up).astype(BF16)

    out = ((rows, columns), BF16, (rows, tile), lambda j, s: (0, j))
    first = gate_at // tile
    return call(
        kernel,
        columns // tile,
        scalars,
        [
            (mid, (rows, width), lambda j, s: (0, 0), True),
            (full_first, (width, tile), lambda j, s: (0, first + j), False),
            (full_up, (width, tile), lambda j, s: (0, j), False),
        ],
        [out] * 3,
    )


def feed_out(hidden, block, size, full_down_t, dtype, scalars):
    inner = hidden.shape[1]
    width = full_down_t.shape[0]
    tile = tile_of(width, 256)

    def kernel(_, hidden_ref, down_ref, out):
        out[...] = dot_nt(hidden_ref[...], down_ref[...]).astype(dtype)

    (out,) = call(
        kernel,
        width // tile,
        scalars,
        [
            (hidden, (size, inner), lambda j, s: (block, 0), True),
            (full_down_t, (tile, inner), lambda j, s: (j, 0), False),
        ],
        [((size, width), dtype, (size, tile), lambda j, s: (0, j))],
    )
    return out


def hidden_back(line, pieces, full_down_t, scalars):
    width, columns = full_down_t.shape
    tile = tile_of(columns)
    count = len(pieces)
    sizes = [piece[0].shape[0] for piece in pieces]

    def kernel(_, *refs):
        down = refs[3 * count][...]
        for index in range(count):
            rows_ref, active_ref, slope_ref = refs[index::count][:3]
            gate_ref, up_ref = refs[3 * count + 1 + index :: count][:2]
            d_hidden = dot(rows_ref[...], down)
            gate_ref[...] = (d_hidden * slope_ref[...].astype(F32)).astype(BF16)
            up_ref[...] = (d_hidden * active_ref[...].astype(F32)).astype(BF16)

    rows = [line.next(piece[0]) if index == 0 else piece[0] for index, piece in enumerate(pieces)]
    place = lambda j, s: (0, j)
    factors = [
        (piece[factor], (size, tile), lambda j, s, block=piece[3]: (block, j), False)
        for factor in (1, 2)
        for piece, size in zip(pieces, sizes)
    ]
    outs = line.mark(
        call(
            kernel,
            columns // tile,
            scalars,
            [(array, array.shape, lambda j, s: (0, 0), True) for array in rows]
            + factors
            + [(full_down_t, (width, tile), lambda j, s: (0, j), False)],
            [((size, columns), BF16, (size, tile), place) for size in sizes] * 2,
        )
    )
    return outs[:count], outs[count:]


def mid_back(d_gate, d_up, full_first, gate_at, full_up, dtype, scalars):
    inner = d_gate[0].shape[1]
    width = full_up.shape[0]
    tile = tile_of(width, 256)
    part = 1536
    parts = inner // part
    count = len(d_gate)

    def kernel(_, *refs):
        gates, ups, refs = refs[:count], refs[count : 2 * count], refs[2 * count :]
        for gate_ref, up_ref, out in zip(gates, ups, refs[parts + 1 :]):
            total = dot_nt(up_ref[...], refs[parts][...])
            for index in range(parts):
                here = slice(index * part, (index + 1) * part)
                total += dot_nt(gate_ref[:, here], refs[index][...])
            out[...] = total.astype(dtype)

    return call(
        kernel,
        width // tile,
        scalars,
        [(piece, piece.shape, lambda j, s: (0, 0), True) for piece in [*d_gate, *d_up]]
        + [
            (full_first, (tile, part), lambda j, s, index=index: (j, gate_at // part + index), False)
            for index in range(parts)
        ]
        + [(full_up, (tile, inner), lambda j, s: (j, 0), False)],
        [
            ((piece.shape[0], width), dtype, (piece.shape[0], tile), lambda j, s: (0, j))
            for piece in d_gate
        ],
    )


def dot_tn(left, right):
    return lax.dot_general(left, right, (((0,), (0,)), ((), ())), preferred_element_type=F32)


def soft(query, keys, start):
    scores = dot_nt(query, keys)
    tangent = jnp.tanh(scores * (HEAD_WIDTH**-0.5 / LOGIT_CAP))
    row = lax.broadcasted_iota(jnp.int32, scores.shape, 0) + start
    column = lax.broadcasted_iota(jnp.int32, scores.shape, 1)
    capped = jnp.where(column <= row, LOGIT_CAP * tangent, -jnp.inf)
    terms = jnp.exp(capped - jnp.max(capped, axis=1, keepdims=True))
    return terms / jnp.sum(terms, axis=1, keepdims=True), tangent


def attend(qkv, heads, group, length, scalars, block=256):
    total = qkv.shape[0]
    block = min(block, length)
    seqs = total // length

    def kernel(_, query_ref, key_ref, value_ref, out_ref):
        for start in range(0, length, block):
            end = start + block
            weights, _ = soft(query_ref[start:end, :], key_ref[:end, :], start)
            out_ref[start:end, :] = dot(weights.astype(BF16), value_ref[:end, :]).astype(BF16)

    shape = (length, HEAD_WIDTH)
    (out,) = call(
        kernel,
        seqs * heads,
        scalars,
        [
            (qkv, shape, lambda j, s: (j // heads, j % heads), False),
            (qkv, shape, lambda j, s: (j // heads, heads + 2 * (j % heads // group)), False),
            (qkv, shape, lambda j, s: (j // heads, heads + 2 * (j % heads // group) + 1), False),
        ],
        [((total, heads * HEAD_WIDTH), BF16, shape, lambda j, s: (j // heads, j % heads))],
    )
    return out


def attend_back(qkv, d_attended, heads, group, length, scalars, block=256):
    total = qkv.shape[0]
    block = min(block, length)
    seqs = total // length
    key_heads = heads // group
    scale = HEAD_WIDTH**-0.5

    def kernel(_, query_ref, pair_ref, d_ref, d_query_ref, d_pair_ref, d_key, d_value):
        d_key[...] = jnp.zeros_like(d_key)
        d_value[...] = jnp.zeros_like(d_value)
        for member in range(group):
            columns = slice(member * HEAD_WIDTH, (member + 1) * HEAD_WIDTH)
            for start in range(0, length, block):
                end = start + block
                query = query_ref[start:end, columns]
                d_rows = d_ref[start:end, columns]
                keys, values = pair_ref[:end, :HEAD_WIDTH], pair_ref[:end, HEAD_WIDTH:]
                weights, tangent = soft(query, keys, start)
                d_soft = dot_nt(d_rows, values)
                d_capped = weights * (
                    d_soft - jnp.sum(weights * d_soft, axis=1, keepdims=True)
                )
                d_scores = (d_capped * (1.0 - tangent * tangent)).astype(BF16)
                d_query_ref[start:end, columns] = (dot(d_scores, keys) * scale).astype(BF16)
                d_key[:end, :] += dot_tn(d_scores, query)
                d_value[:end, :] += dot_tn(weights.astype(BF16), d_rows)
        d_pair_ref[:, :HEAD_WIDTH] = (d_key[...] * scale).astype(BF16)
        d_pair_ref[:, HEAD_WIDTH:] = d_value[...].astype(BF16)

    wide, pair = (length, group * HEAD_WIDTH), (length, 2 * HEAD_WIDTH)
    first_pair = heads // 2
    place = lambda j, s: (j // key_heads, j % key_heads)
    return call(
        kernel,
        seqs * key_heads,
        scalars,
        [
            (qkv, wide, place, False),
            (qkv, pair, lambda j, s: (j // key_heads, first_pair + j % key_heads), False),
            (d_attended, wide, place, False),
        ],
        [
            ((total, heads * HEAD_WIDTH), BF16, wide, place),
            ((total, key_heads * 2 * HEAD_WIDTH), BF16, pair, place),
        ],
        scratch=[pltpu.VMEM((length, HEAD_WIDTH), F32)] * 2,
    )


class Grad:
    def __init__(self, dp, chunks, lefts, rights, first_column, columns, scalars):
        self.dp, self.chunks, self.scalars = dp, chunks, scalars
        width = lefts[0].shape[0]
        self.rest, self.rows = dp // 4, width // dp
        self.lefts = [left.reshape(self.rest, 2, 2, self.rows, left.shape[1]) for left in lefts]
        self.rights = rights
        self.columns, self.tile = columns, tile_of(columns)
        self.first = first_column // self.tile
        self.count = len(lefts) + len(rights)

    def inputs(self, block, place):
        return [
            (
                left,
                (self.rest, block, None, *left.shape[3:]),
                lambda j, s: (0, *place(s), 0, 0),
                True,
            )
            for left in self.lefts
        ] + [
            (array, (size, self.tile), lambda j, s, row=row: (row(s), self.first + j), False)
            for array, size, row in self.rights
        ]

    def product(self, refs):
        return sum_of_products(refs[: len(self.lefts)], refs[len(self.lefts) : self.count])

    def run(self, kernel, inputs, outputs):
        return call(kernel, self.columns // self.tile, self.scalars, inputs, outputs)

    def give(self):
        def kernel(_, *refs):
            refs[-1][...] = self.product(refs).astype(BF16)

        shape = (self.rest, 2, self.rows)
        (self.given,) = self.run(
            kernel,
            self.inputs(2, lambda s: (0, 1 - s[0])),
            [((*shape, self.columns), BF16, (*shape, self.tile), lambda j, s: (0, 0, 0, j))],
        )
        return self.given

    def to_core(self):
        return self.given, lambda array: flip(array, 0, self.dp)

    def side(self, from_core):
        self.from_core = from_core
        size = self.rest // self.chunks

        def kernel(_, *refs):
            core = refs[self.count]
            result = (self.product(refs) + core[...].astype(F32)).astype(BF16)
            for index, out in enumerate(refs[self.count + 1 :]):
                out[...] = result[index * size : (index + 1) * size]

        self.give_side = self.run(
            kernel,
            self.inputs(None, lambda s: (1 - s[1], s[0]))
            + [
                (
                    from_core,
                    (self.rest, None, self.rows, self.tile),
                    lambda j, s: (0, 1 - s[1], 0, j),
                    False,
                )
            ],
            [
                (
                    (size, self.rows, self.columns),
                    BF16,
                    (size, self.rows, self.tile),
                    lambda j, s: (0, 0, j),
                )
            ]
            * self.chunks,
        )
        return self.give_side[0]

    def both(self, from_core):
        def kernel(_, *refs):
            result = self.product(refs) + refs[self.count][...].astype(F32)
            refs[-1][...] = result.astype(BF16)

        shape = (self.rest, 2, self.rows)
        place = lambda j, s: (0, 0, 0, j)
        (self.total,) = self.run(
            kernel,
            self.inputs(2, lambda s: (0, s[0]))
            + [(from_core, (*shape, self.tile), place, False)],
            [((*shape, self.columns), BF16, (*shape, self.tile), place)],
        )
        return self.total

    def to_side_last(self):
        side = (lax.axis_index("dp") >> 1) & 1
        parts = self.sums.reshape(2, self.rows, self.columns)
        self.sums = pick(parts, side)
        return pick(parts, 1 - side), lambda array: flip(array, 1, self.dp)

    def add_side(self, part):
        self.sums = self.sums.astype(F32) + part.astype(F32)

    def to_side(self, chunk):
        return self.give_side[chunk], lambda array: flip(array, 1, self.dp)

    def own(self, *from_side):
        size = self.rest // self.chunks

        def kernel(_, *refs):
            core, sides, out = refs[self.count], refs[self.count + 1 : -1], refs[-1]
            result = self.product(refs) + core[...].astype(F32)
            for index, ref in enumerate(sides):
                here = slice(index * size, (index + 1) * size)
                out[here] = (result[here] + ref[...].astype(F32)).astype(BF16)

        place = lambda j, s: (0, 0, j)
        (self.total,) = self.run(
            kernel,
            self.inputs(None, lambda s: (s[1], s[0]))
            + [
                (
                    self.from_core,
                    (self.rest, None, self.rows, self.tile),
                    lambda j, s: (0, s[1], 0, j),
                    False,
                )
            ]
            + [(part, (size, self.rows, self.tile), place, False) for part in from_side],
            [
                (
                    (self.rest, self.rows, self.columns),
                    BF16,
                    (self.rest, self.rows, self.tile),
                    place,
                )
            ],
        )
        return self.total

    def along_rest(self, line):
        groups = [[low + 4 * high for high in range(self.rest)] for low in range(4)]
        self.sums = lax.psum_scatter(
            line.next(self.total).reshape(-1, self.columns),
            "dp",
            scatter_dimension=0,
            axis_index_groups=groups,
            tiled=True,
        )

    def to_owner(self):
        place = lax.axis_index("dp") >> 2
        transfers = []
        for shift in range(1, self.rest):
            pairs = [(i, (i + 4 * shift) % self.dp) for i in range(self.dp)]
            part = pick(self.total, (place + shift) % self.rest)
            transfers.append((part, lambda array, pairs=pairs: lax.ppermute(array, "dp", pairs)))
        return transfers

    def gather(self, parts):
        place = lax.axis_index("dp") >> 2
        total = pick(self.total, place).astype(F32)
        self.sums = sum((part.astype(F32) for part in parts), total)

    def result(self):
        return self.sums.astype(F32)


def pick(array, index):
    return lax.dynamic_index_in_dim(array, index, 0, keepdims=False)


def sum_of_products(lefts, rights):
    *lead, rows, _ = lefts[0].shape
    columns = rights[0].shape[1]
    count = 1
    for extent in lead:
        count *= extent
    rights = [right[...] for right in rights]
    pairs, index = [], 0
    for left in lefts:
        left, at = left[...], 0
        while at < left.shape[-1]:
            size = rights[index].shape[0]
            pairs.append((left[..., at : at + size], rights[index]))
            at += size
            index += 1

    def total(pick_block):
        result = None
        for left, right in pairs:
            term = dot(pick_block(left), right)
            result = term if result is None else result + term
        return result

    if rows % 16 == 0:
        blocks = total(lambda left: left.reshape(count * rows, left.shape[-1]))
    else:
        blocks = jnp.stack(
            [
                total(lambda left, block=block: left.reshape(count, rows, -1)[block])
                for block in range(count)
            ]
        )
    return blocks.reshape(*lead, rows, columns)


def tied(*arrays):
    return lax.optimization_barrier(arrays)


class Line:
    def __init__(self):
        self.last = None

    def next(self, array):
        if self.last is not None:
            array, _ = tied(array, self.last)
        return array

    def mark(self, array):
        self.last = array[0] if isinstance(array, (list, tuple)) else array
        return array

    def send(self, *transfers):
        return [send(self.next(array)) for array, send in transfers]

    def land(self, *flying, sums=()):
        count = len(flying)
        *taken, self.last = tied(*flying, *(grad.sums for grad in sums), self.last)
        for grad, value in zip(sums, taken[count:]):
            grad.sums = value
        return taken[:count]


def projected(pieces, weights, first_column, columns, scalars):
    count = len(pieces)
    half = sum(piece.shape[0] for piece in pieces) // 2
    width = pieces[0].shape[1]
    tile = tile_of(columns)

    def kernel(scalar_ref, *refs):
        *ins, weight_ref, out = refs
        weight = weight_ref[...]
        at = 0
        for ref in ins:
            owner = scalar_ref[2] if at < half else 1 - scalar_ref[2]
            size = ref.shape[0]
            start = pl.multiple_of(owner * half + at % half, size)
            out[pl.ds(start, size), :] = dot(ref[...], weight).astype(BF16)
            at += size

    (out,) = call(
        kernel,
        columns // tile,
        scalars,
        [(piece, piece.shape, lambda j, s: (0, 0), True) for piece in pieces]
        + [(weights, (width, tile), lambda j, s: (0, first_column // tile + j), False)],
        [((2 * half, columns), BF16, (2 * half, tile), lambda j, s: (0, j))],
    )
    return out


def projected_back(sources, weights, owner, pieces, dtype, scalars):
    half = sources[0][0].shape[0] // 2
    width = weights.shape[0]
    tile = tile_of(width, 256)
    size = half // pieces
    count = len(sources)

    def kernel(_, *refs):
        total = None
        for rows, weight in zip(refs[:count], refs[count : 2 * count]):
            term = dot_nt(rows[...], weight[...])
            total = term if total is None else total + term
        result = total.astype(dtype)
        for index, out in enumerate(refs[2 * count :]):
            out[...] = result[index * size : (index + 1) * size]

    return call(
        kernel,
        width // tile,
        scalars,
        [
            (array, (half, array.shape[1]), lambda j, s: (owner(s), 0), True)
            for array, _ in sources
        ]
        + [
            (weights, (tile, array.shape[1]), lambda j, s, block=block: (j, block), False)
            for array, block in sources
        ],
        [((size, width), dtype, (size, tile), lambda j, s: (0, j))] * pieces,
    )


def norms_back(line, sums, middle, gain_mid, upstream, branch, gain_branch, scalars):
    rows, width = middle.shape
    count = len(sums)
    size = sums[0][0].shape[0]
    block = 64
    steps, each = rows // block, size // block
    given = [(middle, gain_mid)] + ([] if branch is None else [(branch, gain_branch)])
    norms = len(given)
    outs = 1 if branch is None else 1 + count

    def back(values, gain, d_normed):
        values = values.astype(F32)
        scale = lax.rsqrt(jnp.mean(values * values, axis=1, keepdims=True) + EPSILON)
        normed = values * scale
        weighted = d_normed * gain
        inner = jnp.mean(weighted * normed, axis=1, keepdims=True)
        grad = scale * (weighted - normed * inner)
        return grad, jnp.sum(d_normed * normed, axis=0, keepdims=True)

    def kernel(_, *refs):
        parts, upstream_ref, refs = refs[: 2 * count], refs[2 * count], refs[2 * count + 1 :]
        values_refs, gain_refs, refs = refs[:norms], refs[norms : 2 * norms], refs[2 * norms :]
        grad_refs, gain_grad_refs = refs[:outs], refs[outs:]
        step = pl.program_id(0)

        @pl.when(step == 0)
        def _():
            for ref in gain_grad_refs:
                ref[...] = jnp.zeros_like(ref)

        for index in range(count):

            @pl.when(step // each == index)
            def _(index=index):
                d_normed = parts[2 * index][...] + parts[2 * index + 1][...].astype(F32)
                grad, grad_gain = back(values_refs[0][...], gain_refs[0][...], d_normed)
                gain_grad_refs[0][...] += grad_gain
                total = upstream_ref[...].astype(F32) + grad
                grad_refs[0][...] = total
                if norms > 1:
                    grad, grad_gain = back(values_refs[1][...], gain_refs[1][...], total)
                    gain_grad_refs[1][...] += grad_gain
                    grad_refs[1 + index][...] = grad.astype(BF16)

    def piece(index):
        return lambda j, s: (jnp.clip(j - index * each, 0, each - 1), 0)

    shape = (block, width)
    every = lambda j, s: (j, 0)
    once = lambda j, s: (0, 0)
    (first, *others), *later = sums
    sums = [(line.next(first), *others), *later]
    return line.mark(
        call(
            kernel,
            steps,
            scalars,
            [
                (array, shape, piece(index), False)
                for index, pair in enumerate(sums)
                for array in pair
            ]
            + [(array, shape, every, False) for array in (upstream, *(v for v, _ in given))]
            + [(gain[None], (1, width), once, True) for _, gain in given],
            [((rows, width), F32, shape, every)]
            + [((size, width), BF16, shape, piece(index)) for index in range(outs - 1)]
            + [((1, width), F32, (1, width), once)] * norms,
        )
    )


def joined(weights):
    rows = weights[0].shape[0]
    width = sum(weight.shape[1] for weight in weights)

    def kernel(query_ref, key_ref, value_ref, output_ref, gate_ref, out_ref):
        parts = [query_ref[...]]
        for head in range(key_ref.shape[1] // HEAD_WIDTH):
            here = slice(head * HEAD_WIDTH, (head + 1) * HEAD_WIDTH)
            parts += [key_ref[:, here], value_ref[:, here]]
        at = 0
        for part in [*parts, output_ref[...], gate_ref[...]]:
            out_ref[:, at : at + part.shape[1]] = part
            at += part.shape[1]

    return pl.pallas_call(
        kernel,
        out_shape=jax.ShapeDtypeStruct((rows, width), BF16),
        in_specs=[pl.BlockSpec(memory_space=pltpu.VMEM)] * 5,
        out_specs=pl.BlockSpec(memory_space=pltpu.VMEM),
        compiler_params=pltpu.CompilerParams(vmem_limit_bytes=VMEM_BYTES),
    )(*weights)


def owner_parts(partial):
    count, width = partial.shape
    devices = lax.axis_size("dp") * lax.axis_size("tensor")
    return partial.reshape(count, devices, width // devices).transpose(1, 0, 2)


def to_owners(parts):
    return lax.all_to_all(parts, ("dp", "tensor"), 0, 0, tiled=True)


def make_body(dp):
    def body(
        layer_input,
        query_weight,
        key_weight,
        value_weight,
        w_output,
        w_gate,
        w_up,
        w_down,
        gain_attn_in,
        gain_attn_out,
        gain_ffn_in,
        gain_ffn_out,
        cotangent,
    ):
        line = Line()
        place, turn = lax.axis_index("dp"), lax.axis_index("tensor")
        scalars = [place & 1, (place >> 1) & 1, turn]
        to_other = lambda array: (array, swap)
        mine, theirs = (lambda s: s[2]), (lambda s: 1 - s[2])
        query_cols, key_cols = query_weight.shape[1], key_weight.shape[1]
        qkv_cols = query_cols + 2 * key_cols
        gate_at = qkv_cols + query_cols
        columns = w_gate.shape[1]
        half = layer_input.shape[0]
        quarter = half // 2
        heads = query_cols // HEAD_WIDTH
        group = QUERY_HEADS // KEY_VALUE_HEADS
        full_first = lax.all_gather(
            joined([query_weight, key_weight, value_weight, w_output.T, w_gate]),
            "dp",
            axis=0,
            tiled=True,
        )
        full_up = lax.all_gather(w_up, "dp", axis=0, tiled=True)
        full_down_t = lax.all_gather(w_down.T, "dp", axis=0, tiled=True)
        gains = gather_small(
            jnp.stack([gain_attn_in, gain_attn_out, gain_ffn_in, gain_ffn_out]), dp
        )
        gain_a, gain_b, gain_c, gain_d = gains[0], gains[1], gains[2], gains[3]

        residual_in = layer_input.astype(F32)
        upstream = cotangent.astype(F32)
        input_own = line.mark(rms_norm(residual_in, gain_a).astype(BF16))
        input_other = swap(input_own)
        input_own_t = line.mark(turned([input_own], scalars))
        (input_other,) = line.land(input_other)
        input_other_t = line.mark(turned([input_other], scalars))
        qkv = line.mark(
            projected([input_own, line.next(input_other)], full_first, 0, qkv_cols, scalars)
        )
        attended = line.mark(attend(qkv, heads, group, SEQ_LEN, scalars))
        output_block = qkv_cols // query_cols
        (give,) = line.mark(
            projected_back([(attended, output_block)], full_first, theirs, 1, BF16, scalars)
        )
        (taken,) = line.send(to_other(give))
        (kept,) = line.mark(
            projected_back(
                [(line.next(attended), output_block)], full_first, mine, 1, F32, scalars
            )
        )
        branch_attn = kept + taken.astype(F32)
        middle = residual_in + rms_norm(branch_attn, gain_b)
        mid_own = line.mark(rms_norm(middle, gain_c).astype(BF16))
        (mid_other,) = line.send(to_other(mid_own))
        hidden_own, active_own, slope_own = line.mark(
            feed(mid_own, full_first, gate_at, full_up, scalars)
        )
        mid_own_t = line.mark(turned([line.next(mid_own)], scalars))
        (mid_other,) = line.land(mid_other)
        hidden_other, active_other, slope_other = line.mark(
            feed(line.next(mid_other), full_first, gate_at, full_up, scalars)
        )
        mid_other_t = line.mark(turned([line.next(mid_other)], scalars))

        def ffn_back(kept, taken, middle, upstream):
            branch = kept + taken.astype(F32)
            ffn_out, pull = jax.vjp(rms_norm, branch, gain_d)
            d_ffn, grad_gain = pull(upstream)
            return (middle + ffn_out).astype(BF16), line.mark(d_ffn.astype(BF16)), grad_gain

        low, high = slice(0, quarter), slice(quarter, half)
        give_1 = line.mark(
            feed_out(line.next(hidden_other), 0, quarter, full_down_t, BF16, scalars)
        )
        (taken_1,) = line.send(to_other(give_1))
        give_2 = line.mark(
            feed_out(line.next(hidden_other), 1, quarter, full_down_t, BF16, scalars)
        )
        (taken_1,) = line.land(taken_1)
        (taken_2,) = line.send(to_other(give_2))
        kept = line.mark(feed_out(line.next(hidden_own), 0, half, full_down_t, F32, scalars))
        output_1, d_ffn_1, grad_d_1 = ffn_back(
            line.next(kept)[low], taken_1, middle[low], upstream[low]
        )
        (taken_2,) = line.land(taken_2)
        (d_ffn_3,) = line.send(to_other(d_ffn_1))
        output_2, d_ffn_2, grad_d_2 = ffn_back(
            line.next(kept)[high], taken_2, middle[high], upstream[high]
        )
        d_ffn_own_t = line.mark(turned([line.next(d_ffn_1), d_ffn_2], scalars))
        (d_gate_1,), (d_up_1,) = hidden_back(
            line, [(d_ffn_1, active_own, slope_own, 0)], full_down_t, scalars
        )
        (d_ffn_3,) = line.land(d_ffn_3)
        (d_ffn_4,) = line.send(to_other(d_ffn_2))
        layer_output = jnp.concatenate([output_1, output_2], axis=0)
        grad_d = grad_d_1 + grad_d_2
        (d_gate_2, d_gate_3), (d_up_2, d_up_3) = hidden_back(
            line,
            [(d_ffn_2, active_own, slope_own, 1), (d_ffn_3, active_other, slope_other, 0)],
            full_down_t,
            scalars,
        )
        (d_ffn_4,) = line.land(d_ffn_4)
        d_ffn_other_t = line.mark(turned([line.next(d_ffn_3), d_ffn_4], scalars))

        first = lambda s: 0
        tile = tile_of(columns)
        tiles = columns // tile
        cuts = [0, 2 * tile, 4 * tile, columns]
        split = tile * -(-tiles // 2)
        halves = [(0, split), (split, columns - split)]
        hidden_rights = [(hidden_own, half, first), (hidden_other, half, first)]
        mid_lefts = [mid_own_t, mid_other_t]

        def down_part(part, chunks):
            lefts = [line.next(d_ffn_own_t), d_ffn_other_t]
            start, end = cuts[part], cuts[part + 1]
            return Grad(dp, chunks, lefts, hidden_rights, start, end - start, scalars)

        def mid_part(pieces, part):
            rights = [(line.next(piece), quarter, first) for piece in pieces]
            return Grad(dp, 2, mid_lefts, rights, *halves[part], scalars)

        def mid_back_of(gates, ups, dtype):
            gates = [line.next(gates[0]), *gates[1:]]
            return line.mark(mid_back(gates, ups, full_first, gate_at, full_up, dtype, scalars))

        down_0 = down_part(0, 1)
        line.mark(down_0.give())
        (core_0,) = line.send(down_0.to_core())
        down_2 = down_part(2, 2)
        line.mark(down_2.give())
        (core_0,) = line.land(core_0)
        line.mark(down_0.side(line.next(core_0)))

        down_0_side, core_2 = line.send(down_0.to_side(0), down_2.to_core())
        down_1 = down_part(1, 1)
        line.mark(down_1.give())
        (d_gate_4,), (d_up_4,) = hidden_back(
            line, [(d_ffn_4, active_other, slope_other, 1)], full_down_t, scalars
        )
        d_gates = [d_gate_1, d_gate_2, d_gate_3, d_gate_4]
        d_ups = [d_up_1, d_up_2, d_up_3, d_up_4]
        (core_2,) = line.land(core_2)
        line.mark(down_2.side(line.next(core_2)))
        (down_0_side,) = line.land(down_0_side)

        side_0, core_1 = line.send(down_2.to_side(0), down_1.to_core())
        line.mark(down_0.own(line.next(down_0_side)))
        gate_0 = mid_part(d_gates, 0)
        line.mark(gate_0.give())
        (core_1,) = line.land(core_1)
        line.mark(down_1.both(line.next(core_1)))
        gate_1 = mid_part(d_gates, 1)
        line.mark(gate_1.give())
        (side_0,) = line.land(side_0)

        side_1, core_0, core_1 = line.send(
            down_2.to_side(1), gate_0.to_core(), gate_1.to_core()
        )
        down_0.along_rest(line)
        give_1, give_2 = mid_back_of(d_gates[2:], d_ups[2:], BF16)
        core_0, core_1 = line.land(core_0, core_1)
        line.mark(gate_0.side(line.next(core_0)))
        (side_1,) = line.land(
            side_1, sums=[down_0]
        )

        gate_0_side_0, gate_0_side_1, taken_1, taken_2 = line.send(
            gate_0.to_side(0), gate_0.to_side(1), to_other(give_1), to_other(give_2)
        )
        down_1.along_rest(line)
        line.mark(down_2.own(line.next(side_0), side_1))
        line.mark(gate_1.side(line.next(core_1)))
        up_0 = mid_part(d_ups, 0)
        line.mark(up_0.give())
        kept_1, kept_2 = mid_back_of(d_gates[:2], d_ups[:2], F32)
        gate_0_side_0, gate_0_side_1, taken_1, taken_2 = line.land(
            gate_0_side_0, gate_0_side_1, taken_1, taken_2, sums=[down_1]
        )

        gate_1_side_0, core_0 = line.send(gate_1.to_side(0), up_0.to_core())
        down_2.along_rest(line)
        d_middle, d_branch_1, d_branch_2, grad_c, grad_b = norms_back(
            line,
            [(kept_1, taken_1), (kept_2, taken_2)],
            middle,
            gain_c,
            cotangent,
            branch_attn,
            gain_b,
            scalars,
        )
        (core_0,) = line.land(core_0)
        line.mark(up_0.side(line.next(core_0)))
        (gate_1_side_0,) = line.land(gate_1_side_0)

        gate_1_side_1, d_branch_3, down_1_side = line.send(
            gate_1.to_side(1), to_other(d_branch_1), down_1.to_side_last()
        )
        line.mark(gate_0.own(line.next(gate_0_side_0), gate_0_side_1))
        up_1 = mid_part(d_ups, 1)
        line.mark(up_1.give())
        d_branch_own_t = line.mark(turned([line.next(d_branch_1), d_branch_2], scalars))
        gate_1_side_1, d_branch_3, down_1_side = line.land(
            gate_1_side_1, d_branch_3, down_1_side, sums=[down_2]
        )
        down_1.add_side(down_1_side)

        up_0_side_0, core_1, d_branch_4 = line.send(
            up_0.to_side(0), up_1.to_core(), to_other(d_branch_2)
        )
        gate_0.along_rest(line)
        line.mark(gate_1.own(line.next(gate_1_side_0), gate_1_side_1))
        (core_1,) = line.land(core_1)
        line.mark(up_1.side(line.next(core_1)))
        up_0_side_0, d_branch_4 = line.land(up_0_side_0, d_branch_4)

        (up_0_side_1,) = line.send(up_0.to_side(1))
        gate_1.along_rest(line)
        d_attended = line.mark(
            projected(
                [line.next(d_branch_1), d_branch_2, d_branch_3, d_branch_4],
                full_first,
                qkv_cols,
                query_cols,
                scalars,
            )
        )
        d_branch_other_t = line.mark(turned([line.next(d_branch_3), d_branch_4], scalars))
        d_query, d_pair = line.mark(
            attend_back(qkv, line.next(d_attended), heads, group, SEQ_LEN, scalars)
        )
        (up_0_side_1,) = line.land(
            up_0_side_1, sums=[gate_0]
        )

        (up_1_side_0,) = line.send(up_1.to_side(0))
        line.mark(up_0.own(line.next(up_0_side_0), up_0_side_1))
        output = Grad(
            dp,
            1,
            [d_branch_own_t, line.next(d_branch_other_t)],
            [(attended, half, mine), (attended, half, theirs)],
            0,
            query_cols,
            scalars,
        )
        line.mark(output.give())

        def input_part(array, width):
            rights = [(line.next(array), half, mine), (array, half, theirs)]
            return Grad(dp, 1, [input_own_t, input_other_t], rights, 0, width, scalars)

        query = input_part(d_query, query_cols)
        line.mark(query.give())
        pair = input_part(d_pair, 2 * key_cols)
        line.mark(pair.give())
        (up_1_side_0,) = line.land(up_1_side_0)

        up_1_side_1, core, query_core, pair_core = line.send(
            up_1.to_side(1), output.to_core(), query.to_core(), pair.to_core()
        )
        up_0.along_rest(line)
        give_1, give_2 = line.mark(
            projected_back(
                [(line.next(d_query), 0), (d_pair, 1)], full_first, theirs, 2, BF16, scalars
            )
        )
        core, query_core, pair_core = line.land(core, query_core, pair_core)
        line.mark(output.side(line.next(core)))
        line.mark(query.side(line.next(query_core)))
        line.mark(pair.side(line.next(pair_core)))
        (up_1_side_1,) = line.land(up_1_side_1, sums=[gate_1])

        output_side, taken_1 = line.send(output.to_side(0), to_other(give_1))
        line.mark(up_1.own(line.next(up_1_side_0), up_1_side_1))
        kept_1, kept_2 = line.mark(
            projected_back(
                [(line.next(d_query), 0), (d_pair, 1)], full_first, mine, 2, F32, scalars
            )
        )
        output_side, taken_1 = line.land(output_side, taken_1)

        query_side, taken_2 = line.send(query.to_side(0), to_other(give_2))
        up_1.along_rest(line)
        line.mark(output.own(line.next(output_side)))
        query_side, taken_2 = line.land(query_side, taken_2, sums=[up_0])
        line.mark(query.own(line.next(query_side)))

        pair_side, *query_parts = line.send(pair.to_side(0), *query.to_owner())
        input_grad, grad_a = norms_back(
            line,
            [(kept_1, taken_1), (kept_2, taken_2)],
            layer_input,
            gain_a,
            d_middle,
            None,
            None,
            scalars,
        )
        gain_grads = jnp.stack([grad_a[0], grad_b[0], grad_c[0], grad_d])
        gain_grads = line.mark(owner_parts(gain_grads))
        (pair_side,) = line.land(pair_side)
        line.mark(pair.own(line.next(pair_side)))
        output.along_rest(line)
        query_parts = line.land(*query_parts, sums=[up_1])
        pair_parts = line.send(*pair.to_owner())
        pair_parts = line.land(*pair_parts)
        (gain_parts,) = line.send((gain_grads, to_owners))
        (gain_parts,) = line.land(gain_parts)
        small = jnp.sum(gain_parts, axis=0)
        query.gather(query_parts)
        pair.gather(pair_parts)

        down, gate, up = [down_0, down_1, down_2], [gate_0, gate_1], [up_0, up_1]
        grad_pair = pair.result().reshape(-1, key_cols // HEAD_WIDTH, 2, HEAD_WIDTH)
        grad_down = jnp.concatenate([part.result() for part in down], axis=1).T
        return (
            layer_output,
            input_grad,
            query.result(),
            grad_pair[:, :, 0].reshape(-1, key_cols),
            grad_pair[:, :, 1].reshape(-1, key_cols),
            output.result().T,
            jnp.concatenate([part.result() for part in gate], axis=1),
            jnp.concatenate([part.result() for part in up], axis=1),
            grad_down,
            small[0],
            small[1],
            small[2],
            small[3],
        )

    return body


def solution(mesh):
    rows = P(("dp", "tensor"), None)
    gain = P(("dp", "tensor"))
    into, out_of = P("dp", "tensor"), P("tensor", "dp")
    return jax.shard_map(
        make_body(mesh.shape["dp"]),
        mesh=mesh,
        in_specs=(rows, into, into, into, out_of, into, into, out_of, gain, gain, gain, gain, rows),
        out_specs=(rows, rows, into, into, into, out_of, into, into, out_of, gain, gain, gain, gain),
        check_vma=False,
    )
```

```python
import jax
import jax.numpy as jnp
from jax import lax
from jax.experimental import pallas as pl
from jax.experimental.pallas import tpu as pltpu
from jax.sharding import PartitionSpec as P

QUERY_HEADS = 8
KEY_VALUE_HEADS = 4
HEAD_WIDTH = 256
SEQ_LEN = 1024

EPSILON = 1e-06
LOGIT_CAP = 50.0

BF16 = jnp.bfloat16
F32 = jnp.float32
VMEM_BYTES = 56 * 1024 * 1024


def rms_norm(values, gain):
    return values * lax.rsqrt(jnp.mean(values * values, axis=-1, keepdims=True) + EPSILON) * gain


def swap(rows):
    return lax.ppermute(rows, "tensor", [(0, 1), (1, 0)])


def flip(array, bit, dp):
    return lax.ppermute(array, "dp", [(i, i ^ (1 << bit)) for i in range(dp)])


def gather_small(piece, dp):
    other = swap(piece)
    whole = jnp.where(
        lax.axis_index("tensor") == 0,
        jnp.concatenate([piece, other], axis=1),
        jnp.concatenate([other, piece], axis=1),
    )
    bit = 0
    while (1 << bit) < dp:
        other = flip(whole, bit, dp)
        high = (lax.axis_index("dp") >> bit) & 1
        whole = jnp.where(
            high == 0,
            jnp.concatenate([whole, other], axis=1),
            jnp.concatenate([other, whole], axis=1),
        )
        bit += 1
    return whole


def dot(left, right):
    return lax.dot_general(left, right, (((1,), (0,)), ((), ())), preferred_element_type=F32)


def dot_nt(left, right):
    return lax.dot_general(left, right, (((1,), (1,)), ((), ())), preferred_element_type=F32)


def call(kernel, steps, scalars, inputs, outputs, scratch=()):
    in_specs = [
        pl.BlockSpec(block, index, pipeline_mode=pl.Buffered(1) if whole else None)
        for _, block, index, whole in inputs
    ]
    out_specs = [pl.BlockSpec(block, index) for _, _, block, index in outputs]
    shapes = [jax.ShapeDtypeStruct(shape, dtype) for shape, dtype, _, _ in outputs]
    return pl.pallas_call(
        kernel,
        grid_spec=pltpu.PrefetchScalarGridSpec(
            num_scalar_prefetch=1,
            grid=(steps,),
            in_specs=in_specs,
            out_specs=out_specs,
            scratch_shapes=list(scratch),
        ),
        out_shape=shapes,
        compiler_params=pltpu.CompilerParams(vmem_limit_bytes=VMEM_BYTES),
        cost_estimate=pl.CostEstimate(flops=1, bytes_accessed=1, transcendentals=0),
    )(jnp.stack(scalars).astype(jnp.int32), *(array for array, *_ in inputs))


def tile_of(extent, most=512):
    tile = most
    while extent % tile:
        tile //= 2
    return tile


def turned(pieces, scalars):
    rows = [piece.shape[0] for piece in pieces]
    width = pieces[0].shape[1]
    tile = tile_of(width, 768)

    def kernel(_, *refs):
        *ins, out = refs
        row = lax.broadcasted_iota(jnp.int32, (tile, tile), 0)
        column = lax.broadcasted_iota(jnp.int32, (tile, tile), 1)
        same = (row == column).astype(F32).astype(BF16)
        at = 0
        for ref, count in zip(ins, rows):
            out[:, at : at + count] = dot_nt(same, ref[...]).astype(BF16)
            at += count

    (out,) = call(
        kernel,
        width // tile,
        scalars,
        [(piece, (count, tile), lambda j, s: (0, j), False) for piece, count in zip(pieces, rows)],
        [((width, sum(rows)), BF16, (tile, sum(rows)), lambda j, s: (j, 0))],
    )
    return out


def feed(mid, full_first, gate_at, full_up, scalars):
    rows, width = mid.shape
    columns = full_up.shape[1]
    tile = tile_of(columns)

    def kernel(_, mid_ref, gate_ref, up_ref, hidden_ref, active_ref, slope_ref):
        gate = dot(mid_ref[...], gate_ref[...])
        up = dot(mid_ref[...], up_ref[...])
        inner = 0.7978845608028654 * (gate + 0.044715 * gate * gate * gate)
        bent = jnp.tanh(inner)
        half = 0.5 * (1.0 + bent)
        active = gate * half
        slope = half + gate * (0.5 * (1.0 - bent * bent)) * (
            0.7978845608028654 * (1.0 + 3 * 0.044715 * gate * gate)
        )
        hidden_ref[...] = (active * up).astype(BF16)
        active_ref[...] = active.astype(BF16)
        slope_ref[...] = (slope * up).astype(BF16)

    out = ((rows, columns), BF16, (rows, tile), lambda j, s: (0, j))
    first = gate_at // tile
    return call(
        kernel,
        columns // tile,
        scalars,
        [
            (mid, (rows, width), lambda j, s: (0, 0), True),
            (full_first, (width, tile), lambda j, s: (0, first + j), False),
            (full_up, (width, tile), lambda j, s: (0, j), False),
        ],
        [out] * 3,
    )


def feed_out(hidden, block, size, full_down_t, dtype, scalars):
    inner = hidden.shape[1]
    width = full_down_t.shape[0]
    tile = tile_of(width, 256)

    def kernel(_, hidden_ref, down_ref, out):
        out[...] = dot_nt(hidden_ref[...], down_ref[...]).astype(dtype)

    (out,) = call(
        kernel,
        width // tile,
        scalars,
        [
            (hidden, (size, inner), lambda j, s: (block, 0), True),
            (full_down_t, (tile, inner), lambda j, s: (j, 0), False),
        ],
        [((size, width), dtype, (size, tile), lambda j, s: (0, j))],
    )
    return out


def hidden_back(line, pieces, full_down_t, scalars):
    width, columns = full_down_t.shape
    tile = tile_of(columns)
    count = len(pieces)
    sizes = [piece[0].shape[0] for piece in pieces]

    def kernel(_, *refs):
        down = refs[3 * count][...]
        for index in range(count):
            rows_ref, active_ref, slope_ref = refs[index::count][:3]
            gate_ref, up_ref = refs[3 * count + 1 + index :: count][:2]
            d_hidden = dot(rows_ref[...], down)
            gate_ref[...] = (d_hidden * slope_ref[...].astype(F32)).astype(BF16)
            up_ref[...] = (d_hidden * active_ref[...].astype(F32)).astype(BF16)

    rows = [line.next(piece[0]) if index == 0 else piece[0] for index, piece in enumerate(pieces)]
    place = lambda j, s: (0, j)
    factors = [
        (piece[factor], (size, tile), lambda j, s, block=piece[3]: (block, j), False)
        for factor in (1, 2)
        for piece, size in zip(pieces, sizes)
    ]
    outs = line.mark(
        call(
            kernel,
            columns // tile,
            scalars,
            [(array, array.shape, lambda j, s: (0, 0), True) for array in rows]
            + factors
            + [(full_down_t, (width, tile), lambda j, s: (0, j), False)],
            [((size, columns), BF16, (size, tile), place) for size in sizes] * 2,
        )
    )
    return outs[:count], outs[count:]


def mid_back(d_gate, d_up, full_first, gate_at, full_up, dtype, scalars):
    inner = d_gate[0].shape[1]
    width = full_up.shape[0]
    tile = tile_of(width, 256)
    part = 1536
    parts = inner // part
    count = len(d_gate)

    def kernel(_, *refs):
        gates, ups, refs = refs[:count], refs[count : 2 * count], refs[2 * count :]
        for gate_ref, up_ref, out in zip(gates, ups, refs[parts + 1 :]):
            total = dot_nt(up_ref[...], refs[parts][...])
            for index in range(parts):
                here = slice(index * part, (index + 1) * part)
                total += dot_nt(gate_ref[:, here], refs[index][...])
            out[...] = total.astype(dtype)

    return call(
        kernel,
        width // tile,
        scalars,
        [(piece, piece.shape, lambda j, s: (0, 0), True) for piece in [*d_gate, *d_up]]
        + [
            (full_first, (tile, part), lambda j, s, index=index: (j, gate_at // part + index), False)
            for index in range(parts)
        ]
        + [(full_up, (tile, inner), lambda j, s: (j, 0), False)],
        [
            ((piece.shape[0], width), dtype, (piece.shape[0], tile), lambda j, s: (0, j))
            for piece in d_gate
        ],
    )


def dot_tn(left, right):
    return lax.dot_general(left, right, (((0,), (0,)), ((), ())), preferred_element_type=F32)


def soft(query, keys, start):
    scores = dot_nt(query, keys)
    tangent = jnp.tanh(scores * (HEAD_WIDTH**-0.5 / LOGIT_CAP))
    row = lax.broadcasted_iota(jnp.int32, scores.shape, 0) + start
    column = lax.broadcasted_iota(jnp.int32, scores.shape, 1)
    capped = jnp.where(column <= row, LOGIT_CAP * tangent, -jnp.inf)
    terms = jnp.exp(capped - jnp.max(capped, axis=1, keepdims=True))
    return terms / jnp.sum(terms, axis=1, keepdims=True), tangent


def attend(qkv, heads, group, length, scalars, block=256):
    total = qkv.shape[0]
    block = min(block, length)
    seqs = total // length

    def kernel(_, query_ref, key_ref, value_ref, out_ref):
        for start in range(0, length, block):
            end = start + block
            weights, _ = soft(query_ref[start:end, :], key_ref[:end, :], start)
            out_ref[start:end, :] = dot(weights.astype(BF16), value_ref[:end, :]).astype(BF16)

    shape = (length, HEAD_WIDTH)
    (out,) = call(
        kernel,
        seqs * heads,
        scalars,
        [
            (qkv, shape, lambda j, s: (j // heads, j % heads), False),
            (qkv, shape, lambda j, s: (j // heads, heads + 2 * (j % heads // group)), False),
            (qkv, shape, lambda j, s: (j // heads, heads + 2 * (j % heads // group) + 1), False),
        ],
        [((total, heads * HEAD_WIDTH), BF16, shape, lambda j, s: (j // heads, j % heads))],
    )
    return out


def attend_back(qkv, d_attended, heads, group, length, scalars, block=256):
    total = qkv.shape[0]
    block = min(block, length)
    seqs = total // length
    key_heads = heads // group
    scale = HEAD_WIDTH**-0.5

    def kernel(_, query_ref, pair_ref, d_ref, d_query_ref, d_pair_ref, d_key, d_value):
        d_key[...] = jnp.zeros_like(d_key)
        d_value[...] = jnp.zeros_like(d_value)
        for member in range(group):
            columns = slice(member * HEAD_WIDTH, (member + 1) * HEAD_WIDTH)
            for start in range(0, length, block):
                end = start + block
                query = query_ref[start:end, columns]
                d_rows = d_ref[start:end, columns]
                keys, values = pair_ref[:end, :HEAD_WIDTH], pair_ref[:end, HEAD_WIDTH:]
                weights, tangent = soft(query, keys, start)
                d_soft = dot_nt(d_rows, values)
                d_capped = weights * (
                    d_soft - jnp.sum(weights * d_soft, axis=1, keepdims=True)
                )
                d_scores = (d_capped * (1.0 - tangent * tangent)).astype(BF16)
                d_query_ref[start:end, columns] = (dot(d_scores, keys) * scale).astype(BF16)
                d_key[:end, :] += dot_tn(d_scores, query)
                d_value[:end, :] += dot_tn(weights.astype(BF16), d_rows)
        d_pair_ref[:, :HEAD_WIDTH] = (d_key[...] * scale).astype(BF16)
        d_pair_ref[:, HEAD_WIDTH:] = d_value[...].astype(BF16)

    wide, pair = (length, group * HEAD_WIDTH), (length, 2 * HEAD_WIDTH)
    first_pair = heads // 2
    place = lambda j, s: (j // key_heads, j % key_heads)
    return call(
        kernel,
        seqs * key_heads,
        scalars,
        [
            (qkv, wide, place, False),
            (qkv, pair, lambda j, s: (j // key_heads, first_pair + j % key_heads), False),
            (d_attended, wide, place, False),
        ],
        [
            ((total, heads * HEAD_WIDTH), BF16, wide, place),
            ((total, key_heads * 2 * HEAD_WIDTH), BF16, pair, place),
        ],
        scratch=[pltpu.VMEM((length, HEAD_WIDTH), F32)] * 2,
    )


class Grad:
    def __init__(self, dp, chunks, lefts, rights, first_column, columns, scalars):
        self.dp, self.chunks, self.scalars = dp, chunks, scalars
        width = lefts[0].shape[0]
        self.rest, self.rows = dp // 4, width // dp
        self.lefts = [left.reshape(self.rest, 2, 2, self.rows, left.shape[1]) for left in lefts]
        self.rights = rights
        self.columns, self.tile = columns, tile_of(columns)
        self.first = first_column // self.tile
        self.count = len(lefts) + len(rights)

    def inputs(self, block, place):
        return [
            (
                left,
                (self.rest, block, None, *left.shape[3:]),
                lambda j, s: (0, *place(s), 0, 0),
                True,
            )
            for left in self.lefts
        ] + [
            (array, (size, self.tile), lambda j, s, row=row: (row(s), self.first + j), False)
            for array, size, row in self.rights
        ]

    def product(self, refs):
        return sum_of_products(refs[: len(self.lefts)], refs[len(self.lefts) : self.count])

    def run(self, kernel, inputs, outputs):
        return call(kernel, self.columns // self.tile, self.scalars, inputs, outputs)

    def give(self):
        def kernel(_, *refs):
            refs[-1][...] = self.product(refs).astype(BF16)

        shape = (self.rest, 2, self.rows)
        (self.given,) = self.run(
            kernel,
            self.inputs(2, lambda s: (0, 1 - s[0])),
            [((*shape, self.columns), BF16, (*shape, self.tile), lambda j, s: (0, 0, 0, j))],
        )
        return self.given

    def to_core(self):
        return self.given, lambda array: flip(array, 0, self.dp)

    def side(self, from_core):
        self.from_core = from_core
        size = self.rest // self.chunks

        def kernel(_, *refs):
            core = refs[self.count]
            result = (self.product(refs) + core[...].astype(F32)).astype(BF16)
            for index, out in enumerate(refs[self.count + 1 :]):
                out[...] = result[index * size : (index + 1) * size]

        self.give_side = self.run(
            kernel,
            self.inputs(None, lambda s: (1 - s[1], s[0]))
            + [
                (
                    from_core,
                    (self.rest, None, self.rows, self.tile),
                    lambda j, s: (0, 1 - s[1], 0, j),
                    False,
                )
            ],
            [
                (
                    (size, self.rows, self.columns),
                    BF16,
                    (size, self.rows, self.tile),
                    lambda j, s: (0, 0, j),
                )
            ]
            * self.chunks,
        )
        return self.give_side[0]

    def both(self, from_core):
        def kernel(_, *refs):
            result = self.product(refs) + refs[self.count][...].astype(F32)
            refs[-1][...] = result.astype(BF16)

        shape = (self.rest, 2, self.rows)
        place = lambda j, s: (0, 0, 0, j)
        (self.total,) = self.run(
            kernel,
            self.inputs(2, lambda s: (0, s[0]))
            + [(from_core, (*shape, self.tile), place, False)],
            [((*shape, self.columns), BF16, (*shape, self.tile), place)],
        )
        return self.total

    def to_side_last(self):
        side = (lax.axis_index("dp") >> 1) & 1
        parts = self.sums.reshape(2, self.rows, self.columns)
        self.sums = pick(parts, side)
        return pick(parts, 1 - side), lambda array: flip(array, 1, self.dp)

    def add_side(self, part):
        self.sums = self.sums.astype(F32) + part.astype(F32)

    def to_side(self, chunk):
        return self.give_side[chunk], lambda array: flip(array, 1, self.dp)

    def own(self, *from_side):
        size = self.rest // self.chunks

        def kernel(_, *refs):
            core, sides, out = refs[self.count], refs[self.count + 1 : -1], refs[-1]
            result = self.product(refs) + core[...].astype(F32)
            for index, ref in enumerate(sides):
                here = slice(index * size, (index + 1) * size)
                out[here] = (result[here] + ref[...].astype(F32)).astype(BF16)

        place = lambda j, s: (0, 0, j)
        (self.total,) = self.run(
            kernel,
            self.inputs(None, lambda s: (s[1], s[0]))
            + [
                (
                    self.from_core,
                    (self.rest, None, self.rows, self.tile),
                    lambda j, s: (0, s[1], 0, j),
                    False,
                )
            ]
            + [(part, (size, self.rows, self.tile), place, False) for part in from_side],
            [
                (
                    (self.rest, self.rows, self.columns),
                    BF16,
                    (self.rest, self.rows, self.tile),
                    place,
                )
            ],
        )
        return self.total

    def along_rest(self, line):
        groups = [[low + 4 * high for high in range(self.rest)] for low in range(4)]
        self.sums = lax.psum_scatter(
            line.next(self.total).reshape(-1, self.columns),
            "dp",
            scatter_dimension=0,
            axis_index_groups=groups,
            tiled=True,
        )

    def to_owner(self):
        place = lax.axis_index("dp") >> 2
        transfers = []
        for shift in range(1, self.rest):
            pairs = [(i, (i + 4 * shift) % self.dp) for i in range(self.dp)]
            part = pick(self.total, (place + shift) % self.rest)
            transfers.append((part, lambda array, pairs=pairs: lax.ppermute(array, "dp", pairs)))
        return transfers

    def gather(self, parts):
        place = lax.axis_index("dp") >> 2
        total = pick(self.total, place).astype(F32)
        self.sums = sum((part.astype(F32) for part in parts), total)

    def result(self):
        return self.sums.astype(F32)


def pick(array, index):
    return lax.dynamic_index_in_dim(array, index, 0, keepdims=False)


def sum_of_products(lefts, rights):
    *lead, rows, _ = lefts[0].shape
    columns = rights[0].shape[1]
    count = 1
    for extent in lead:
        count *= extent
    rights = [right[...] for right in rights]
    pairs, index = [], 0
    for left in lefts:
        left, at = left[...], 0
        while at < left.shape[-1]:
            size = rights[index].shape[0]
            pairs.append((left[..., at : at + size], rights[index]))
            at += size
            index += 1

    def total(pick_block):
        result = None
        for left, right in pairs:
            term = dot(pick_block(left), right)
            result = term if result is None else result + term
        return result

    if rows % 16 == 0:
        blocks = total(lambda left: left.reshape(count * rows, left.shape[-1]))
    else:
        blocks = jnp.stack(
            [
                total(lambda left, block=block: left.reshape(count, rows, -1)[block])
                for block in range(count)
            ]
        )
    return blocks.reshape(*lead, rows, columns)


def tied(*arrays):
    return lax.optimization_barrier(arrays)


class Line:
    def __init__(self):
        self.last = None

    def next(self, array):
        if self.last is not None:
            array, _ = tied(array, self.last)
        return array

    def mark(self, array):
        self.last = array[0] if isinstance(array, (list, tuple)) else array
        return array

    def send(self, *transfers):
        return [send(self.next(array)) for array, send in transfers]

    def land(self, *flying, sums=()):
        count = len(flying)
        *taken, self.last = tied(*flying, *(grad.sums for grad in sums), self.last)
        for grad, value in zip(sums, taken[count:]):
            grad.sums = value
        return taken[:count]


def projected(pieces, weights, first_column, columns, scalars):
    count = len(pieces)
    half = sum(piece.shape[0] for piece in pieces) // 2
    width = pieces[0].shape[1]
    tile = tile_of(columns)

    def kernel(scalar_ref, *refs):
        *ins, weight_ref, out = refs
        weight = weight_ref[...]
        at = 0
        for ref in ins:
            owner = scalar_ref[2] if at < half else 1 - scalar_ref[2]
            size = ref.shape[0]
            start = pl.multiple_of(owner * half + at % half, size)
            out[pl.ds(start, size), :] = dot(ref[...], weight).astype(BF16)
            at += size

    (out,) = call(
        kernel,
        columns // tile,
        scalars,
        [(piece, piece.shape, lambda j, s: (0, 0), True) for piece in pieces]
        + [(weights, (width, tile), lambda j, s: (0, first_column // tile + j), False)],
        [((2 * half, columns), BF16, (2 * half, tile), lambda j, s: (0, j))],
    )
    return out


def projected_back(sources, weights, owner, pieces, dtype, scalars):
    half = sources[0][0].shape[0] // 2
    width = weights.shape[0]
    tile = tile_of(width, 256)
    size = half // pieces
    count = len(sources)

    def kernel(_, *refs):
        total = None
        for rows, weight in zip(refs[:count], refs[count : 2 * count]):
            term = dot_nt(rows[...], weight[...])
            total = term if total is None else total + term
        result = total.astype(dtype)
        for index, out in enumerate(refs[2 * count :]):
            out[...] = result[index * size : (index + 1) * size]

    return call(
        kernel,
        width // tile,
        scalars,
        [
            (array, (half, array.shape[1]), lambda j, s: (owner(s), 0), True)
            for array, _ in sources
        ]
        + [
            (weights, (tile, array.shape[1]), lambda j, s, block=block: (j, block), False)
            for array, block in sources
        ],
        [((size, width), dtype, (size, tile), lambda j, s: (0, j))] * pieces,
    )


def norms_back(line, sums, middle, gain_mid, upstream, branch, gain_branch, scalars):
    rows, width = middle.shape
    count = len(sums)
    size = sums[0][0].shape[0]
    block = 64
    steps, each = rows // block, size // block
    given = [(middle, gain_mid)] + ([] if branch is None else [(branch, gain_branch)])
    norms = len(given)
    outs = 1 if branch is None else 1 + count

    def back(values, gain, d_normed):
        values = values.astype(F32)
        scale = lax.rsqrt(jnp.mean(values * values, axis=1, keepdims=True) + EPSILON)
        normed = values * scale
        weighted = d_normed * gain
        inner = jnp.mean(weighted * normed, axis=1, keepdims=True)
        grad = scale * (weighted - normed * inner)
        return grad, jnp.sum(d_normed * normed, axis=0, keepdims=True)

    def kernel(_, *refs):
        parts, upstream_ref, refs = refs[: 2 * count], refs[2 * count], refs[2 * count + 1 :]
        values_refs, gain_refs, refs = refs[:norms], refs[norms : 2 * norms], refs[2 * norms :]
        grad_refs, gain_grad_refs = refs[:outs], refs[outs:]
        step = pl.program_id(0)

        @pl.when(step == 0)
        def _():
            for ref in gain_grad_refs:
                ref[...] = jnp.zeros_like(ref)

        for index in range(count):

            @pl.when(step // each == index)
            def _(index=index):
                d_normed = parts[2 * index][...] + parts[2 * index + 1][...].astype(F32)
                grad, grad_gain = back(values_refs[0][...], gain_refs[0][...], d_normed)
                gain_grad_refs[0][...] += grad_gain
                total = upstream_ref[...].astype(F32) + grad
                grad_refs[0][...] = total
                if norms > 1:
                    grad, grad_gain = back(values_refs[1][...], gain_refs[1][...], total)
                    gain_grad_refs[1][...] += grad_gain
                    grad_refs[1 + index][...] = grad.astype(BF16)

    def piece(index):
        return lambda j, s: (jnp.clip(j - index * each, 0, each - 1), 0)

    shape = (block, width)
    every = lambda j, s: (j, 0)
    once = lambda j, s: (0, 0)
    (first, *others), *later = sums
    sums = [(line.next(first), *others), *later]
    return line.mark(
        call(
            kernel,
            steps,
            scalars,
            [
                (array, shape, piece(index), False)
                for index, pair in enumerate(sums)
                for array in pair
            ]
            + [(array, shape, every, False) for array in (upstream, *(v for v, _ in given))]
            + [(gain[None], (1, width), once, True) for _, gain in given],
            [((rows, width), F32, shape, every)]
            + [((size, width), BF16, shape, piece(index)) for index in range(outs - 1)]
            + [((1, width), F32, (1, width), once)] * norms,
        )
    )


def joined(weights):
    rows = weights[0].shape[0]
    width = sum(weight.shape[1] for weight in weights)

    def kernel(query_ref, key_ref, value_ref, output_ref, gate_ref, out_ref):
        parts = [query_ref[...]]
        for head in range(key_ref.shape[1] // HEAD_WIDTH):
            here = slice(head * HEAD_WIDTH, (head + 1) * HEAD_WIDTH)
            parts += [key_ref[:, here], value_ref[:, here]]
        at = 0
        for part in [*parts, output_ref[...], gate_ref[...]]:
            out_ref[:, at : at + part.shape[1]] = part
            at += part.shape[1]

    return pl.pallas_call(
        kernel,
        out_shape=jax.ShapeDtypeStruct((rows, width), BF16),
        in_specs=[pl.BlockSpec(memory_space=pltpu.VMEM)] * 5,
        out_specs=pl.BlockSpec(memory_space=pltpu.VMEM),
        compiler_params=pltpu.CompilerParams(vmem_limit_bytes=VMEM_BYTES),
    )(*weights)


def owner_parts(partial):
    count, width = partial.shape
    devices = lax.axis_size("dp") * lax.axis_size("tensor")
    return partial.reshape(count, devices, width // devices).transpose(1, 0, 2)


def to_owners(parts):
    return lax.all_to_all(parts, ("dp", "tensor"), 0, 0, tiled=True)


def make_body(dp):
    def body(
        layer_input,
        query_weight,
        key_weight,
        value_weight,
        w_output,
        w_gate,
        w_up,
        w_down,
        gain_attn_in,
        gain_attn_out,
        gain_ffn_in,
        gain_ffn_out,
        cotangent,
    ):
        line = Line()
        place, turn = lax.axis_index("dp"), lax.axis_index("tensor")
        scalars = [place & 1, (place >> 1) & 1, turn]
        to_other = lambda array: (array, swap)
        mine, theirs = (lambda s: s[2]), (lambda s: 1 - s[2])
        query_cols, key_cols = query_weight.shape[1], key_weight.shape[1]
        qkv_cols = query_cols + 2 * key_cols
        gate_at = qkv_cols + query_cols
        columns = w_gate.shape[1]
        half = layer_input.shape[0]
        quarter = half // 2
        heads = query_cols // HEAD_WIDTH
        group = QUERY_HEADS // KEY_VALUE_HEADS
        full_first = lax.all_gather(
            joined([query_weight, key_weight, value_weight, w_output.T, w_gate]),
            "dp",
            axis=0,
            tiled=True,
        )
        full_up = lax.all_gather(w_up, "dp", axis=0, tiled=True)
        full_down_t = lax.all_gather(w_down.T, "dp", axis=0, tiled=True)
        gains = gather_small(
            jnp.stack([gain_attn_in, gain_attn_out, gain_ffn_in, gain_ffn_out]), dp
        )
        gain_a, gain_b, gain_c, gain_d = gains[0], gains[1], gains[2], gains[3]

        residual_in = layer_input.astype(F32)
        upstream = cotangent.astype(F32)
        input_own = line.mark(rms_norm(residual_in, gain_a).astype(BF16))
        input_other = swap(input_own)
        input_own_t = line.mark(turned([input_own], scalars))
        (input_other,) = line.land(input_other)
        input_other_t = line.mark(turned([input_other], scalars))
        qkv = line.mark(
            projected([input_own, line.next(input_other)], full_first, 0, qkv_cols, scalars)
        )
        attended = line.mark(attend(qkv, heads, group, SEQ_LEN, scalars))
        output_block = qkv_cols // query_cols
        (give,) = line.mark(
            projected_back([(attended, output_block)], full_first, theirs, 1, BF16, scalars)
        )
        (taken,) = line.send(to_other(give))
        (kept,) = line.mark(
            projected_back(
                [(line.next(attended), output_block)], full_first, mine, 1, F32, scalars
            )
        )
        branch_attn = kept + taken.astype(F32)
        middle = residual_in + rms_norm(branch_attn, gain_b)
        mid_own = line.mark(rms_norm(middle, gain_c).astype(BF16))
        (mid_other,) = line.send(to_other(mid_own))
        hidden_own, active_own, slope_own = line.mark(
            feed(mid_own, full_first, gate_at, full_up, scalars)
        )
        mid_own_t = line.mark(turned([line.next(mid_own)], scalars))
        (mid_other,) = line.land(mid_other)
        hidden_other, active_other, slope_other = line.mark(
            feed(line.next(mid_other), full_first, gate_at, full_up, scalars)
        )
        mid_other_t = line.mark(turned([line.next(mid_other)], scalars))

        def ffn_back(kept, taken, middle, upstream):
            branch = kept + taken.astype(F32)
            ffn_out, pull = jax.vjp(rms_norm, branch, gain_d)
            d_ffn, grad_gain = pull(upstream)
            return (middle + ffn_out).astype(BF16), line.mark(d_ffn.astype(BF16)), grad_gain

        low, high = slice(0, quarter), slice(quarter, half)
        give_1 = line.mark(
            feed_out(line.next(hidden_other), 0, quarter, full_down_t, BF16, scalars)
        )
        (taken_1,) = line.send(to_other(give_1))
        give_2 = line.mark(
            feed_out(line.next(hidden_other), 1, quarter, full_down_t, BF16, scalars)
        )
        (taken_1,) = line.land(taken_1)
        (taken_2,) = line.send(to_other(give_2))
        kept = line.mark(feed_out(line.next(hidden_own), 0, half, full_down_t, F32, scalars))
        output_1, d_ffn_1, grad_d_1 = ffn_back(
            line.next(kept)[low], taken_1, middle[low], upstream[low]
        )
        (taken_2,) = line.land(taken_2)
        (d_ffn_3,) = line.send(to_other(d_ffn_1))
        output_2, d_ffn_2, grad_d_2 = ffn_back(
            line.next(kept)[high], taken_2, middle[high], upstream[high]
        )
        d_ffn_own_t = line.mark(turned([line.next(d_ffn_1), d_ffn_2], scalars))
        (d_gate_1,), (d_up_1,) = hidden_back(
            line, [(d_ffn_1, active_own, slope_own, 0)], full_down_t, scalars
        )
        (d_ffn_3,) = line.land(d_ffn_3)
        (d_ffn_4,) = line.send(to_other(d_ffn_2))
        layer_output = jnp.concatenate([output_1, output_2], axis=0)
        grad_d = grad_d_1 + grad_d_2
        (d_gate_2, d_gate_3), (d_up_2, d_up_3) = hidden_back(
            line,
            [(d_ffn_2, active_own, slope_own, 1), (d_ffn_3, active_other, slope_other, 0)],
            full_down_t,
            scalars,
        )
        (d_ffn_4,) = line.land(d_ffn_4)
        d_ffn_other_t = line.mark(turned([line.next(d_ffn_3), d_ffn_4], scalars))

        first = lambda s: 0
        tile = tile_of(columns)
        tiles = columns // tile
        cuts = [0, 2 * tile, 4 * tile, columns]
        split = tile * -(-tiles // 2)
        halves = [(0, split), (split, columns - split)]
        hidden_rights = [(hidden_own, half, first), (hidden_other, half, first)]
        mid_lefts = [mid_own_t, mid_other_t]

        def down_part(part, chunks):
            lefts = [line.next(d_ffn_own_t), d_ffn_other_t]
            start, end = cuts[part], cuts[part + 1]
            return Grad(dp, chunks, lefts, hidden_rights, start, end - start, scalars)

        def mid_part(pieces, part):
            rights = [(line.next(piece), quarter, first) for piece in pieces]
            return Grad(dp, 2, mid_lefts, rights, *halves[part], scalars)

        def mid_back_of(gates, ups, dtype):
            gates = [line.next(gates[0]), *gates[1:]]
            return line.mark(mid_back(gates, ups, full_first, gate_at, full_up, dtype, scalars))

        down_0 = down_part(0, 1)
        line.mark(down_0.give())
        (core_0,) = line.send(down_0.to_core())
        down_2 = down_part(2, 2)
        line.mark(down_2.give())
        (core_0,) = line.land(core_0)
        line.mark(down_0.side(line.next(core_0)))

        down_0_side, core_2 = line.send(down_0.to_side(0), down_2.to_core())
        down_1 = down_part(1, 1)
        line.mark(down_1.give())
        (d_gate_4,), (d_up_4,) = hidden_back(
            line, [(d_ffn_4, active_other, slope_other, 1)], full_down_t, scalars
        )
        d_gates = [d_gate_1, d_gate_2, d_gate_3, d_gate_4]
        d_ups = [d_up_1, d_up_2, d_up_3, d_up_4]
        (core_2,) = line.land(core_2)
        line.mark(down_2.side(line.next(core_2)))
        (down_0_side,) = line.land(down_0_side)

        side_0, core_1 = line.send(down_2.to_side(0), down_1.to_core())
        line.mark(down_0.own(line.next(down_0_side)))
        gate_0 = mid_part(d_gates, 0)
        line.mark(gate_0.give())
        (core_1,) = line.land(core_1)
        line.mark(down_1.both(line.next(core_1)))
        gate_1 = mid_part(d_gates, 1)
        line.mark(gate_1.give())
        (side_0,) = line.land(side_0)

        side_1, core_0, core_1 = line.send(
            down_2.to_side(1), gate_0.to_core(), gate_1.to_core()
        )
        down_0.along_rest(line)
        give_1, give_2 = mid_back_of(d_gates[2:], d_ups[2:], BF16)
        core_0, core_1 = line.land(core_0, core_1)
        line.mark(gate_0.side(line.next(core_0)))
        (side_1,) = line.land(
            side_1, sums=[down_0]
        )

        gate_0_side_0, gate_0_side_1, taken_1, taken_2 = line.send(
            gate_0.to_side(0), gate_0.to_side(1), to_other(give_1), to_other(give_2)
        )
        down_1.along_rest(line)
        line.mark(down_2.own(line.next(side_0), side_1))
        line.mark(gate_1.side(line.next(core_1)))
        up_0 = mid_part(d_ups, 0)
        line.mark(up_0.give())
        kept_1, kept_2 = mid_back_of(d_gates[:2], d_ups[:2], F32)
        gate_0_side_0, gate_0_side_1, taken_1, taken_2 = line.land(
            gate_0_side_0, gate_0_side_1, taken_1, taken_2, sums=[down_1]
        )

        gate_1_side_0, core_0 = line.send(gate_1.to_side(0), up_0.to_core())
        down_2.along_rest(line)
        d_middle, d_branch_1, d_branch_2, grad_c, grad_b = norms_back(
            line,
            [(kept_1, taken_1), (kept_2, taken_2)],
            middle,
            gain_c,
            cotangent,
            branch_attn,
            gain_b,
            scalars,
        )
        (core_0,) = line.land(core_0)
        line.mark(up_0.side(line.next(core_0)))
        (gate_1_side_0,) = line.land(gate_1_side_0)

        gate_1_side_1, d_branch_3, down_1_side = line.send(
            gate_1.to_side(1), to_other(d_branch_1), down_1.to_side_last()
        )
        line.mark(gate_0.own(line.next(gate_0_side_0), gate_0_side_1))
        up_1 = mid_part(d_ups, 1)
        line.mark(up_1.give())
        d_branch_own_t = line.mark(turned([line.next(d_branch_1), d_branch_2], scalars))
        gate_1_side_1, d_branch_3, down_1_side = line.land(
            gate_1_side_1, d_branch_3, down_1_side, sums=[down_2]
        )
        down_1.add_side(down_1_side)

        up_0_side_0, core_1, d_branch_4 = line.send(
            up_0.to_side(0), up_1.to_core(), to_other(d_branch_2)
        )
        gate_0.along_rest(line)
        line.mark(gate_1.own(line.next(gate_1_side_0), gate_1_side_1))
        (core_1,) = line.land(core_1)
        line.mark(up_1.side(line.next(core_1)))
        up_0_side_0, d_branch_4 = line.land(up_0_side_0, d_branch_4)

        (up_0_side_1,) = line.send(up_0.to_side(1))
        gate_1.along_rest(line)
        d_attended = line.mark(
            projected(
                [line.next(d_branch_1), d_branch_2, d_branch_3, d_branch_4],
                full_first,
                qkv_cols,
                query_cols,
                scalars,
            )
        )
        d_branch_other_t = line.mark(turned([line.next(d_branch_3), d_branch_4], scalars))
        d_query, d_pair = line.mark(
            attend_back(qkv, line.next(d_attended), heads, group, SEQ_LEN, scalars)
        )
        (up_0_side_1,) = line.land(
            up_0_side_1, sums=[gate_0]
        )

        (up_1_side_0,) = line.send(up_1.to_side(0))
        line.mark(up_0.own(line.next(up_0_side_0), up_0_side_1))
        output = Grad(
            dp,
            1,
            [d_branch_own_t, line.next(d_branch_other_t)],
            [(attended, half, mine), (attended, half, theirs)],
            0,
            query_cols,
            scalars,
        )
        line.mark(output.give())

        def input_part(array, width):
            rights = [(line.next(array), half, mine), (array, half, theirs)]
            return Grad(dp, 1, [input_own_t, input_other_t], rights, 0, width, scalars)

        query = input_part(d_query, query_cols)
        line.mark(query.give())
        pair = input_part(d_pair, 2 * key_cols)
        line.mark(pair.give())
        (up_1_side_0,) = line.land(up_1_side_0)

        up_1_side_1, core, query_core, pair_core = line.send(
            up_1.to_side(1), output.to_core(), query.to_core(), pair.to_core()
        )
        up_0.along_rest(line)
        give_1, give_2 = line.mark(
            projected_back(
                [(line.next(d_query), 0), (d_pair, 1)], full_first, theirs, 2, BF16, scalars
            )
        )
        core, query_core, pair_core = line.land(core, query_core, pair_core)
        line.mark(output.side(line.next(core)))
        line.mark(query.side(line.next(query_core)))
        line.mark(pair.side(line.next(pair_core)))
        (up_1_side_1,) = line.land(up_1_side_1, sums=[gate_1])

        output_side, taken_1 = line.send(output.to_side(0), to_other(give_1))
        line.mark(up_1.own(line.next(up_1_side_0), up_1_side_1))
        kept_1, kept_2 = line.mark(
            projected_back(
                [(line.next(d_query), 0), (d_pair, 1)], full_first, mine, 2, F32, scalars
            )
        )
        output_side, taken_1 = line.land(output_side, taken_1)

        query_side, taken_2 = line.send(query.to_side(0), to_other(give_2))
        up_1.along_rest(line)
        line.mark(output.own(line.next(output_side)))
        query_side, taken_2 = line.land(query_side, taken_2, sums=[up_0])
        line.mark(query.own(line.next(query_side)))

        pair_side, *query_parts = line.send(pair.to_side(0), *query.to_owner())
        input_grad, grad_a = norms_back(
            line,
            [(kept_1, taken_1), (kept_2, taken_2)],
            layer_input,
            gain_a,
            d_middle,
            None,
            None,
            scalars,
        )
        gain_grads = jnp.stack([grad_a[0], grad_b[0], grad_c[0], grad_d])
        gain_grads = line.mark(owner_parts(gain_grads))
        (pair_side,) = line.land(pair_side)
        line.mark(pair.own(line.next(pair_side)))
        output.along_rest(line)
        query_parts = line.land(*query_parts, sums=[up_1])
        *pair_parts, gain_parts = line.send(*pair.to_owner(), (gain_grads, to_owners))
        pair_parts = line.land(*pair_parts)
        (gain_parts,) = line.land(gain_parts)
        small = jnp.sum(gain_parts, axis=0)
        query.gather(query_parts)
        pair.gather(pair_parts)

        down, gate, up = [down_0, down_1, down_2], [gate_0, gate_1], [up_0, up_1]
        grad_pair = pair.result().reshape(-1, key_cols // HEAD_WIDTH, 2, HEAD_WIDTH)
        grad_down = jnp.concatenate([part.result() for part in down], axis=1).T
        return (
            layer_output,
            input_grad,
            query.result(),
            grad_pair[:, :, 0].reshape(-1, key_cols),
            grad_pair[:, :, 1].reshape(-1, key_cols),
            output.result().T,
            jnp.concatenate([part.result() for part in gate], axis=1),
            jnp.concatenate([part.result() for part in up], axis=1),
            grad_down,
            small[0],
            small[1],
            small[2],
            small[3],
        )

    return body


def solution(mesh):
    rows = P(("dp", "tensor"), None)
    gain = P(("dp", "tensor"))
    into, out_of = P("dp", "tensor"), P("tensor", "dp")
    return jax.shard_map(
        make_body(mesh.shape["dp"]),
        mesh=mesh,
        in_specs=(rows, into, into, into, out_of, into, into, out_of, gain, gain, gain, gain, rows),
        out_specs=(rows, rows, into, into, into, out_of, into, into, out_of, gain, gain, gain, gain),
        check_vma=False,
    )
```
